128 devices in a mesh: section: 2 (over y_lo), ctx: 32 (over z, x, core), shard: 2 (over y_hi).
Axes of the slice: x: 4, y: 4 (y_hi: 2, y_lo: 2; y = y_hi * 2 + y_lo), z: 4, core: 2. Of those that a mesh axis runs over, the one named last changes fastest.
Arguments:
- ends: float32 [2, 2, 2048, 1536], P('section', None, 'ctx'), may hold values from -6 to 6
- w_query: bfloat16 [2, 1536, 1536], P('section', 'ctx', 'shard'), may hold values from -0.15625 to 0.15625
- w_kv: bfloat16 [2, 1536, 2, 256], P('section', 'ctx', None, 'shard'), may hold values from -0.15625 to 0.15625
- w_out: bfloat16 [2, 1536, 1536], P('section', 'ctx', 'shard'), may hold values from -1.25 to 1.25
- w_gate_up: bfloat16 [2, 1536, 2, 8960], P('section', 'ctx', None, 'shard'), may hold values from -0.15625 to 0.15625
- w_down: bfloat16 [2, 1536, 8960], P('section', 'ctx', 'shard'), may hold values from -0.0625 to 0.0625
- gains: bfloat16 [2, 2, 1536], P('section', None, 'ctx'), may hold values from 0.5 to 1.5
- bias_query: bfloat16 [2, 12, 128], P('section', 'shard', 'ctx'), may hold values from -3 to 3
- bias_kv: bfloat16 [2, 2, 2, 128], P('section', None, 'shard', 'ctx'), may hold values from -3 to 3
Outputs:
- boundary: float32 [2, 2, 2048, 1536], P('section', None, 'ctx')
- grad_query: float32 [2, 1536, 1536], P('section', 'ctx', 'shard')
- grad_kv: float32 [2, 1536, 2, 256], P('section', 'ctx', None, 'shard')
- grad_out: float32 [2, 1536, 1536], P('section', 'ctx', 'shard')
- grad_gate_up: float32 [2, 1536, 2, 8960], P('section', 'ctx', None, 'shard')
- grad_down: float32 [2, 1536, 8960], P('section', 'ctx', 'shard')
- grad_gains: float32 [2, 2, 1536], P('section', None, 'ctx')
- grad_bias_query: float32 [2, 12, 128], P('section', 'shard', 'ctx')
- grad_bias_kv: float32 [2, 2, 2, 128], P('section', None, 'shard', 'ctx')
The draws below stay inside these ranges and needn't reach their ends.
All inputs are finite; a program needn't handle non-finite values.
Results may differ from the reference program's by a relative error of at most 0.038.
Values may be sent and summed in bfloat16 or wider, within the bound.
A program may use at most 192 MiB of HBM per device.

```python
import jax
import jax.numpy as jnp
from jax import lax

D = 1536
QH = 12
KV = 2
HD = 128
FF = 8960
MICRO = 2
LAYERS = 2
SEQ = 2048


def levels(rng, extent, pieces, low, top_value):
    level = 1.0
    for dim, shards_of in pieces:
        heights = jax.random.uniform(jax.random.fold_in(jax.random.fold_in(rng, 6), dim), (shards_of,), jnp.float32, low / len(pieces), top_value / len(pieces))
        level = level * jnp.repeat(jnp.exp(heights), extent[dim] // shards_of).reshape((-1,) + (1,) * (len(extent) - 1 - dim))
    return level


def bell_draw(own_key, dims, scale, most, shards=(), kind=jnp.bfloat16):
    entries = jax.random.normal(own_key, dims, jnp.float32) * scale
    if len(shards) > 0:
        entries = levels(own_key, dims, shards, -0.22, 0.18) * entries
    return jnp.clip(entries, min=-most, max=most).astype(kind)


def setup_inputs(seed: int = 0) -> dict:
    splits = jax.random.split(jax.random.key(seed), 10)
    return {
        "ends": bell_draw(splits[0], (LAYERS, MICRO, SEQ, D), 1.0, 6.0, ((0, 2), (2, 32)), jnp.float32),
        "w_query": bell_draw(splits[1], (LAYERS, D, QH * HD), D ** -0.5, 0.15625, ((0, 2), (1, 32), (2, 2))),
        "w_kv": bell_draw(splits[2], (LAYERS, D, 2, KV * HD), D ** -0.5, 0.15625, ((0, 2), (1, 32), (3, 2))),
        "w_out": bell_draw(splits[3], (LAYERS, D, QH * HD), (max(1, QH * HD * 32 // SEQ)) ** -0.5, 1.25, ((0, 2), (1, 32), (2, 2))),
        "w_gate_up": bell_draw(splits[4], (LAYERS, D, 2, FF), D ** -0.5, 0.15625, ((0, 2), (1, 32), (3, 2))),
        "w_down": bell_draw(splits[5], (LAYERS, D, FF), FF ** -0.5, 0.0625, ((0, 2), (1, 32), (2, 2))),
        "gains": jnp.clip(1.0 + 0.1 * jax.random.normal(splits[6], (LAYERS, 2, D), jnp.float32), 0.5, 1.5).astype(jnp.bfloat16),
        "bias_query": bell_draw(splits[7], (LAYERS, QH, HD), 0.5, 3.0, ((0, 2), (1, 2), (2, 32))),
        "bias_kv": bell_draw(splits[8], (LAYERS, 2, KV, HD), 0.5, 3.0, ((0, 2), (2, 2), (3, 32))),
    }


EPS = 1e-06
THETA = 1000000.0
PRECISE = lax.Precision.HIGHEST

@jax.custom_vjp
def low(v):
    return lax.optimization_barrier(v.astype(jnp.bfloat16)).astype(jnp.float32)

@jax.custom_vjp
def low_back(v):
    return v

def low_keep(v):
    return (low(v), None)

def low_pass(kept, grad):
    return (grad,)

def back_keep(v):
    return (v, None)

def back_low(kept, grad):
    return (low(grad),)
low.defvjp(low_keep, low_pass)
low_back.defvjp(back_keep, back_low)

def tables(length, width):
    positions = jnp.arange(length, dtype=jnp.float32)
    inverse = 1.0 / THETA ** (jnp.arange(0, width, 2, dtype=jnp.float32) / width)
    angles = positions[:, None] * inverse[None, :]
    angles = jnp.concatenate([angles, angles], axis=1)
    return (jnp.cos(angles), jnp.sin(angles))

def rotate(values, cos_table, sine_table):
    half_width = values.shape[-1] // 2
    turned = jnp.concatenate([-values[..., half_width:], values[..., :half_width]], axis=-1)
    return values * cos_table[:, None, :] + turned * sine_table[:, None, :]

def normalize(inputs, gain):
    return inputs * lax.rsqrt(lax.optimization_barrier(jnp.mean(inputs * inputs, axis=-1, keepdims=True)) + EPS) * gain

def attend(queries, keys, values):
    seq_len = queries.shape[0]
    block = min(512, seq_len)
    group = QH // KV
    keys_all = jnp.repeat(keys, group, axis=1)
    values_all = jnp.repeat(values, group, axis=1)
    scale = HD ** (-0.5)
    blocks = queries.reshape(seq_len // block, block, QH, HD)

    @jax.checkpoint
    def one_block(item):
        query_block, index = item
        raw_scores = jnp.einsum('qhd,khd->hqk', query_block, keys_all, precision=PRECISE) * scale
        raw_scores = low_back(raw_scores)
        query_pos = index * block + jnp.arange(block, dtype=jnp.int32)
        key_pos = jnp.arange(seq_len, dtype=jnp.int32)
        allowed = key_pos[None, :] <= query_pos[:, None]
        raw_scores = jnp.where(allowed[None], raw_scores, -1e+30)
        soft = low(jax.nn.softmax(raw_scores, axis=-1))
        return jnp.einsum('hqk,khd->qhd', soft, values_all, precision=PRECISE)
    outputs = lax.map(one_block, (blocks, jnp.arange(seq_len // block, dtype=jnp.int32)))
    return outputs.reshape(seq_len, QH * HD)

def layer(params, inputs):
    w_query, w_kv, w_out, w_gate_up, w_down, gains, bias_query, bias_kv = params
    seq_len = inputs.shape[0]
    cos_table, sine_table = tables(seq_len, HD)
    hidden = low(normalize(inputs, gains[0]))
    query_proj = jnp.dot(hidden, w_query, precision=PRECISE) + bias_query.reshape(-1)
    key_value = jnp.dot(hidden, w_kv.reshape(D, -1), precision=PRECISE) + bias_kv.reshape(-1)
    kv_width = KV * HD
    queries = low(rotate(low_back(query_proj).reshape(seq_len, QH, HD), cos_table, sine_table))
    keys = low(rotate(low_back(key_value[:, :kv_width]).reshape(seq_len, KV, HD), cos_table, sine_table))
    values = low(low_back(key_value[:, kv_width:])).reshape(seq_len, KV, HD)
    attended = low(low_back(attend(queries, keys, values)))
    residual_mid = inputs + low_back(jnp.dot(attended, w_out.T, precision=PRECISE))
    hidden2 = low(normalize(residual_mid, gains[1]))
    gate_up = jnp.einsum('td,dcf->tcf', hidden2, w_gate_up, precision=PRECISE)
    gate_part = low_back(gate_up[:, 0])
    up_part = low_back(gate_up[:, 1])
    product = low(jax.nn.silu(gate_part) * up_part)
    return residual_mid + low_back(jnp.dot(product, w_down.T, precision=PRECISE))

def network(params, inputs):
    first_out = layer(tuple((array[0] for array in params)), inputs)
    return layer(tuple((array[1] for array in params)), low(low_back(first_out)))

def reference(ends, w_query, w_kv, w_out, w_gate_up, w_down, gains, bias_query, bias_kv):
    params = tuple((array.astype(jnp.float32) for array in (w_query, w_kv, w_out, w_gate_up, w_down, gains, bias_query, bias_kv)))

    def one_micro(totals, item):
        inputs, cotangent = item
        result, pull = jax.vjp(network, params, inputs)
        grad_params, grad_inputs = pull(cotangent)
        summed = tuple((total_grad + new_grad for total_grad, new_grad in zip(totals, grad_params)))
        return (summed, (result, grad_inputs))
    zero_grads = tuple((jnp.zeros(array.shape, jnp.float32) for array in params))
    totals, (results, grad_inputs) = lax.scan(one_micro, zero_grads, (ends[0], ends[1]))
    boundary = jnp.stack([grad_inputs, results])
    return (boundary, totals[0], totals[1], totals[2], totals[3], totals[4], totals[5], totals[6], totals[7])
```

```python
import jax
import jax.numpy as jnp
from jax import lax
from jax.experimental import pallas as pl
from jax.experimental.pallas import tpu as pltpu
from jax.sharding import PartitionSpec as P

MESH = pl.DeviceIdType.MESH
BF = jnp.bfloat16
F32 = jnp.float32
EPS = 1e-06
THETA = 1000000.0
D = 1536
HD = 128
HEADS = 3
UNITS = 1152
CHUNK = 384
TOK = 64
OWN = 32
QKW = 512
ANY = pl.BlockSpec(memory_space=pl.ANY)
VM = pl.BlockSpec(memory_space=pltpu.VMEM)


class Place:
    def __init__(self):
        self.ctx = lax.axis_index("ctx")
        self.s = lax.axis_index("section")
        self.h = lax.axis_index("shard")
        self.z = self.ctx // 8
        self.x = (self.ctx // 2) % 4
        self.c = self.ctx % 2
        self.y = self.h * 2 + self.s

    def yp(self, k):
        other = (self.y + k) % 4
        return {"section": other % 2, "shard": other // 2}

    def xp(self, k):
        return {"ctx": self.z * 8 + ((self.x + k) % 4) * 2 + self.c}

    def zp(self, k):
        return {"ctx": (self.ctx + 8 * k) % 32}

    def cp(self):
        return {"ctx": self.ctx + 1 - 2 * self.c}


def greet(peers):
    barrier = pltpu.get_barrier_semaphore()
    for peer in peers:
        pl.semaphore_signal(barrier, 1, device_id=peer, device_id_type=MESH)
    pl.semaphore_wait(barrier, len(peers))


class Links:
    def __init__(self, send, recv):
        self.send, self.recv, self.count = send, recv, 0

    def go(self, src, dst, peer):
        index = self.count
        self.count += 1
        copy = pltpu.make_async_remote_copy(
            src, dst, self.send.at[index], self.recv.at[index], device_id=peer, device_id_type=MESH
        )
        copy.start()
        return copy


def landed(copies):
    for copy in copies:
        copy.wait_recv()


def left(copies):
    for copy in copies:
        copy.wait_send()


def dot(a, b, ca=1, cb=0):
    return lax.dot_general(a, b, (((ca,), (cb,)), ((), ())), preferred_element_type=F32)


ORDER = (1, 3, 2)


def unit_rms(u):
    scale = lax.rsqrt(jnp.mean(u * u, axis=1, keepdims=True) + EPS)
    return u * scale, scale


def norm_back(u, gain, dy):
    n, scale = unit_rms(u)
    sd = dy * gain
    return scale * (sd - n * jnp.mean(sd * n, axis=1, keepdims=True)), jnp.sum(dy * n, axis=0, keepdims=True)


def turned(u, cos, sin):
    return u * cos + pltpu.roll(u, 64, 1) * sin


def turned_back(w, cos, sin):
    return w * cos - pltpu.roll(w, 64, 1) * sin


def twice(table):
    return jnp.concatenate([table, table], axis=0)


def key_places(micro_rows):
    j = lax.broadcasted_iota(jnp.int32, (micro_rows, 2048), 1)
    core = j // 1024
    chip = (j % 1024) // TOK
    return chip * (2 * TOK) + core * TOK + j % TOK


def masked(raw, ctx):
    rows = raw.shape[0]
    query = ctx * TOK + lax.broadcasted_iota(jnp.int32, (rows, 2048), 0) % TOK
    return jnp.where(key_places(rows) <= query, raw * (HD**-0.5), -1e30)


def attn_forward_kernel(
    x_ref, gain_ref, w_ref, bias_ref, cos_ref, sin_ref,
    mid_ref, hid_ref, q_ref, kv_ref, att_ref, wf_ref,
    part_ref, got_ref, wsem, send, recv,
):
    me = Place()
    greet([me.yp(1), me.yp(2), me.yp(3), me.xp(1), me.xp(2), me.xp(3), me.zp(1), me.zp(2), me.zp(3), me.cp()])
    net = Links(send, recv)
    weights_over = net.go(w_ref, wf_ref.at[me.c], me.cp())
    weights_here = pltpu.make_async_copy(w_ref, wf_ref.at[me.c], wsem)
    weights_here.start()
    x = x_ref[...]
    normed, _ = unit_rms(x)
    hid_ref[me.y] = (normed * gain_ref[...]).astype(BF)
    hid_copies = [net.go(hid_ref.at[me.y], hid_ref.at[me.y], me.yp(k)) for k in ORDER]
    cos, sin = twice(cos_ref[...]), twice(sin_ref[...])
    weights_here.wait()
    weights_over.wait()
    landed(hid_copies)
    hidden = hid_ref[...].reshape(2 * TOK, D)
    keyval = []
    proj = dot(hidden, wf_ref[0]) + bias_ref[:, :QKW]
    key = turned(proj[:, 384:], cos, sin).astype(BF)
    value = (dot(hidden, wf_ref[1, :, 384:]) + bias_ref[:, QKW:]).astype(BF)
    keyval = jnp.concatenate([key, value], axis=1)
    for m in range(2):
        kv_ref[me.c, m, me.z, me.x] = keyval[m * TOK : (m + 1) * TOK]
    first0 = [net.go(kv_ref.at[me.c, 0, me.z, me.x], kv_ref.at[me.c, 0, me.z, me.x], me.xp(k)) for k in ORDER]
    first1 = [net.go(kv_ref.at[me.c, 1, me.z, me.x], kv_ref.at[me.c, 1, me.z, me.x], me.zp(k)) for k in ORDER]
    for head in range(HEADS):
        query = turned(proj[:, head * HD : (head + 1) * HD], cos, sin).astype(BF)
        for m in range(2):
            q_ref[m, head] = query[m * TOK : (m + 1) * TOK]
    landed(first0)
    second0 = [net.go(kv_ref.at[me.c, 0, me.z], kv_ref.at[me.c, 0, me.z], me.zp(k)) for k in ORDER]
    landed(first1)
    second1 = [net.go(kv_ref.at[me.c, 1, :, me.x], kv_ref.at[me.c, 1, :, me.x], me.xp(k)) for k in ORDER]
    landed(second0)
    third0 = net.go(kv_ref.at[me.c, 0], kv_ref.at[me.c, 0], me.cp())
    landed(second1)
    third1 = net.go(kv_ref.at[me.c, 1], kv_ref.at[me.c, 1], me.cp())
    for m, third in ((0, third0), (1, third1)):
        third.wait_recv()
        queries = q_ref[m].reshape(HEADS * TOK, HD)
        keys = kv_ref[:, m, :, :, :, :HD].reshape(2048, HD)
        values = kv_ref[:, m, :, :, :, HD:].reshape(2048, HD)
        scores = masked(dot(queries, keys, 1, 1), me.ctx)
        weight = jnp.exp(scores - jnp.max(scores, axis=1, keepdims=True))
        total = jnp.sum(weight, axis=1, keepdims=True)
        out = (dot(weight.astype(BF), values) / total).astype(BF)
        for head in range(HEADS):
            att_ref[m * TOK : (m + 1) * TOK, head * HD : (head + 1) * HD] = out[head * TOK : (head + 1) * TOK]
    part_ref[...] = dot(att_ref[...], wf_ref[1, :, :384], 1, 1).astype(BF).reshape(4, OWN, D)
    back = [net.go(part_ref.at[(me.y + k) % 4], got_ref.at[k - 1], me.yp(k)) for k in ORDER]
    total = x + part_ref[me.y].astype(F32)
    landed(back)
    for k in range(3):
        total = total + got_ref[k].astype(F32)
    mid_ref[...] = total
    left(hid_copies + first0 + first1 + second0 + second1 + [third0, third1] + back)


def attn_forward(x, gain, w_half, bias, cos, sin):
    return pl.pallas_call(
        attn_forward_kernel,
        out_shape=(
            jax.ShapeDtypeStruct((OWN, D), F32),
            jax.ShapeDtypeStruct((4, OWN, D), BF),
            jax.ShapeDtypeStruct((2, HEADS, TOK, HD), BF),
            jax.ShapeDtypeStruct((2, 2, 4, 4, TOK, 2 * HD), BF),
            jax.ShapeDtypeStruct((2 * TOK, HEADS * HD), BF),
            jax.ShapeDtypeStruct((2, D, QKW), BF),
        ),
        in_specs=[VM, VM, ANY, VM, VM, VM],
        out_specs=(VM,) * 6,
        scratch_shapes=[
            pltpu.VMEM((4, OWN, D), BF),
            pltpu.VMEM((3, OWN, D), BF),
            pltpu.SemaphoreType.DMA,
            pltpu.SemaphoreType.DMA((21,)),
            pltpu.SemaphoreType.DMA((21,)),
        ],
        compiler_params=pltpu.CompilerParams(collective_id=0, has_side_effects=True, vmem_limit_bytes=48 << 20),
        name="attn_forward",
    )(x, gain, w_half, bias, cos, sin)


def fetch_mlp(w_ref, w_vmem, sems):
    copies = []
    for part in range(3):
        copy = pltpu.make_async_copy(w_ref.at[:, part * UNITS : (part + 1) * UNITS], w_vmem.at[part], sems.at[part])
        copy.start()
        copies.append(copy)
    return copies


def gather_yc(net, me, buf):
    sent = [net.go(buf.at[me.c, me.y], buf.at[me.c, me.y], me.yp(k)) for k in ORDER]
    crossed = [net.go(buf.at[me.c, me.y], buf.at[me.c, me.y], me.cp())]
    for k, copy in zip(ORDER, sent):
        copy.wait_recv()
        slot = (me.y + 4 - k) % 4
        crossed.append(net.go(buf.at[me.c, slot], buf.at[me.c, slot], me.cp()))
    landed(crossed)
    return sent + crossed


def scatter_yc_start(net, me, part, mate):
    return net.go(part.at[1 - me.c], mate, me.cp())


def scatter_yc_middle(net, me, part, mate, got, swap):
    swap.wait_recv()
    mate[...] = (part[me.c].astype(F32) + mate[...].astype(F32)).astype(BF)
    return [net.go(mate.at[(me.y + k) % 4], got.at[k - 1], me.yp(k)) for k in ORDER]


def scatter_yc_end(me, mate, got, back):
    total = mate[me.y].astype(F32)
    landed(back)
    for k in range(3):
        total = total + got[k].astype(F32)
    return total


def mlp_forward_kernel(
    mid_ref, gain_ref, w_ref,
    out_ref, hid_ref, gate_ref, up_ref, prod_ref,
    w_vmem, acc, part, mate, got, wsem, send, recv,
):
    me = Place()
    weights = fetch_mlp(w_ref, w_vmem, wsem)
    greet([me.yp(1), me.yp(2), me.yp(3), me.cp()])
    net = Links(send, recv)
    normed, _ = unit_rms(mid_ref[...])
    hid_ref[me.c, me.y] = (normed * gain_ref[...]).astype(BF)
    gathered = gather_yc(net, me, hid_ref)
    for copy in weights:
        copy.wait()
    hidden = hid_ref[...].reshape(256, D)
    acc[...] = jnp.zeros_like(acc)

    def step(i, _):
        cols = pl.ds(pl.multiple_of(i * CHUNK, CHUNK), CHUNK)
        gate = dot(hid_ref[...].reshape(256, D), w_vmem[0, :, cols])
        up = dot(hid_ref[...].reshape(256, D), w_vmem[1, :, cols])
        product = (gate * jax.nn.sigmoid(gate) * up).astype(BF)
        gate_ref[:, cols] = gate
        up_ref[:, cols] = up
        prod_ref[:, cols] = product
        acc[...] += dot(product, w_vmem[2, :, cols], 1, 1)
        return 0

    lax.fori_loop(0, UNITS // CHUNK, step, 0)
    part[...] = acc[...].astype(BF).reshape(2, 4, OWN, D)
    swap = scatter_yc_start(net, me, part, mate)
    back = scatter_yc_middle(net, me, part, mate, got, swap)
    out_ref[...] = mid_ref[...] + scatter_yc_end(me, mate, got, back)
    left(gathered + [swap] + back)


def mlp_forward(mid, gain, w):
    return pl.pallas_call(
        mlp_forward_kernel,
        out_shape=(
            jax.ShapeDtypeStruct((OWN, D), F32),
            jax.ShapeDtypeStruct((2, 4, OWN, D), BF),
            jax.ShapeDtypeStruct((256, UNITS), F32),
            jax.ShapeDtypeStruct((256, UNITS), F32),
            jax.ShapeDtypeStruct((256, UNITS), BF),
        ),
        in_specs=[VM, VM, ANY],
        out_specs=(VM,) * 5,
        scratch_shapes=[
            pltpu.VMEM((3, D, UNITS), BF),
            pltpu.VMEM((256, D), F32),
            pltpu.VMEM((2, 4, OWN, D), BF),
            pltpu.VMEM((4, OWN, D), BF),
            pltpu.VMEM((3, OWN, D), BF),
            pltpu.SemaphoreType.DMA((3,)),
            pltpu.SemaphoreType.DMA((11,)),
            pltpu.SemaphoreType.DMA((11,)),
        ],
        compiler_params=pltpu.CompilerParams(collective_id=1, has_side_effects=True, vmem_limit_bytes=48 << 20),
        name="mlp_forward",
    )(mid, gain, w)


def mlp_backward_kernel(
    g_ref, mid_ref, gain_ref, w_ref, hid_ref, gate_ref, up_ref, prod_ref,
    gmid_ref, ggain_ref, dw_ref,
    w_vmem, low, dgate, dup, acc, part, mate, got, wsem, send, recv,
):
    me = Place()
    weights = fetch_mlp(w_ref, w_vmem, wsem)
    greet([me.yp(1), me.yp(2), me.yp(3), me.cp()])
    net = Links(send, recv)
    low[me.c, me.y] = g_ref[...].astype(BF)
    gathered = gather_yc(net, me, low)
    for copy in weights:
        copy.wait()
    acc[...] = jnp.zeros_like(acc)

    def step(i, _):
        cols = pl.ds(pl.multiple_of(i * CHUNK, CHUNK), CHUNK)
        dprod = dot(low[...].reshape(256, D), w_vmem[2, :, cols])
        gate, up = gate_ref[:, cols], up_ref[:, cols]
        sigma = jax.nn.sigmoid(gate)
        dg = (dprod * up * sigma * (1.0 + gate * (1.0 - sigma))).astype(BF)
        du = (dprod * gate * sigma).astype(BF)
        dgate[:, cols] = dg
        dup[:, cols] = du
        acc[...] += dot(dg, w_vmem[0, :, cols], 1, 1) + dot(du, w_vmem[1, :, cols], 1, 1)
        return 0

    lax.fori_loop(0, UNITS // CHUNK, step, 0)
    part[...] = acc[...].astype(BF).reshape(2, 4, OWN, D)
    swap = scatter_yc_start(net, me, part, mate)

    def weight_grads(index, left_ref, right_ref):
        def step_w(i, _):
            cols = pl.ds(pl.multiple_of(i * CHUNK, CHUNK), CHUNK)
            where = pl.ds(pl.multiple_of(index * UNITS + i * CHUNK, CHUNK), CHUNK)
            dw_ref[:, where] = dot(left_ref[...].reshape(256, D), right_ref[:, cols], 0, 0).astype(BF)
            return 0

        lax.fori_loop(0, UNITS // CHUNK, step_w, 0)

    back = scatter_yc_middle(net, me, part, mate, got, swap)
    weight_grads(0, hid_ref, dgate)
    weight_grads(1, hid_ref, dup)
    weight_grads(2, low, prod_ref)
    dy = scatter_yc_end(me, mate, got, back)
    du, ggain_ref[...] = norm_back(mid_ref[...], gain_ref[...], dy)
    gmid_ref[...] = g_ref[...] + du
    left(gathered + [swap] + back)


def mlp_backward(g, mid, gain, w, hid, gate, up, prod):
    return pl.pallas_call(
        mlp_backward_kernel,
        out_shape=(
            jax.ShapeDtypeStruct((OWN, D), F32),
            jax.ShapeDtypeStruct((1, D), F32),
            jax.ShapeDtypeStruct((D, 3 * UNITS), BF),
        ),
        in_specs=[VM, VM, VM, ANY, VM, VM, VM, VM],
        out_specs=(VM,) * 3,
        scratch_shapes=[
            pltpu.VMEM((3, D, UNITS), BF),
            pltpu.VMEM((2, 4, OWN, D), BF),
            pltpu.VMEM((256, UNITS), BF),
            pltpu.VMEM((256, UNITS), BF),
            pltpu.VMEM((256, D), F32),
            pltpu.VMEM((2, 4, OWN, D), BF),
            pltpu.VMEM((4, OWN, D), BF),
            pltpu.VMEM((3, OWN, D), BF),
            pltpu.SemaphoreType.DMA((3,)),
            pltpu.SemaphoreType.DMA((11,)),
            pltpu.SemaphoreType.DMA((11,)),
        ],
        compiler_params=pltpu.CompilerParams(collective_id=2, has_side_effects=True, vmem_limit_bytes=56 << 20),
        name="mlp_backward",
    )(g, mid, gain, w, hid, gate, up, prod)


def attn_backward_kernel(
    gm_ref, x_ref, gain_ref, w_ref, hid_ref, q_ref, kv_ref, att_ref, cos_ref, sin_ref,
    gin_ref, ggain_ref, gbias_ref, dw_ref,
    low, dkv, kmate, kz, kx, k2, k3, kpair, kpair_got, dqs, dws, dw_got, part, got, send, recv,
):
    me = Place()
    greet([me.yp(1), me.yp(2), me.yp(3), me.xp(1), me.xp(2), me.xp(3), me.zp(1), me.zp(2), me.zp(3), me.cp()])
    net = Links(send, recv)
    low[me.y] = gm_ref[...].astype(BF)
    gathered = [net.go(low.at[me.y], low.at[me.y], me.yp(k)) for k in ORDER]
    cos, sin = twice(cos_ref[...]), twice(sin_ref[...])
    landed(gathered)
    grad_mid = low[...].reshape(2 * TOK, D)
    grad_att = dot(grad_mid, w_ref[1, :, :384]).astype(BF)
    for m in range(2):
        rows = slice(m * TOK, (m + 1) * TOK)
        queries = q_ref[m].reshape(HEADS * TOK, HD)
        keys = kv_ref[:, m, :, :, :, :HD].reshape(2048, HD)
        values = kv_ref[:, m, :, :, :, HD:].reshape(2048, HD)
        grad_out = jnp.concatenate([grad_att[rows, h * HD : (h + 1) * HD] for h in range(HEADS)], axis=0)
        scores = masked(dot(queries, keys, 1, 1), me.ctx)
        weight = jnp.exp(scores - jnp.max(scores, axis=1, keepdims=True))
        soft = weight / jnp.sum(weight, axis=1, keepdims=True)
        grad_soft = dot(grad_out, values, 1, 1)
        delta = jnp.sum(soft * grad_soft, axis=1, keepdims=True)
        grad_scores = (soft * (grad_soft - delta)).astype(BF)
        grad_values = dot(soft.astype(BF), grad_out, 0, 0)
        grad_keys = dot(grad_scores, queries, 0, 0) * (HD**-0.5)
        dkv[:, m] = jnp.concatenate([grad_keys, grad_values], axis=1).astype(BF).reshape(2, 4, 4, TOK, 2 * HD)
        dq = dot(grad_scores, keys) * (HD**-0.5)
        for h in range(HEADS):
            dqs[rows, h * HD : (h + 1) * HD] = dq[h * TOK : (h + 1) * TOK]
    swap = net.go(dkv.at[1 - me.c], kmate, me.cp())
    dq_low = jnp.concatenate(
        [turned_back(dqs[:, h * HD : (h + 1) * HD], cos, sin).astype(BF) for h in range(HEADS)], axis=1
    )
    hidden = hid_ref[...].reshape(2 * TOK, D)
    swap.wait_recv()
    kmate[...] = (kmate[...].astype(F32) + dkv[me.c].astype(F32)).astype(BF)
    first0 = [net.go(kmate.at[0, (me.z + k) % 4], kz.at[k - 1], me.zp(k)) for k in ORDER]
    first1 = [net.go(kmate.at[1, :, (me.x + k) % 4], kx.at[k - 1], me.xp(k)) for k in ORDER]
    dws[0, :, :384] = dot(hidden, dq_low, 0, 0).astype(BF)
    dws[1, :, :384] = dot(grad_mid, att_ref[...], 0, 0).astype(BF)
    dws[1, :, 384:] = jnp.zeros((D, HD), BF)
    landed(first0)
    total0 = kmate[0, me.z].astype(F32)
    for k in range(3):
        total0 = total0 + kz[k].astype(F32)
    k2[0] = total0.astype(BF)
    second0 = [net.go(k2.at[0, (me.x + k) % 4], k3.at[0, k - 1], me.xp(k)) for k in ORDER]
    landed(first1)
    total1 = kmate[1, :, me.x].astype(F32)
    for k in range(3):
        total1 = total1 + kx[k].astype(F32)
    k2[1] = total1.astype(BF)
    second1 = [net.go(k2.at[1, (me.z + k) % 4], k3.at[1, k - 1], me.zp(k)) for k in ORDER]
    landed(second0 + second1)
    for m, place in ((0, me.x), (1, me.z)):
        total = k2[m, place].astype(F32)
        for k in range(3):
            total = total + k3[m, k].astype(F32)
        kpair[0, m * TOK : (m + 1) * TOK] = total[:, :HD].astype(BF)
        kpair[1, m * TOK : (m + 1) * TOK] = total[:, HD:].astype(BF)
    pair = net.go(kpair.at[1 - me.s], kpair_got, {"section": 1 - me.s})
    pair.wait_recv()
    total = kpair[me.s].astype(F32) + kpair_got[...].astype(F32)
    dk_low = jnp.where(me.s == 0, turned_back(total, cos, sin), total).astype(BF)
    part[...] = (
        (dot(dq_low, w_ref[0, :, :384], 1, 1) + dot(dk_low, w_ref[me.s, :, 384:], 1, 1)).astype(BF).reshape(4, OWN, D)
    )
    back = [net.go(part.at[(me.y + k) % 4], got.at[k - 1], me.yp(k)) for k in ORDER]
    dws[0, :, 384:] = dot(hidden, dk_low, 0, 0).astype(BF)
    dw_swap = net.go(dws.at[1 - me.c], dw_got, me.cp())
    gbias_ref[:, :384] = jnp.sum(dq_low.astype(F32), axis=0, keepdims=True)
    gbias_ref[:, 384:] = jnp.sum(dk_low.astype(F32), axis=0, keepdims=True)
    dy = part[me.y].astype(F32)
    landed(back)
    for k in range(3):
        dy = dy + got[k].astype(F32)
    dx, ggain_ref[...] = norm_back(x_ref[...], gain_ref[...], dy)
    gin_ref[...] = gm_ref[...] + dx
    dw_swap.wait_recv()
    dw_ref[...] = (dws[me.c].astype(F32) + dw_got[...].astype(F32)).astype(BF)
    left(gathered + [swap] + first0 + first1 + second0 + second1 + [pair] + back + [dw_swap])


def attn_backward(gm, x, gain, w, hid, q, kv, att, cos, sin):
    return pl.pallas_call(
        attn_backward_kernel,
        out_shape=(
            jax.ShapeDtypeStruct((OWN, D), F32),
            jax.ShapeDtypeStruct((1, D), F32),
            jax.ShapeDtypeStruct((1, QKW), F32),
            jax.ShapeDtypeStruct((D, QKW), BF),
        ),
        in_specs=[VM] * 10,
        out_specs=(VM,) * 4,
        scratch_shapes=[
            pltpu.VMEM((4, OWN, D), BF),
            pltpu.VMEM((2, 2, 4, 4, TOK, 2 * HD), BF),
            pltpu.VMEM((2, 4, 4, TOK, 2 * HD), BF),
            pltpu.VMEM((3, 4, TOK, 2 * HD), BF),
            pltpu.VMEM((3, 4, TOK, 2 * HD), BF),
            pltpu.VMEM((2, 4, TOK, 2 * HD), BF),
            pltpu.VMEM((2, 3, TOK, 2 * HD), BF),
            pltpu.VMEM((2, 2 * TOK, HD), BF),
            pltpu.VMEM((2 * TOK, HD), BF),
            pltpu.VMEM((2 * TOK, HEADS * HD), F32),
            pltpu.VMEM((2, D, QKW), BF),
            pltpu.VMEM((D, QKW), BF),
            pltpu.VMEM((4, OWN, D), BF),
            pltpu.VMEM((3, OWN, D), BF),
            pltpu.SemaphoreType.DMA((21,)),
            pltpu.SemaphoreType.DMA((21,)),
        ],
        compiler_params=pltpu.CompilerParams(collective_id=3, has_side_effects=True, vmem_limit_bytes=48 << 20),
        name="attn_backward",
    )(gm, x, gain, w, hid, q, kv, att, cos, sin)


def quad(me):
    return (
        (me.c, 1 - me.s, {"section": 1 - me.s}),
        (1 - me.c, me.s, me.cp()),
        (1 - me.c, 1 - me.s, {"section": 1 - me.s, "ctx": me.ctx + 1 - 2 * me.c}),
    )


def spread_kernel(attn_ref, mlp_ref, attn_out, mlp_out, lsem, send, recv):
    me = Place()
    peers = quad(me)
    greet([peer for _, _, peer in peers])
    net = Links(send, recv)
    copies = []
    for src, dst in ((attn_ref, attn_out), (mlp_ref, mlp_out)):
        for core, section, peer in peers:
            copies.append(net.go(src.at[section, core], dst.at[me.s, me.c], peer))
    here = []
    for i, (src, dst) in enumerate(((attn_ref, attn_out), (mlp_ref, mlp_out))):
        copy = pltpu.make_async_copy(src.at[me.s, me.c], dst.at[me.s, me.c], lsem.at[i])
        copy.start()
        here.append(copy)
    for copy in here + copies:
        copy.wait()


def spread(attn, mlp):
    return pl.pallas_call(
        spread_kernel,
        out_shape=(jax.ShapeDtypeStruct(attn.shape, BF), jax.ShapeDtypeStruct(mlp.shape, BF)),
        in_specs=[ANY, ANY],
        out_specs=(ANY, ANY),
        scratch_shapes=[
            pltpu.SemaphoreType.DMA((2,)),
            pltpu.SemaphoreType.DMA((6,)),
            pltpu.SemaphoreType.DMA((6,)),
        ],
        compiler_params=pltpu.CompilerParams(collective_id=4, has_side_effects=True),
        name="spread",
    )(attn, mlp)


def gather_back_kernel(attn_ref, mlp_ref, ends_ref, attn_out, mlp_out, ends_out, lsem, send, recv):
    me = Place()
    peers = quad(me)
    far = {"section": me.s, "shard": 1 - me.h}
    cross = {"section": 1 - me.s, "shard": 1 - me.h}
    greet([peer for _, _, peer in peers] + [far, cross])
    net = Links(send, recv)
    copies = []
    for src, dst in ((attn_ref, attn_out), (mlp_ref, mlp_out)):
        for core, section, peer in peers:
            copies.append(net.go(src.at[section, core], dst.at[me.s, me.c], peer))
    for k in ORDER:
        copies.append(net.go(ends_ref.at[((me.y + k) % 4) % 2], ends_out.at[me.y], me.yp(k)))
    here = []
    pairs = (
        (attn_ref.at[me.s, me.c], attn_out.at[me.s, me.c]),
        (mlp_ref.at[me.s, me.c], mlp_out.at[me.s, me.c]),
        (ends_ref.at[me.s], ends_out.at[me.y]),
    )
    for i, (src, dst) in enumerate(pairs):
        copy = pltpu.make_async_copy(src, dst, lsem.at[i])
        copy.start()
        here.append(copy)
    for copy in here + copies:
        copy.wait()


def gather_back(attn, mlp, ends):
    return pl.pallas_call(
        gather_back_kernel,
        out_shape=(
            jax.ShapeDtypeStruct(attn.shape, BF),
            jax.ShapeDtypeStruct(mlp.shape, BF),
            jax.ShapeDtypeStruct((4, OWN, D), F32),
        ),
        in_specs=[ANY] * 3,
        out_specs=(ANY,) * 3,
        scratch_shapes=[
            pltpu.SemaphoreType.DMA((3,)),
            pltpu.SemaphoreType.DMA((9,)),
            pltpu.SemaphoreType.DMA((9,)),
        ],
        compiler_params=pltpu.CompilerParams(collective_id=5, has_side_effects=True),
        name="gather_back",
    )(attn, mlp, ends)


SAME_CORE = [[core + 2 * chip for chip in range(16)] for core in range(2)]


def all_rows(block):
    return lax.all_gather(block, "ctx", axis=0, tiled=True, axis_index_groups=SAME_CORE)


def own_rows(block):
    return lax.psum_scatter(block, "ctx", scatter_dimension=0, tiled=True, axis_index_groups=SAME_CORE)


def unit_slices(w):
    padded = jnp.pad(w, ((0, 0), (0, 4 * UNITS - w.shape[1])))
    return padded.reshape(w.shape[0], 2, 2, UNITS).transpose(1, 2, 0, 3)


def body(ends, w_query, w_kv, w_out, w_gate_up, w_down, gains, bias_query, bias_kv):
    me = Place()
    rows = w_query.shape[1]
    mine = lax.dynamic_slice(ends[0], (me.h, me.s * OWN, 0), (1, OWN, D))[0]
    other = lax.dynamic_slice(ends[0], (me.h, (1 - me.s) * OWN, 0), (1, OWN, D))[0]
    crossed = lax.ppermute(other, "section", [(0, 1), (1, 0)])
    x = jnp.where(me.s == 0, mine, crossed)
    cotangent = jnp.where(me.s == 0, crossed, mine)

    wq = w_query[0].reshape(rows, 2, 384)
    wo = w_out[0].reshape(rows, 2, 384)
    attn_pieces = jnp.stack(
        [
            jnp.stack(
                [
                    jnp.concatenate([wq[:, s], w_kv[0, :, 0]], axis=1),
                    jnp.concatenate([wo[:, s], w_kv[0, :, 1]], axis=1),
                ]
            )
            for s in range(2)
        ]
    )
    mlp_pieces = jnp.concatenate(
        [unit_slices(w_gate_up[0, :, 0]), unit_slices(w_gate_up[0, :, 1]), unit_slices(w_down[0])], axis=3
    )
    attn_rows, mlp_rows = spread(attn_pieces, mlp_pieces)
    attn_w = [None, None]
    mlp_w = [None, None]
    for l in range(2):
        attn_w[l] = all_rows(attn_rows[l].reshape(2 * rows, QKW))
        mlp_w[l] = all_rows(mlp_rows[l].reshape(2 * rows, 3 * UNITS))

    packed = jnp.concatenate([gains[0].reshape(-1), bias_query[0].reshape(-1), bias_kv[0].reshape(-1)])[None]
    everything = lax.all_gather(packed, ("section", "ctx", "shard"), axis=0, tiled=True).astype(F32)
    everything = everything.reshape(2, 32, 2, 128)
    gain_all = everything[:, :, 0, :96].reshape(2, 32, 2, 48).transpose(0, 2, 1, 3).reshape(2, 2, 1, D)
    bias_all = everything[:, :, :, 96:].reshape(2, 32, 2, 8, 4).transpose(2, 0, 3, 1, 4).reshape(2, 2, 8, 128)
    bias_here = lax.dynamic_index_in_dim(bias_all, me.h, 0, keepdims=False)
    bias_q = lax.dynamic_slice(bias_here, (0, me.s * HEADS, 0), (2, HEADS, 128)).reshape(2, 1, 384)
    bias = jnp.concatenate([bias_q, bias_here[:, 6:8].reshape(2, 1, 256)], axis=2)

    positions = (me.ctx * TOK + jnp.arange(TOK, dtype=jnp.int32)).astype(F32)
    inverse = 1.0 / THETA ** (jnp.arange(0, HD, 2, dtype=F32) / HD)
    angles = positions[:, None] * inverse[None, :]
    cos = jnp.concatenate([jnp.cos(angles), jnp.cos(angles)], axis=1)
    sin = jnp.concatenate([-jnp.sin(angles), jnp.sin(angles)], axis=1)

    inputs, kept = [], []
    for l in range(2):
        inputs.append(x)
        mid, hid, q, kv, att, wf = attn_forward(x, gain_all[l, 0], attn_w[l], bias[l], cos, sin)
        out, hid2, gate, up, prod = mlp_forward(mid, gain_all[l, 1], mlp_w[l])
        kept.append((mid, hid, q, kv, att, wf, hid2, gate, up, prod))
        x = out.astype(BF).astype(F32)

    g = cotangent
    attn_g, mlp_g, gain_g, bias_g = [None, None], [None, None], [None, None], [None, None]
    for l in (1, 0):
        mid, hid, q, kv, att, wf, hid2, gate, up, prod = kept[l]
        gmid, ggain1, dw_mlp = mlp_backward(g, mid, gain_all[l, 1], mlp_w[l], hid2, gate, up, prod)
        mlp_g[l] = own_rows(dw_mlp)
        gin, ggain0, gbias, dw_attn = attn_backward(gmid, inputs[l], gain_all[l, 0], wf, hid, q, kv, att, cos, sin)
        attn_g[l] = own_rows(dw_attn)
        gain_g[l] = jnp.concatenate([ggain0, ggain1], axis=0)
        bias_g[l] = gbias
        g = gin.astype(BF).astype(F32) if l == 1 else gin

    small = jnp.stack(bias_g)
    small = jnp.where(jnp.arange(4)[None, :, None] == me.y, small, 0.0)
    small = jnp.concatenate([jnp.stack(gain_g).reshape(-1), small.reshape(-1)]).reshape(-1, 128)
    small = lax.psum(small, ("section", "ctx", "shard")).reshape(-1)
    gain_sum = small[: 4 * D].reshape(2, 2, 32, 48)
    bias_sum = small[4 * D :].reshape(2, 2, 2, 4, 32, 4)
    gain_sum = lax.dynamic_index_in_dim(gain_sum, me.s, 0, keepdims=False)
    gain_sum = lax.dynamic_index_in_dim(gain_sum, me.ctx, 1, keepdims=False)
    bias_sum = lax.dynamic_index_in_dim(bias_sum, me.s, 0, keepdims=False)
    bias_sum = lax.dynamic_index_in_dim(bias_sum, me.h, 0, keepdims=False)
    bias_sum = lax.dynamic_index_in_dim(bias_sum, me.ctx, 2, keepdims=False)

    attn_home, mlp_home, boundary = gather_back(
        jnp.stack(attn_g).reshape(2, 2, rows, QKW),
        jnp.stack(mlp_g).reshape(2, 2, rows, 3 * UNITS),
        jnp.stack([g, out]),
    )
    attn_home = attn_home.astype(F32)
    mlp_home = mlp_home.astype(F32).reshape(2, 2, rows, 3, UNITS).transpose(2, 3, 0, 1, 4).reshape(rows, 3, 4 * UNITS)
    mlp_home = mlp_home[:, :, : w_down.shape[2]]
    return (
        boundary.reshape(1, 2, TOK, D),
        attn_home[:, 0, :, :384].transpose(1, 0, 2).reshape(1, rows, 768),
        attn_home[:, 0, :, 384:].transpose(1, 0, 2)[None],
        attn_home[:, 1, :, :384].transpose(1, 0, 2).reshape(1, rows, 768),
        mlp_home[:, :2][None],
        mlp_home[:, 2][None],
        gain_sum[None],
        bias_sum[:, :HEADS].reshape(1, 6, 4),
        bias_sum[:, HEADS].reshape(1, 2, 1, 4),
    )


def solution(mesh):
    placed = (
        P("section", None, "ctx", None),
        P("section", "ctx", "shard"),
        P("section", "ctx", None, "shard"),
        P("section", "ctx", "shard"),
        P("section", "ctx", None, "shard"),
        P("section", "ctx", "shard"),
        P("section", None, "ctx"),
        P("section", "shard", "ctx"),
        P("section", None, "shard", "ctx"),
    )
    return jax.shard_map(
        body,
        mesh=mesh,
        in_specs=placed,
        out_specs=(
            P("section", None, "ctx", None),
            P("section", "ctx", "shard"),
            P("section", "ctx", None, "shard"),
            P("section", "ctx", "shard"),
            P("section", "ctx", None, "shard"),
            P("section", "ctx", "shard"),
            P("section", None, "ctx"),
            P("section", "shard", "ctx"),
            P("section", None, "shard", "ctx"),
        ),
        check_vma=False,
    )
```

```python
import jax
import jax.numpy as jnp
from jax import lax
from jax.experimental import pallas as pl
from jax.experimental.pallas import tpu as pltpu
from jax.sharding import PartitionSpec as P

MESH = pl.DeviceIdType.MESH
BF = jnp.bfloat16
F32 = jnp.float32
EPS = 1e-06
THETA = 1000000.0
D = 1536
HD = 128
HEADS = 3
UNITS = 1152
CHUNK = 384
TOK = 64
OWN = 32
QKW = 512
ANY = pl.BlockSpec(memory_space=pl.ANY)
VM = pl.BlockSpec(memory_space=pltpu.VMEM)


class Place:
    def __init__(self):
        self.ctx = lax.axis_index("ctx")
        self.s = lax.axis_index("section")
        self.h = lax.axis_index("shard")
        self.z = self.ctx // 8
        self.x = (self.ctx // 2) % 4
        self.c = self.ctx % 2
        self.y = self.h * 2 + self.s

    def yp(self, k):
        other = (self.y + k) % 4
        return {"section": other % 2, "shard": other // 2}

    def xp(self, k):
        return {"ctx": self.z * 8 + ((self.x + k) % 4) * 2 + self.c}

    def zp(self, k):
        return {"ctx": (self.ctx + 8 * k) % 32}

    def cp(self):
        return {"ctx": self.ctx + 1 - 2 * self.c}


def greet(peers):
    barrier = pltpu.get_barrier_semaphore()
    for peer in peers:
        pl.semaphore_signal(barrier, 1, device_id=peer, device_id_type=MESH)
    pl.semaphore_wait(barrier, len(peers))


class Links:
    def __init__(self, send, recv):
        self.send, self.recv, self.count = send, recv, 0

    def go(self, src, dst, peer):
        index = self.count
        self.count += 1
        copy = pltpu.make_async_remote_copy(
            src, dst, self.send.at[index], self.recv.at[index], device_id=peer, device_id_type=MESH
        )
        copy.start()
        return copy


def landed(copies):
    for copy in copies:
        copy.wait_recv()


def left(copies):
    for copy in copies:
        copy.wait_send()


def dot(a, b, ca=1, cb=0):
    return lax.dot_general(a, b, (((ca,), (cb,)), ((), ())), preferred_element_type=F32)


ORDER = (1, 3, 2)


def unit_rms(u):
    scale = lax.rsqrt(jnp.mean(u * u, axis=1, keepdims=True) + EPS)
    return u * scale, scale


def norm_back(u, gain, dy):
    n, scale = unit_rms(u)
    sd = dy * gain
    return scale * (sd - n * jnp.mean(sd * n, axis=1, keepdims=True)), jnp.sum(dy * n, axis=0, keepdims=True)


def turned(u, cos, sin):
    return u * cos + pltpu.roll(u, 64, 1) * sin


def turned_back(w, cos, sin):
    return w * cos - pltpu.roll(w, 64, 1) * sin


def twice(table):
    return jnp.concatenate([table, table], axis=0)


def key_places(micro_rows):
    j = lax.broadcasted_iota(jnp.int32, (micro_rows, 2048), 1)
    core = j // 1024
    chip = (j % 1024) // TOK
    return chip * (2 * TOK) + core * TOK + j % TOK


def masked(raw, ctx):
    rows = raw.shape[0]
    query = ctx * TOK + lax.broadcasted_iota(jnp.int32, (rows, 2048), 0) % TOK
    return jnp.where(key_places(rows) <= query, raw * (HD**-0.5), -1e30)


def attn_forward_kernel(
    x_ref, gain_ref, w_ref, bias_ref, cos_ref, sin_ref,
    mid_ref, hid_ref, q_ref, kv_ref, att_ref, wf_ref,
    part_ref, got_ref, wsem, send, recv,
):
    me = Place()
    greet([me.yp(1), me.yp(2), me.yp(3), me.xp(1), me.xp(2), me.xp(3), me.zp(1), me.zp(2), me.zp(3), me.cp()])
    net = Links(send, recv)
    weights_over = net.go(w_ref, wf_ref.at[me.c], me.cp())
    weights_here = pltpu.make_async_copy(w_ref, wf_ref.at[me.c], wsem)
    weights_here.start()
    x = x_ref[...]
    normed, _ = unit_rms(x)
    hid_ref[me.y] = (normed * gain_ref[...]).astype(BF)
    hid_copies = [net.go(hid_ref.at[me.y], hid_ref.at[me.y], me.yp(k)) for k in ORDER]
    cos, sin = twice(cos_ref[...]), twice(sin_ref[...])
    weights_here.wait()
    weights_over.wait()
    landed(hid_copies)
    hidden = hid_ref[...].reshape(2 * TOK, D)
    keyval = []
    proj = dot(hidden, wf_ref[0]) + bias_ref[:, :QKW]
    key = turned(proj[:, 384:], cos, sin).astype(BF)
    value = (dot(hidden, wf_ref[1, :, 384:]) + bias_ref[:, QKW:]).astype(BF)
    keyval = jnp.concatenate([key, value], axis=1)
    for m in range(2):
        kv_ref[me.c, m, me.z, me.x] = keyval[m * TOK : (m + 1) * TOK]
    first0 = [net.go(kv_ref.at[me.c, 0, me.z, me.x], kv_ref.at[me.c, 0, me.z, me.x], me.xp(k)) for k in ORDER]
    first1 = [net.go(kv_ref.at[me.c, 1, me.z, me.x], kv_ref.at[me.c, 1, me.z, me.x], me.zp(k)) for k in ORDER]
    for head in range(HEADS):
        query = turned(proj[:, head * HD : (head + 1) * HD], cos, sin).astype(BF)
        for m in range(2):
            q_ref[m, head] = query[m * TOK : (m + 1) * TOK]
    landed(first0)
    second0 = [net.go(kv_ref.at[me.c, 0, me.z], kv_ref.at[me.c, 0, me.z], me.zp(k)) for k in ORDER]
    landed(first1)
    second1 = [net.go(kv_ref.at[me.c, 1, :, me.x], kv_ref.at[me.c, 1, :, me.x], me.xp(k)) for k in ORDER]
    landed(second0)
    third0 = net.go(kv_ref.at[me.c, 0], kv_ref.at[me.c, 0], me.cp())
    landed(second1)
    third1 = net.go(kv_ref.at[me.c, 1], kv_ref.at[me.c, 1], me.cp())
    for m, third in ((0, third0), (1, third1)):
        third.wait_recv()
        queries = q_ref[m].reshape(HEADS * TOK, HD)
        keys = kv_ref[:, m, :, :, :, :HD].reshape(2048, HD)
        values = kv_ref[:, m, :, :, :, HD:].reshape(2048, HD)
        scores = masked(dot(queries, keys, 1, 1), me.ctx)
        weight = jnp.exp(scores - jnp.max(scores, axis=1, keepdims=True))
        total = jnp.sum(weight, axis=1, keepdims=True)
        out = (dot(weight.astype(BF), values) / total).astype(BF)
        for head in range(HEADS):
            att_ref[m * TOK : (m + 1) * TOK, head * HD : (head + 1) * HD] = out[head * TOK : (head + 1) * TOK]
    part_ref[...] = dot(att_ref[...], wf_ref[1, :, :384], 1, 1).astype(BF).reshape(4, OWN, D)
    back = [net.go(part_ref.at[(me.y + k) % 4], got_ref.at[k - 1], me.yp(k)) for k in ORDER]
    total = x + part_ref[me.y].astype(F32)
    landed(back)
    for k in range(3):
        total = total + got_ref[k].astype(F32)
    mid_ref[...] = total
    left(hid_copies + first0 + first1 + second0 + second1 + [third0, third1] + back)


def attn_forward(x, gain, w_half, bias, cos, sin):
    return pl.pallas_call(
        attn_forward_kernel,
        out_shape=(
            jax.ShapeDtypeStruct((OWN, D), F32),
            jax.ShapeDtypeStruct((4, OWN, D), BF),
            jax.ShapeDtypeStruct((2, HEADS, TOK, HD), BF),
            jax.ShapeDtypeStruct((2, 2, 4, 4, TOK, 2 * HD), BF),
            jax.ShapeDtypeStruct((2 * TOK, HEADS * HD), BF),
            jax.ShapeDtypeStruct((2, D, QKW), BF),
        ),
        in_specs=[VM, VM, ANY, VM, VM, VM],
        out_specs=(VM,) * 6,
        scratch_shapes=[
            pltpu.VMEM((4, OWN, D), BF),
            pltpu.VMEM((3, OWN, D), BF),
            pltpu.SemaphoreType.DMA,
            pltpu.SemaphoreType.DMA((21,)),
            pltpu.SemaphoreType.DMA((21,)),
        ],
        compiler_params=pltpu.CompilerParams(collective_id=0, has_side_effects=True, vmem_limit_bytes=48 << 20),
        name="attn_forward",
    )(x, gain, w_half, bias, cos, sin)


def fetch_mlp(w_ref, w_vmem, sems):
    copies = []
    for part in range(3):
        copy = pltpu.make_async_copy(w_ref.at[:, part * UNITS : (part + 1) * UNITS], w_vmem.at[part], sems.at[part])
        copy.start()
        copies.append(copy)
    return copies


def gather_yc(net, me, buf):
    sent = [net.go(buf.at[me.c, me.y], buf.at[me.c, me.y], me.yp(k)) for k in ORDER]
    crossed = [net.go(buf.at[me.c, me.y], buf.at[me.c, me.y], me.cp())]
    for k, copy in zip(ORDER, sent):
        copy.wait_recv()
        slot = (me.y + 4 - k) % 4
        crossed.append(net.go(buf.at[me.c, slot], buf.at[me.c, slot], me.cp()))
    landed(crossed)
    return sent + crossed


def scatter_yc_start(net, me, part, mate):
    return net.go(part.at[1 - me.c], mate, me.cp())


def scatter_yc_middle(net, me, part, mate, got, swap):
    swap.wait_recv()
    mate[...] = (part[me.c].astype(F32) + mate[...].astype(F32)).astype(BF)
    return [net.go(mate.at[(me.y + k) % 4], got.at[k - 1], me.yp(k)) for k in ORDER]


def scatter_yc_end(me, mate, got, back):
    total = mate[me.y].astype(F32)
    landed(back)
    for k in range(3):
        total = total + got[k].astype(F32)
    return total


def mlp_forward_kernel(
    mid_ref, gain_ref, w_ref,
    out_ref, hid_ref, gate_ref, up_ref, prod_ref,
    w_vmem, acc, part, mate, got, wsem, send, recv,
):
    me = Place()
    weights = fetch_mlp(w_ref, w_vmem, wsem)
    greet([me.yp(1), me.yp(2), me.yp(3), me.cp()])
    net = Links(send, recv)
    normed, _ = unit_rms(mid_ref[...])
    hid_ref[me.c, me.y] = (normed * gain_ref[...]).astype(BF)
    gathered = gather_yc(net, me, hid_ref)
    for copy in weights:
        copy.wait()
    hidden = hid_ref[...].reshape(256, D)
    acc[...] = jnp.zeros_like(acc)

    def step(i, _):
        cols = pl.ds(pl.multiple_of(i * CHUNK, CHUNK), CHUNK)
        gate = dot(hid_ref[...].reshape(256, D), w_vmem[0, :, cols])
        up = dot(hid_ref[...].reshape(256, D), w_vmem[1, :, cols])
        product = (gate * jax.nn.sigmoid(gate) * up).astype(BF)
        gate_ref[:, cols] = gate
        up_ref[:, cols] = up
        prod_ref[:, cols] = product
        acc[...] += dot(product, w_vmem[2, :, cols], 1, 1)
        return 0

    lax.fori_loop(0, UNITS // CHUNK, step, 0)
    part[...] = acc[...].astype(BF).reshape(2, 4, OWN, D)
    swap = scatter_yc_start(net, me, part, mate)
    back = scatter_yc_middle(net, me, part, mate, got, swap)
    out_ref[...] = mid_ref[...] + scatter_yc_end(me, mate, got, back)
    left(gathered + [swap] + back)


def mlp_forward(mid, gain, w):
    return pl.pallas_call(
        mlp_forward_kernel,
        out_shape=(
            jax.ShapeDtypeStruct((OWN, D), F32),
            jax.ShapeDtypeStruct((2, 4, OWN, D), BF),
            jax.ShapeDtypeStruct((256, UNITS), F32),
            jax.ShapeDtypeStruct((256, UNITS), F32),
            jax.ShapeDtypeStruct((256, UNITS), BF),
        ),
        in_specs=[VM, VM, ANY],
        out_specs=(VM,) * 5,
        scratch_shapes=[
            pltpu.VMEM((3, D, UNITS), BF),
            pltpu.VMEM((256, D), F32),
            pltpu.VMEM((2, 4, OWN, D), BF),
            pltpu.VMEM((4, OWN, D), BF),
            pltpu.VMEM((3, OWN, D), BF),
            pltpu.SemaphoreType.DMA((3,)),
            pltpu.SemaphoreType.DMA((11,)),
            pltpu.SemaphoreType.DMA((11,)),
        ],
        compiler_params=pltpu.CompilerParams(collective_id=1, has_side_effects=True, vmem_limit_bytes=48 << 20),
        name="mlp_forward",
    )(mid, gain, w)


def mlp_backward_kernel(
    g_ref, mid_ref, gain_ref, w_ref, hid_ref, gate_ref, up_ref, prod_ref,
    gmid_ref, ggain_ref, dw_ref,
    w_vmem, low, dgate, dup, acc, part, mate, got, wsem, send, recv,
):
    me = Place()
    weights = fetch_mlp(w_ref, w_vmem, wsem)
    greet([me.yp(1), me.yp(2), me.yp(3), me.cp()])
    net = Links(send, recv)
    low[me.c, me.y] = g_ref[...].astype(BF)
    gathered = gather_yc(net, me, low)
    for copy in weights:
        copy.wait()
    acc[...] = jnp.zeros_like(acc)

    def step(i, _):
        cols = pl.ds(pl.multiple_of(i * CHUNK, CHUNK), CHUNK)
        dprod = dot(low[...].reshape(256, D), w_vmem[2, :, cols])
        gate, up = gate_ref[:, cols], up_ref[:, cols]
        sigma = jax.nn.sigmoid(gate)
        dg = (dprod * up * sigma * (1.0 + gate * (1.0 - sigma))).astype(BF)
        du = (dprod * gate * sigma).astype(BF)
        dgate[:, cols] = dg
        dup[:, cols] = du
        acc[...] += dot(dg, w_vmem[0, :, cols], 1, 1) + dot(du, w_vmem[1, :, cols], 1, 1)
        return 0

    lax.fori_loop(0, UNITS // CHUNK, step, 0)
    part[...] = acc[...].astype(BF).reshape(2, 4, OWN, D)
    swap = scatter_yc_start(net, me, part, mate)

    def weight_grads(index, left_ref, right_ref):
        def step_w(i, _):
            cols = pl.ds(pl.multiple_of(i * CHUNK, CHUNK), CHUNK)
            where = pl.ds(pl.multiple_of(index * UNITS + i * CHUNK, CHUNK), CHUNK)
            dw_ref[:, where] = dot(left_ref[...].reshape(256, D), right_ref[:, cols], 0, 0).astype(BF)
            return 0

        lax.fori_loop(0, UNITS // CHUNK, step_w, 0)

    back = scatter_yc_middle(net, me, part, mate, got, swap)
    weight_grads(0, hid_ref, dgate)
    weight_grads(1, hid_ref, dup)
    weight_grads(2, low, prod_ref)
    dy = scatter_yc_end(me, mate, got, back)
    du, ggain_ref[...] = norm_back(mid_ref[...], gain_ref[...], dy)
    gmid_ref[...] = g_ref[...] + du
    left(gathered + [swap] + back)


def mlp_backward(g, mid, gain, w, hid, gate, up, prod):
    return pl.pallas_call(
        mlp_backward_kernel,
        out_shape=(
            jax.ShapeDtypeStruct((OWN, D), F32),
            jax.ShapeDtypeStruct((1, D), F32),
            jax.ShapeDtypeStruct((D, 3 * UNITS), BF),
        ),
        in_specs=[VM, VM, VM, ANY, VM, VM, VM, VM],
        out_specs=(VM,) * 3,
        scratch_shapes=[
            pltpu.VMEM((3, D, UNITS), BF),
            pltpu.VMEM((2, 4, OWN, D), BF),
            pltpu.VMEM((256, UNITS), BF),
            pltpu.VMEM((256, UNITS), BF),
            pltpu.VMEM((256, D), F32),
            pltpu.VMEM((2, 4, OWN, D), BF),
            pltpu.VMEM((4, OWN, D), BF),
            pltpu.VMEM((3, OWN, D), BF),
            pltpu.SemaphoreType.DMA((3,)),
            pltpu.SemaphoreType.DMA((11,)),
            pltpu.SemaphoreType.DMA((11,)),
        ],
        compiler_params=pltpu.CompilerParams(collective_id=2, has_side_effects=True, vmem_limit_bytes=56 << 20),
        name="mlp_backward",
    )(g, mid, gain, w, hid, gate, up, prod)


def attn_backward_kernel(
    gm_ref, x_ref, gain_ref, w_ref, hid_ref, q_ref, kv_ref, att_ref, cos_ref, sin_ref,
    gin_ref, ggain_ref, gbias_ref, dw_ref,
    low, dkv, kmate, kz, kx, k2, k3, kpair, kpair_got, dqs, dws, dw_got, part, got, send, recv,
):
    me = Place()
    greet([me.yp(1), me.yp(2), me.yp(3), me.xp(1), me.xp(2), me.xp(3), me.zp(1), me.zp(2), me.zp(3), me.cp()])
    net = Links(send, recv)
    low[me.y] = gm_ref[...].astype(BF)
    gathered = [net.go(low.at[me.y], low.at[me.y], me.yp(k)) for k in ORDER]
    cos, sin = twice(cos_ref[...]), twice(sin_ref[...])
    landed(gathered)
    grad_mid = low[...].reshape(2 * TOK, D)
    grad_att = dot(grad_mid, w_ref[1, :, :384]).astype(BF)
    for m in range(2):
        rows = slice(m * TOK, (m + 1) * TOK)
        queries = q_ref[m].reshape(HEADS * TOK, HD)
        keys = kv_ref[:, m, :, :, :, :HD].reshape(2048, HD)
        values = kv_ref[:, m, :, :, :, HD:].reshape(2048, HD)
        grad_out = jnp.concatenate([grad_att[rows, h * HD : (h + 1) * HD] for h in range(HEADS)], axis=0)
        scores = masked(dot(queries, keys, 1, 1), me.ctx)
        weight = jnp.exp(scores - jnp.max(scores, axis=1, keepdims=True))
        soft = weight / jnp.sum(weight, axis=1, keepdims=True)
        grad_soft = dot(grad_out, values, 1, 1)
        delta = jnp.sum(soft * grad_soft, axis=1, keepdims=True)
        grad_scores = (soft * (grad_soft - delta)).astype(BF)
        grad_values = dot(soft.astype(BF), grad_out, 0, 0)
        grad_keys = dot(grad_scores, queries, 0, 0) * (HD**-0.5)
        dkv[:, m] = jnp.concatenate([grad_keys, grad_values], axis=1).astype(BF).reshape(2, 4, 4, TOK, 2 * HD)
        dq = dot(grad_scores, keys) * (HD**-0.5)
        for h in range(HEADS):
            dqs[rows, h * HD : (h + 1) * HD] = dq[h * TOK : (h + 1) * TOK]
    swap = net.go(dkv.at[1 - me.c], kmate, me.cp())
    dq_low = jnp.concatenate(
        [turned_back(dqs[:, h * HD : (h + 1) * HD], cos, sin).astype(BF) for h in range(HEADS)], axis=1
    )
    hidden = hid_ref[...].reshape(2 * TOK, D)
    swap.wait_recv()
    kmate[...] = (kmate[...].astype(F32) + dkv[me.c].astype(F32)).astype(BF)
    first0 = [net.go(kmate.at[0, (me.z + k) % 4], kz.at[k - 1], me.zp(k)) for k in ORDER]
    first1 = [net.go(kmate.at[1, :, (me.x + k) % 4], kx.at[k - 1], me.xp(k)) for k in ORDER]
    dws[0, :, :384] = dot(hidden, dq_low, 0, 0).astype(BF)
    dws[1, :, :384] = dot(grad_mid, att_ref[...], 0, 0).astype(BF)
    dws[1, :, 384:] = jnp.zeros((D, HD), BF)
    landed(first0)
    total0 = kmate[0, me.z].astype(F32)
    for k in range(3):
        total0 = total0 + kz[k].astype(F32)
    k2[0] = total0.astype(BF)
    second0 = [net.go(k2.at[0, (me.x + k) % 4], k3.at[0, k - 1], me.xp(k)) for k in ORDER]
    landed(first1)
    total1 = kmate[1, :, me.x].astype(F32)
    for k in range(3):
        total1 = total1 + kx[k].astype(F32)
    k2[1] = total1.astype(BF)
    second1 = [net.go(k2.at[1, (me.z + k) % 4], k3.at[1, k - 1], me.zp(k)) for k in ORDER]
    landed(second0 + second1)
    for m, place in ((0, me.x), (1, me.z)):
        total = k2[m, place].astype(F32)
        for k in range(3):
            total = total + k3[m, k].astype(F32)
        kpair[0, m * TOK : (m + 1) * TOK] = total[:, :HD].astype(BF)
        kpair[1, m * TOK : (m + 1) * TOK] = total[:, HD:].astype(BF)
    pair = net.go(kpair.at[1 - me.s], kpair_got, {"section": 1 - me.s})
    pair.wait_recv()
    total = kpair[me.s].astype(F32) + kpair_got[...].astype(F32)
    dk_low = jnp.where(me.s == 0, turned_back(total, cos, sin), total).astype(BF)
    part[...] = (
        (dot(dq_low, w_ref[0, :, :384], 1, 1) + dot(dk_low, w_ref[me.s, :, 384:], 1, 1)).astype(BF).reshape(4, OWN, D)
    )
    back = [net.go(part.at[(me.y + k) % 4], got.at[k - 1], me.yp(k)) for k in ORDER]
    dws[0, :, 384:] = dot(hidden, dk_low, 0, 0).astype(BF)
    dw_swap = net.go(dws.at[1 - me.c], dw_got, me.cp())
    gbias_ref[:, :384] = jnp.sum(dq_low.astype(F32), axis=0, keepdims=True)
    gbias_ref[:, 384:] = jnp.sum(dk_low.astype(F32), axis=0, keepdims=True)
    dy = part[me.y].astype(F32)
    landed(back)
    for k in range(3):
        dy = dy + got[k].astype(F32)
    dx, ggain_ref[...] = norm_back(x_ref[...], gain_ref[...], dy)
    gin_ref[...] = gm_ref[...] + dx
    dw_swap.wait_recv()
    dw_ref[...] = (dws[me.c].astype(F32) + dw_got[...].astype(F32)).astype(BF)
    left(gathered + [swap] + first0 + first1 + second0 + second1 + [pair] + back + [dw_swap])


def attn_backward(gm, x, gain, w, hid, q, kv, att, cos, sin):
    return pl.pallas_call(
        attn_backward_kernel,
        out_shape=(
            jax.ShapeDtypeStruct((OWN, D), F32),
            jax.ShapeDtypeStruct((1, D), F32),
            jax.ShapeDtypeStruct((1, QKW), F32),
            jax.ShapeDtypeStruct((D, QKW), BF),
        ),
        in_specs=[VM] * 10,
        out_specs=(VM,) * 4,
        scratch_shapes=[
            pltpu.VMEM((4, OWN, D), BF),
            pltpu.VMEM((2, 2, 4, 4, TOK, 2 * HD), BF),
            pltpu.VMEM((2, 4, 4, TOK, 2 * HD), BF),
            pltpu.VMEM((3, 4, TOK, 2 * HD), BF),
            pltpu.VMEM((3, 4, TOK, 2 * HD), BF),
            pltpu.VMEM((2, 4, TOK, 2 * HD), BF),
            pltpu.VMEM((2, 3, TOK, 2 * HD), BF),
            pltpu.VMEM((2, 2 * TOK, HD), BF),
            pltpu.VMEM((2 * TOK, HD), BF),
            pltpu.VMEM((2 * TOK, HEADS * HD), F32),
            pltpu.VMEM((2, D, QKW), BF),
            pltpu.VMEM((D, QKW), BF),
            pltpu.VMEM((4, OWN, D), BF),
            pltpu.VMEM((3, OWN, D), BF),
            pltpu.SemaphoreType.DMA((21,)),
            pltpu.SemaphoreType.DMA((21,)),
        ],
        compiler_params=pltpu.CompilerParams(collective_id=3, has_side_effects=True, vmem_limit_bytes=48 << 20),
        name="attn_backward",
    )(gm, x, gain, w, hid, q, kv, att, cos, sin)


def quad(me):
    return (
        (me.c, 1 - me.s, {"section": 1 - me.s}),
        (1 - me.c, me.s, me.cp()),
        (1 - me.c, 1 - me.s, {"section": 1 - me.s, "ctx": me.ctx + 1 - 2 * me.c}),
    )


def spread_kernel(attn_ref, mlp_ref, tiny_ref, ends_ref, attn_out, mlp_out, tiny_out, ends_out, lsem, send, recv):
    me = Place()
    peers = quad(me)
    greet([peer for _, _, peer in peers])
    net = Links(send, recv)
    copies, here = [], []
    away = pl.ds(pl.multiple_of((1 - me.s) * OWN, OWN), OWN)
    home = pl.ds(pl.multiple_of(me.s * OWN, OWN), OWN)
    for core, section, peer in peers:
        copies.append(net.go(attn_ref.at[section, core], attn_out.at[me.s, me.c], peer))
        copies.append(net.go(tiny_ref, tiny_out.at[me.s, me.c], peer))
    copies.append(net.go(ends_ref.at[me.h, away], ends_out.at[me.s], {"section": 1 - me.s}))
    for core, section, peer in peers:
        copies.append(net.go(mlp_ref.at[section, core], mlp_out.at[me.s, me.c], peer))
    pairs = (
        (attn_ref.at[me.s, me.c], attn_out.at[me.s, me.c]),
        (tiny_ref, tiny_out.at[me.s, me.c]),
        (ends_ref.at[me.h, home], ends_out.at[me.s]),
        (mlp_ref.at[me.s, me.c], mlp_out.at[me.s, me.c]),
    )
    for i, (src, dst) in enumerate(pairs):
        here.append(pltpu.make_async_copy(src, dst, lsem.at[i]))
        here[-1].start()
    for copy in here + copies:
        copy.wait()


def spread(attn, mlp, tiny, ends):
    return pl.pallas_call(
        spread_kernel,
        out_shape=(
            jax.ShapeDtypeStruct(attn.shape, BF),
            jax.ShapeDtypeStruct(mlp.shape, BF),
            jax.ShapeDtypeStruct((2, 2) + tiny.shape, BF),
            jax.ShapeDtypeStruct((2, OWN, D), F32),
        ),
        in_specs=[ANY] * 4,
        out_specs=(ANY,) * 4,
        scratch_shapes=[
            pltpu.SemaphoreType.DMA((4,)),
            pltpu.SemaphoreType.DMA((10,)),
            pltpu.SemaphoreType.DMA((10,)),
        ],
        compiler_params=pltpu.CompilerParams(collective_id=4, has_side_effects=True),
        name="spread",
    )(attn, mlp, tiny, ends)


def cuts(columns):
    cut = (columns // 256) * 128
    return (slice(0, cut), slice(cut, columns))


SIDES = (1, 3)


class Gather:
    def __init__(self, net, me, src, buf, local):
        self.net, self.me, self.src, self.buf, self.local = net, me, src, buf, local
        self.cuts = cuts(src.shape[-1])
        self.sent = []

    def at(self, half, p, q):
        return self.buf.at[q, p, 0] if half == 0 else self.buf.at[p, q, 1]

    def axes(self, half):
        me = self.me
        return (me.x, me.z, me.xp, me.zp) if half == 0 else (me.z, me.x, me.zp, me.xp)

    def go(self, src, dst, peer):
        copy = self.net.go(src, dst, peer)
        self.sent.append(copy)
        return copy

    def start(self):
        me = self.me
        self.own = pltpu.make_async_copy(self.src, self.buf.at[me.z, me.x], self.local)
        self.own.start()
        self.a, self.c = [None, None], [[None] * 4, [None] * 4]
        for half in range(2):
            p, q, pp, qp = self.axes(half)
            self.a[half] = [self.go(self.src.at[half], self.at(half, p, q), pp(k)) for k in SIDES]
        for half in range(2):
            p, q, pp, qp = self.axes(half)
            self.c[half][0] = [self.go(self.src.at[half], self.at(half, p, q), qp(k)) for k in SIDES]

    def second(self):
        self.f = [[], []]
        for half in range(2):
            p, q, pp, qp = self.axes(half)
            for i, k in enumerate(SIDES):
                self.a[half][i].wait_recv()
                block = self.at(half, (p + 4 - k) % 4, q)
                piece = block.at[:, self.cuts[i]]
                self.f[half].append(self.go(piece, piece, pp(k)))
        for half in range(2):
            p, q, pp, qp = self.axes(half)
            for i, k in enumerate(SIDES):
                block = self.at(half, (p + 4 - k) % 4, q)
                self.c[half][i + 1] = [self.go(block, block, qp(kk)) for kk in SIDES]

    def third(self):
        for half in range(2):
            p, q, pp, qp = self.axes(half)
            landed(self.f[half])
            block = self.at(half, (p + 2) % 4, q)
            self.c[half][3] = [self.go(block, block, qp(kk)) for kk in SIDES]

    def fourth(self):
        self.last = []
        for j, shift in enumerate((0, 3, 1, 2)):
            for half in range(2):
                p, q, pp, qp = self.axes(half)
                for i, k in enumerate(SIDES):
                    self.c[half][j][i].wait_recv()
                    piece = self.at(half, (p + shift) % 4, (q + 4 - k) % 4).at[:, self.cuts[i]]
                    self.last.append(self.go(piece, piece, qp(k)))

    def finish(self):
        landed(self.last)
        self.own.wait()
        left(self.sent)

    copies = 40


def collect_kernel(a0, a1, m0, tiny, a0_out, a1_out, m0_out, tiny_out, lsem, send, recv):
    me = Place()
    greet([me.xp(1), me.xp(2), me.xp(3), me.zp(1), me.zp(2), me.zp(3)])
    net = Links(send, recv)
    parts = [Gather(net, me, src, dst, lsem.at[i]) for i, (src, dst) in enumerate(((a0, a0_out), (m0, m0_out), (a1, a1_out)))]
    here = pltpu.make_async_copy(tiny, tiny_out.at[me.z, me.x], lsem.at[3])
    here.start()
    one = [net.go(tiny, tiny_out.at[me.z, me.x], me.xp(k)) for k in ORDER]
    for part in parts:
        part.start()
    here.wait()
    landed(one)
    two = [net.go(tiny_out.at[me.z], tiny_out.at[me.z], me.zp(k)) for k in ORDER]
    for part in parts:
        part.second()
    for part in parts:
        part.third()
    for part in parts:
        part.fourth()
    for part in parts:
        part.finish()
    landed(two)
    left(one + two)


def collect(a0, a1, m0, tiny):
    return pl.pallas_call(
        collect_kernel,
        out_shape=tuple(jax.ShapeDtypeStruct((4, 4) + array.shape, BF) for array in (a0, a1, m0, tiny)),
        in_specs=[ANY] * 4,
        out_specs=(ANY,) * 4,
        scratch_shapes=[
            pltpu.SemaphoreType.DMA((4,)),
            pltpu.SemaphoreType.DMA((3 * Gather.copies + 6,)),
            pltpu.SemaphoreType.DMA((3 * Gather.copies + 6,)),
        ],
        compiler_params=pltpu.CompilerParams(collective_id=6, has_side_effects=True),
        name="collect",
    )(a0, a1, m0, tiny)


class Scatter:
    copies = 16

    def __init__(self, net, me, src, buf, r1, r2, t, u1, u2, out, local):
        self.net, self.me, self.src, self.buf, self.local = net, me, src, buf, local
        self.r1, self.r2, self.t, self.u1, self.u2, self.out = r1, r2, t, u1, u2, out
        self.cuts = cuts(src.shape[-1])
        self.sent = []

    @staticmethod
    def scratch(rows, columns):
        wide = columns - (columns // 256) * 128
        return [
            pltpu.VMEM((4, 4, 2, rows, columns), BF),
            pltpu.VMEM((2, 2, 4, rows, wide), BF),
            pltpu.VMEM((2, 2, 4, rows, columns), BF),
            pltpu.VMEM((2, 4, rows, columns), BF),
            pltpu.VMEM((2, 2, rows, wide), BF),
            pltpu.VMEM((2, 2, rows, columns), BF),
        ]

    def group(self, ref, half, q):
        return ref.at[q, :, 0] if half == 0 else ref.at[:, q, 1]

    def axes(self, half):
        me = self.me
        return (me.x, me.z, me.xp, me.zp) if half == 0 else (me.z, me.x, me.zp, me.xp)

    def go(self, src, dst, peer):
        copy = self.net.go(src, dst, peer)
        self.sent.append(copy)
        return copy

    def wide(self, i):
        return slice(0, self.cuts[i].stop - self.cuts[i].start)

    def start(self):
        self.one = [[], []]
        for half in range(2):
            p, q, pp, qp = self.axes(half)
            for i, k in enumerate(SIDES):
                piece = self.group(self.src, half, (q + 2) % 4).at[:, :, self.cuts[i]]
                self.one[half].append(self.go(piece, self.r1.at[half, i, :, :, self.wide(i)], qp(k)))
        self.load = pltpu.make_async_copy(self.src, self.buf, self.local)
        self.load.start()

    def second(self):
        self.load.wait()
        self.two = [[], []]
        for i, k in enumerate(SIDES):
            for half in range(2):
                p, q, pp, qp = self.axes(half)
                self.one[half][i].wait_recv()
                mine = self.group(self.buf, half, (q + k) % 4)

                def add(j, _):
                    mine[j, :, self.cuts[i]] = (
                        mine[j, :, self.cuts[i]].astype(F32) + self.r1[half, i, j, :, self.wide(i)].astype(F32)
                    ).astype(BF)
                    return 0

                lax.fori_loop(0, 4, add, 0)
                self.two[half].append(self.go(mine, self.r2.at[half, i], qp(k)))

    def third(self):
        self.three = [[], []]
        for half in range(2):
            p, q, pp, qp = self.axes(half)
            landed(self.two[half])
            mine = self.group(self.buf, half, q)

            def add(j, _):
                self.t[half, j] = (
                    mine[j].astype(F32) + self.r2[half, 0, j].astype(F32) + self.r2[half, 1, j].astype(F32)
                ).astype(BF)
                return 0

            lax.fori_loop(0, 4, add, 0)
            for i, k in enumerate(SIDES):
                self.three[half].append(
                    self.go(self.t.at[half, (p + 2) % 4, :, self.cuts[i]], self.u1.at[half, i, :, self.wide(i)], pp(k))
                )

    def fourth(self):
        self.four = [[], []]
        for half in range(2):
            p, q, pp, qp = self.axes(half)
            for i, k in enumerate(SIDES):
                self.three[half][i].wait_recv()
                place = (p + k) % 4
                self.t[half, place, :, self.cuts[i]] = (
                    self.t[half, place, :, self.cuts[i]].astype(F32) + self.u1[half, i, :, self.wide(i)].astype(F32)
                ).astype(BF)
                self.four[half].append(self.go(self.t.at[half, place], self.u2.at[half, i], pp(k)))

    def fifth(self, half):
        p, q, pp, qp = self.axes(half)
        landed(self.four[half])
        self.out[half] = (
            self.t[half, p].astype(F32) + self.u2[half, 0].astype(F32) + self.u2[half, 1].astype(F32)
        ).astype(BF)

    def finish(self):
        left(self.sent)


def deposit_kernel(
    a1, a0, m0, m1, small, ends,
    attn_out, mlp_out, small_out, ends_out,
    *scratch,
):
    me = Place()
    peers = quad(me)
    greet(
        [me.yp(1), me.yp(2), me.yp(3), me.xp(1), me.xp(2), me.xp(3), me.zp(1), me.zp(2), me.zp(3), me.cp()]
        + [peers[2][2]]
    )
    res_a, res_m, sum_c, sum_got, lsem, send, recv = scratch[18:]
    net = Links(send, recv)
    scatters = [
        Scatter(net, me, src, *scratch[6 * i : 6 * i + 6], out, lsem.at[i])
        for i, (src, out) in enumerate(((m0, res_m.at[0]), (a0, res_a.at[0]), (a1, res_a.at[1])))
    ]
    for scatter in scatters:
        scatter.start()
    copies = []
    sum_c[0] = small[...]
    rounds = ((me.yp, ORDER), (lambda k: me.cp(), (1,)), (me.xp, ORDER), (me.zp, ORDER))

    def small_round(turn, slot):
        peer, ks = rounds[turn]
        sent = [net.go(sum_c.at[turn], sum_got.at[slot + k - 1], peer(k)) for k in ks]
        copies.extend(sent)
        landed(sent)
        total = sum_c[turn]
        for k in ks:
            total = total + sum_got[slot + k - 1]
        sum_c[turn + 1] = total

    small_round(0, 0)
    small_round(1, 3)
    crossed = [net.go(ends.at[((me.y + k) % 4) % 2], ends_out.at[me.y], me.yp(k)) for k in ORDER]
    here = [
        pltpu.make_async_copy(ends.at[me.s], ends_out.at[me.y], lsem.at[3]),
        pltpu.make_async_copy(m1, res_m.at[1], lsem.at[4]),
    ]
    for copy in here:
        copy.start()
    for scatter in scatters:
        scatter.second()
    small_round(2, 4)
    small_round(3, 7)
    for scatter in scatters:
        scatter.third()
    for scatter in scatters:
        scatter.fourth()
    for scatter in scatters:
        scatter.fifth(0)
        scatter.fifth(1)
    here[1].wait()
    last = []
    for core, section, peer in peers:
        last.append(net.go(res_a.at[section, core], attn_out.at[me.s, me.c], peer))
        last.append(net.go(res_m.at[section, core], mlp_out.at[me.s, me.c], peer))
    for i, (res, out) in enumerate(((res_a, attn_out), (res_m, mlp_out))):
        here.append(pltpu.make_async_copy(res.at[me.s, me.c], out.at[me.s, me.c], lsem.at[5 + i]))
        here[-1].start()
    small_out[...] = sum_c[4]
    here[0].wait()
    here[2].wait()
    here[3].wait()
    landed(crossed + last)
    left(copies + crossed + last)
    for scatter in scatters:
        scatter.finish()


def deposit(a1, a0, m0, m1, small, ends):
    rows = m1.shape[1]
    shape = lambda array: array.reshape(4, 4, 2, rows, -1)
    scratch = [
        ref for columns in (3 * UNITS, QKW, QKW) for ref in Scatter.scratch(rows, columns)[:6]
    ]
    return pl.pallas_call(
        deposit_kernel,
        out_shape=(
            jax.ShapeDtypeStruct((2, 2, rows, QKW), BF),
            jax.ShapeDtypeStruct((2, 2, rows, 3 * UNITS), BF),
            jax.ShapeDtypeStruct(small.shape, F32),
            jax.ShapeDtypeStruct((4, OWN, D), F32),
        ),
        in_specs=[ANY, ANY, ANY, ANY, VM, ANY],
        out_specs=(ANY, ANY, VM, ANY),
        scratch_shapes=scratch
        + [
            pltpu.VMEM((2, 2, rows, QKW), BF),
            pltpu.VMEM((2, 2, rows, 3 * UNITS), BF),
            pltpu.VMEM((5,) + small.shape, F32),
            pltpu.VMEM((10,) + small.shape, F32),
            pltpu.SemaphoreType.DMA((7,)),
            pltpu.SemaphoreType.DMA((3 * Scatter.copies + 19,)),
            pltpu.SemaphoreType.DMA((3 * Scatter.copies + 19,)),
        ],
        compiler_params=pltpu.CompilerParams(collective_id=5, has_side_effects=True, vmem_limit_bytes=56 << 20),
        name="deposit",
    )(shape(a1), shape(a0), shape(m0), m1, small, ends)


SAME_CORE = [[core + 2 * chip for chip in range(16)] for core in range(2)]


def all_rows(block):
    return lax.all_gather(block, "ctx", axis=0, tiled=True, axis_index_groups=SAME_CORE)


def own_rows(block):
    return lax.psum_scatter(block, "ctx", scatter_dimension=0, tiled=True, axis_index_groups=SAME_CORE)


def unit_slices(w):
    padded = jnp.pad(w, ((0, 0), (0, 4 * UNITS - w.shape[1])))
    return padded.reshape(w.shape[0], 2, 2, UNITS).transpose(1, 2, 0, 3)


def body(ends, w_query, w_kv, w_out, w_gate_up, w_down, gains, bias_query, bias_kv):
    me = Place()
    rows = w_query.shape[1]
    wq = w_query[0].reshape(rows, 2, 384)
    wo = w_out[0].reshape(rows, 2, 384)
    attn_pieces = jnp.stack(
        [
            jnp.stack(
                [
                    jnp.concatenate([wq[:, s], w_kv[0, :, 0]], axis=1),
                    jnp.concatenate([wo[:, s], w_kv[0, :, 1]], axis=1),
                ]
            )
            for s in range(2)
        ]
    )
    mlp_pieces = jnp.concatenate(
        [unit_slices(w_gate_up[0, :, 0]), unit_slices(w_gate_up[0, :, 1]), unit_slices(w_down[0])], axis=3
    )
    packed = jnp.concatenate([gains[0].reshape(-1), bias_query[0].reshape(-1), bias_kv[0].reshape(-1)])[None]
    attn_rows, mlp_rows, tiny_rows, tokens = spread(
        attn_pieces, mlp_pieces, jnp.pad(packed, ((0, 15), (0, 0))), ends[0]
    )
    mlp_w1 = all_rows(mlp_rows[1].reshape(2 * rows, 3 * UNITS))
    attn_w0, attn_w1, mlp_w0, tiny_all = collect(attn_rows[0], attn_rows[1], mlp_rows[0], tiny_rows)
    attn_w = [attn_w0.reshape(D, QKW), attn_w1.reshape(D, QKW)]
    mlp_w = [mlp_w0.reshape(D, 3 * UNITS), mlp_w1]

    everything = tiny_all[:, :, :, :, 0].reshape(16, 2, 2, 128).astype(F32)
    gain_all = everything[..., :96].reshape(16, 2, 2, 2, 48).transpose(1, 3, 0, 2, 4).reshape(2, 2, 1, D)
    bias_here = everything[..., 96:].reshape(16, 2, 2, 8, 4).transpose(1, 3, 0, 2, 4).reshape(2, 8, 128)
    bias_q = lax.dynamic_slice(bias_here, (0, me.s * HEADS, 0), (2, HEADS, 128)).reshape(2, 1, 384)
    bias = jnp.concatenate([bias_q, bias_here[:, 6:8].reshape(2, 1, 256)], axis=2)

    positions = (me.ctx * TOK + jnp.arange(TOK, dtype=jnp.int32)).astype(F32)
    inverse = 1.0 / THETA ** (jnp.arange(0, HD, 2, dtype=F32) / HD)
    angles = positions[:, None] * inverse[None, :]
    cos = jnp.concatenate([jnp.cos(angles), jnp.cos(angles)], axis=1)
    sin = jnp.concatenate([-jnp.sin(angles), jnp.sin(angles)], axis=1)

    x = tokens[0]
    inputs, kept = [], []
    for l in range(2):
        inputs.append(x)
        mid, hid, q, kv, att, wf = attn_forward(x, gain_all[l, 0], attn_w[l], bias[l], cos, sin)
        out, hid2, gate, up, prod = mlp_forward(mid, gain_all[l, 1], mlp_w[l])
        kept.append((mid, hid, q, kv, att, wf, hid2, gate, up, prod))
        x = out.astype(BF).astype(F32)

    g = tokens[1]
    attn_g, mlp_g, gain_g, bias_g = [None, None], [None, None], [None, None], [None, None]
    for l in (1, 0):
        mid, hid, q, kv, att, wf, hid2, gate, up, prod = kept[l]
        gmid, ggain1, mlp_g[l] = mlp_backward(g, mid, gain_all[l, 1], mlp_w[l], hid2, gate, up, prod)
        if l == 1:
            mlp_own1 = own_rows(mlp_g[1]).reshape(2, rows, 3 * UNITS)
        gin, ggain0, gbias, attn_g[l] = attn_backward(gmid, inputs[l], gain_all[l, 0], wf, hid, q, kv, att, cos, sin)
        gain_g[l] = jnp.concatenate([ggain0, ggain1], axis=0)
        bias_g[l] = gbias
        g = gin.astype(BF).astype(F32) if l == 1 else gin

    small = jnp.stack(bias_g)
    small = jnp.where(jnp.arange(4)[None, :, None] == me.y, small, 0.0)
    small = jnp.concatenate([jnp.stack(gain_g).reshape(-1), small.reshape(-1)]).reshape(-1, 128)
    attn_home, mlp_home, small, boundary = deposit(
        attn_g[1], attn_g[0], mlp_g[0], mlp_own1, small, jnp.stack([g, out])
    )
    small = small.reshape(-1)
    gain_sum = small[: 4 * D].reshape(2, 2, 32, 48)
    bias_sum = small[4 * D :].reshape(2, 2, 2, 4, 32, 4)
    gain_sum = lax.dynamic_index_in_dim(gain_sum, me.s, 0, keepdims=False)
    gain_sum = lax.dynamic_index_in_dim(gain_sum, me.ctx, 1, keepdims=False)
    bias_sum = lax.dynamic_index_in_dim(bias_sum, me.s, 0, keepdims=False)
    bias_sum = lax.dynamic_index_in_dim(bias_sum, me.h, 0, keepdims=False)
    bias_sum = lax.dynamic_index_in_dim(bias_sum, me.ctx, 2, keepdims=False)

    attn_home = attn_home.astype(F32)
    mlp_home = mlp_home.astype(F32).reshape(2, 2, rows, 3, UNITS).transpose(2, 3, 0, 1, 4).reshape(rows, 3, 4 * UNITS)
    mlp_home = mlp_home[:, :, : w_down.shape[2]]
    return (
        boundary.reshape(1, 2, TOK, D),
        attn_home[:, 0, :, :384].transpose(1, 0, 2).reshape(1, rows, 768),
        attn_home[:, 0, :, 384:].transpose(1, 0, 2)[None],
        attn_home[:, 1, :, :384].transpose(1, 0, 2).reshape(1, rows, 768),
        mlp_home[:, :2][None],
        mlp_home[:, 2][None],
        gain_sum[None],
        bias_sum[:, :HEADS].reshape(1, 6, 4),
        bias_sum[:, HEADS].reshape(1, 2, 1, 4),
    )


def solution(mesh):
    placed = (
        P("section", None, "ctx", None),
        P("section", "ctx", "shard"),
        P("section", "ctx", None, "shard"),
        P("section", "ctx", "shard"),
        P("section", "ctx", None, "shard"),
        P("section", "ctx", "shard"),
        P("section", None, "ctx"),
        P("section", "shard", "ctx"),
        P("section", None, "shard", "ctx"),
    )
    return jax.shard_map(
        body,
        mesh=mesh,
        in_specs=placed,
        out_specs=(
            P("section", None, "ctx", None),
            P("section", "ctx", "shard"),
            P("section", "ctx", None, "shard"),
            P("section", "ctx", "shard"),
            P("section", "ctx", None, "shard"),
            P("section", "ctx", "shard"),
            P("section", None, "ctx"),
            P("section", "shard", "ctx"),
            P("section", None, "shard", "ctx"),
        ),
        check_vma=False,
    )
```

```python
import functools

import jax
import jax.numpy as jnp
from jax import lax
from jax.experimental import pallas as pl
from jax.experimental.pallas import tpu as pltpu
from jax.sharding import PartitionSpec as P

MESH = pl.DeviceIdType.MESH
BF = jnp.bfloat16
F32 = jnp.float32
EPS = 1e-06
THETA = 1000000.0
D = 1536
HD = 128
HEADS = 3
UNITS = 1152
CHUNK = 384
TOK = 64
OWN = 32
QKW = 512
ANY = pl.BlockSpec(memory_space=pl.ANY)
VM = pl.BlockSpec(memory_space=pltpu.VMEM)


class Place:
    def __init__(self):
        self.ctx = lax.axis_index("ctx")
        self.s = lax.axis_index("section")
        self.h = lax.axis_index("shard")
        self.z = self.ctx // 8
        self.x = (self.ctx // 2) % 4
        self.c = self.ctx % 2
        self.y = self.h * 2 + self.s

    def yp(self, k):
        other = (self.y + k) % 4
        return {"section": other % 2, "shard": other // 2}

    def xp(self, k):
        return {"ctx": self.z * 8 + ((self.x + k) % 4) * 2 + self.c}

    def zp(self, k):
        return {"ctx": (self.ctx + 8 * k) % 32}

    def cp(self):
        return {"ctx": self.ctx + 1 - 2 * self.c}


def greet(peers):
    barrier = pltpu.get_barrier_semaphore()
    for peer in peers:
        pl.semaphore_signal(barrier, 1, device_id=peer, device_id_type=MESH)
    pl.semaphore_wait(barrier, len(peers))


class Links:
    def __init__(self, send, recv):
        self.send, self.recv, self.count = send, recv, 0

    def go(self, src, dst, peer):
        index = self.count
        self.count += 1
        copy = pltpu.make_async_remote_copy(
            src, dst, self.send.at[index], self.recv.at[index], device_id=peer, device_id_type=MESH
        )
        copy.start()
        return copy


def landed(copies):
    for copy in copies:
        copy.wait_recv()


def left(copies):
    for copy in copies:
        copy.wait_send()


def dot(a, b, ca=1, cb=0):
    return lax.dot_general(a, b, (((ca,), (cb,)), ((), ())), preferred_element_type=F32)


ORDER = (1, 3, 2)


def cuts(columns):
    cut = (columns // 256) * 128
    return (slice(0, cut), slice(cut, columns))


SIDES = (1, 3)


class Gather:
    def __init__(self, net, me, src, buf, local):
        self.net, self.me, self.src, self.buf, self.local = net, me, src, buf, local
        self.cuts = cuts(src.shape[-1])
        self.sent = []

    def at(self, half, p, q):
        return self.buf.at[q, p, 0] if half == 0 else self.buf.at[p, q, 1]

    def axes(self, half):
        me = self.me
        return (me.x, me.z, me.xp, me.zp) if half == 0 else (me.z, me.x, me.zp, me.xp)

    def go(self, src, dst, peer):
        copy = self.net.go(src, dst, peer)
        self.sent.append(copy)
        return copy

    def start(self):
        me = self.me
        self.own = pltpu.make_async_copy(self.src, self.buf.at[me.z, me.x], self.local)
        self.own.start()
        self.a, self.c = [None, None], [[None] * 4, [None] * 4]
        for half in range(2):
            p, q, pp, qp = self.axes(half)
            self.a[half] = [self.go(self.src.at[half], self.at(half, p, q), pp(k)) for k in SIDES]
        for half in range(2):
            p, q, pp, qp = self.axes(half)
            self.c[half][0] = [self.go(self.src.at[half], self.at(half, p, q), qp(k)) for k in SIDES]

    def second(self):
        self.f = [[], []]
        for half in range(2):
            p, q, pp, qp = self.axes(half)
            for i, k in enumerate(SIDES):
                self.a[half][i].wait_recv()
                block = self.at(half, (p + 4 - k) % 4, q)
                piece = block.at[:, self.cuts[i]]
                self.f[half].append(self.go(piece, piece, pp(k)))
        for half in range(2):
            p, q, pp, qp = self.axes(half)
            for i, k in enumerate(SIDES):
                block = self.at(half, (p + 4 - k) % 4, q)
                self.c[half][i + 1] = [self.go(block, block, qp(kk)) for kk in SIDES]

    def third(self):
        for half in range(2):
            p, q, pp, qp = self.axes(half)
            landed(self.f[half])
            block = self.at(half, (p + 2) % 4, q)
            self.c[half][3] = [self.go(block, block, qp(kk)) for kk in SIDES]
        self.last = []
        self.onward((0,))

    def fourth(self):
        self.onward((1, 2, 3))

    def onward(self, turns):
        for j in turns:
            shift = (0, 3, 1, 2)[j]
            for half in range(2):
                p, q, pp, qp = self.axes(half)
                for i, k in enumerate(SIDES):
                    self.c[half][j][i].wait_recv()
                    piece = self.at(half, (p + shift) % 4, (q + 4 - k) % 4).at[:, self.cuts[i]]
                    self.last.append(self.go(piece, piece, qp(k)))

    def finish(self):
        landed(self.last)
        self.own.wait()
        left(self.sent)

    copies = 40

    def steps(self):
        return [self.start, self.second, self.third, self.fourth, self.finish]


class Scatter:
    copies = 16

    def __init__(self, net, me, src, buf, r1, r2, t, u1, u2, out, local):
        self.net, self.me, self.src, self.buf, self.local = net, me, src, buf, local
        self.r1, self.r2, self.t, self.u1, self.u2, self.out = r1, r2, t, u1, u2, out
        self.cuts = cuts(src.shape[-1])
        self.sent = []

    @staticmethod
    def scratch(rows, columns):
        wide = columns - (columns // 256) * 128
        return [
            pltpu.VMEM((4, 4, 2, rows, columns), BF),
            pltpu.VMEM((2, 2, 4, rows, wide), BF),
            pltpu.VMEM((2, 2, 4, rows, columns), BF),
            pltpu.VMEM((2, 4, rows, columns), BF),
            pltpu.VMEM((2, 2, rows, wide), BF),
            pltpu.VMEM((2, 2, rows, columns), BF),
        ]

    def group(self, ref, half, q):
        return ref.at[q, :, 0] if half == 0 else ref.at[:, q, 1]

    def axes(self, half):
        me = self.me
        return (me.x, me.z, me.xp, me.zp) if half == 0 else (me.z, me.x, me.zp, me.xp)

    def go(self, src, dst, peer):
        copy = self.net.go(src, dst, peer)
        self.sent.append(copy)
        return copy

    def wide(self, i):
        return slice(0, self.cuts[i].stop - self.cuts[i].start)

    def start(self):
        self.one = [[], []]
        for half in range(2):
            p, q, pp, qp = self.axes(half)
            for i, k in enumerate(SIDES):
                piece = self.group(self.src, half, (q + 2) % 4).at[:, :, self.cuts[i]]
                self.one[half].append(self.go(piece, self.r1.at[half, i, :, :, self.wide(i)], qp(k)))
        self.load = pltpu.make_async_copy(self.src, self.buf, self.local)
        self.load.start()

    def second(self):
        self.load.wait()
        self.two = [[], []]
        for i, k in enumerate(SIDES):
            for half in range(2):
                p, q, pp, qp = self.axes(half)
                self.one[half][i].wait_recv()
                mine = self.group(self.buf, half, (q + k) % 4)

                def add(j, _):
                    mine[j, :, self.cuts[i]] = (
                        mine[j, :, self.cuts[i]].astype(F32) + self.r1[half, i, j, :, self.wide(i)].astype(F32)
                    ).astype(BF)
                    return 0

                lax.fori_loop(0, 4, add, 0)
                self.two[half].append(self.go(mine, self.r2.at[half, i], qp(k)))

    def third(self):
        self.three = [[], []]
        for half in range(2):
            p, q, pp, qp = self.axes(half)
            landed(self.two[half])
            mine = self.group(self.buf, half, q)

            def add(j, _):
                self.t[half, j] = (
                    mine[j].astype(F32) + self.r2[half, 0, j].astype(F32) + self.r2[half, 1, j].astype(F32)
                ).astype(BF)
                return 0

            lax.fori_loop(0, 4, add, 0)
            for i, k in enumerate(SIDES):
                self.three[half].append(
                    self.go(self.t.at[half, (p + 2) % 4, :, self.cuts[i]], self.u1.at[half, i, :, self.wide(i)], pp(k))
                )

    def fourth(self):
        self.four = [[], []]
        for half in range(2):
            p, q, pp, qp = self.axes(half)
            for i, k in enumerate(SIDES):
                self.three[half][i].wait_recv()
                place = (p + k) % 4
                self.t[half, place, :, self.cuts[i]] = (
                    self.t[half, place, :, self.cuts[i]].astype(F32) + self.u1[half, i, :, self.wide(i)].astype(F32)
                ).astype(BF)
                self.four[half].append(self.go(self.t.at[half, place], self.u2.at[half, i], pp(k)))

    def fifth(self, half):
        p, q, pp, qp = self.axes(half)
        landed(self.four[half])
        self.out[half] = (
            self.t[half, p].astype(F32) + self.u2[half, 0].astype(F32) + self.u2[half, 1].astype(F32)
        ).astype(BF)

    def end(self):
        self.fifth(0)
        self.fifth(1)

    def finish(self):
        left(self.sent)

    def steps(self):
        return [self.start, self.second, self.third, self.fourth, self.end, self.finish]


class Beside:
    def __init__(self, jobs):
        self.turns = [list(job.steps()) for job in jobs]

    def step(self):
        for turns in self.turns:
            if turns:
                turns.pop(0)()

    def rest(self):
        while any(self.turns):
            self.step()


def gather_jobs(net, me, views, bufs, lsem):
    return Beside([Gather(net, me, src, buf, lsem.at[i]) for i, (src, buf) in enumerate(zip(views, bufs))])


def scatter_jobs(net, me, srcs, outs, scratch, lsem):
    return Beside(
        [Scatter(net, me, src, *scratch[6 * i : 6 * i + 6], out, lsem.at[i]) for i, (src, out) in enumerate(zip(srcs, outs))]
    )


def xz(me):
    return [me.xp(1), me.xp(2), me.xp(3), me.zp(1), me.zp(2), me.zp(3)]


def sems(count, jobs, kind):
    total = count + jobs * kind.copies
    return [pltpu.SemaphoreType.DMA((max(jobs, 1),)), pltpu.SemaphoreType.DMA((total,)), pltpu.SemaphoreType.DMA((total,))]


def params(collective_id):
    return pltpu.CompilerParams(collective_id=collective_id, has_side_effects=True, vmem_limit_bytes=60 << 20)


def gathered(views):
    return tuple(jax.ShapeDtypeStruct((4, 4, 2, view[2], view[1].stop - view[1].start), BF) for view in views)


def view_of(rows_ref, view):
    return rows_ref.at[view[0], :, :, view[1]]


def by_blocks(array):
    return array.reshape(4, 4, 2, array.shape[0] // 32, -1)


def unit_rms(u):
    scale = lax.rsqrt(jnp.mean(u * u, axis=1, keepdims=True) + EPS)
    return u * scale, scale


def norm_back(u, gain, dy):
    n, scale = unit_rms(u)
    sd = dy * gain
    return scale * (sd - n * jnp.mean(sd * n, axis=1, keepdims=True)), jnp.sum(dy * n, axis=0, keepdims=True)


def turned(u, cos, sin):
    return u * cos + pltpu.roll(u, 64, 1) * sin


def turned_back(w, cos, sin):
    return w * cos - pltpu.roll(w, 64, 1) * sin


def twice(table):
    return jnp.concatenate([table, table], axis=0)


def key_places(micro_rows):
    j = lax.broadcasted_iota(jnp.int32, (micro_rows, 2048), 1)
    core = j // 1024
    chip = (j % 1024) // TOK
    return chip * (2 * TOK) + core * TOK + j % TOK


def masked(raw, ctx):
    rows = raw.shape[0]
    query = ctx * TOK + lax.broadcasted_iota(jnp.int32, (rows, 2048), 0) % TOK
    return jnp.where(key_places(rows) <= query, raw * (HD**-0.5), -1e30)


def attn_forward_kernel(views, x_ref, gain_ref, w_ref, bias_ref, cos_ref, sin_ref, rows_ref, *refs):
    mid_ref, hid_ref, q_ref, kv_ref, att_ref, wf_ref = refs[:6]
    bufs = refs[6 : 6 + len(views)]
    part_ref, got_ref, wsem, lsem, send, recv = refs[6 + len(views) :]
    me = Place()
    greet([me.yp(1), me.yp(2), me.yp(3), me.cp()] + xz(me))
    net = Links(send, recv)
    beside = gather_jobs(net, me, [view_of(rows_ref, view) for view in views], bufs, lsem)
    weights_over = net.go(w_ref, wf_ref.at[me.c], me.cp())
    weights_here = pltpu.make_async_copy(w_ref, wf_ref.at[me.c], wsem)
    weights_here.start()
    x = x_ref[...]
    normed, _ = unit_rms(x)
    hid_ref[me.y] = (normed * gain_ref[...]).astype(BF)
    hid_copies = [net.go(hid_ref.at[me.y], hid_ref.at[me.y], me.yp(k)) for k in ORDER]
    beside.step()
    cos, sin = twice(cos_ref[...]), twice(sin_ref[...])
    weights_here.wait()
    weights_over.wait()
    landed(hid_copies)
    hidden = hid_ref[...].reshape(2 * TOK, D)
    keyval = []
    proj = dot(hidden, wf_ref[0]) + bias_ref[:, :QKW]
    key = turned(proj[:, 384:], cos, sin).astype(BF)
    value = (dot(hidden, wf_ref[1, :, 384:]) + bias_ref[:, QKW:]).astype(BF)
    keyval = jnp.concatenate([key, value], axis=1)
    for m in range(2):
        kv_ref[me.c, m, me.z, me.x] = keyval[m * TOK : (m + 1) * TOK]
    first0 = [net.go(kv_ref.at[me.c, 0, me.z, me.x], kv_ref.at[me.c, 0, me.z, me.x], me.xp(k)) for k in ORDER]
    first1 = [net.go(kv_ref.at[me.c, 1, me.z, me.x], kv_ref.at[me.c, 1, me.z, me.x], me.zp(k)) for k in ORDER]
    for head in range(HEADS):
        query = turned(proj[:, head * HD : (head + 1) * HD], cos, sin).astype(BF)
        for m in range(2):
            q_ref[m, head] = query[m * TOK : (m + 1) * TOK]
    beside.step()
    landed(first0)
    second0 = [net.go(kv_ref.at[me.c, 0, me.z], kv_ref.at[me.c, 0, me.z], me.zp(k)) for k in ORDER]
    landed(first1)
    second1 = [net.go(kv_ref.at[me.c, 1, :, me.x], kv_ref.at[me.c, 1, :, me.x], me.xp(k)) for k in ORDER]
    landed(second0)
    third0 = net.go(kv_ref.at[me.c, 0], kv_ref.at[me.c, 0], me.cp())
    landed(second1)
    third1 = net.go(kv_ref.at[me.c, 1], kv_ref.at[me.c, 1], me.cp())
    beside.step()
    for m, third in ((0, third0), (1, third1)):
        third.wait_recv()
        queries = q_ref[m].reshape(HEADS * TOK, HD)
        keys = kv_ref[:, m, :, :, :, :HD].reshape(2048, HD)
        values = kv_ref[:, m, :, :, :, HD:].reshape(2048, HD)
        scores = masked(dot(queries, keys, 1, 1), me.ctx)
        weight = jnp.exp(scores - jnp.max(scores, axis=1, keepdims=True))
        total = jnp.sum(weight, axis=1, keepdims=True)
        out = (dot(weight.astype(BF), values) / total).astype(BF)
        for head in range(HEADS):
            att_ref[m * TOK : (m + 1) * TOK, head * HD : (head + 1) * HD] = out[head * TOK : (head + 1) * TOK]
    part_ref[...] = dot(att_ref[...], wf_ref[1, :, :384], 1, 1).astype(BF).reshape(4, OWN, D)
    back = [net.go(part_ref.at[(me.y + k) % 4], got_ref.at[k - 1], me.yp(k)) for k in ORDER]
    beside.step()
    total = x + part_ref[me.y].astype(F32)
    landed(back)
    for k in range(3):
        total = total + got_ref[k].astype(F32)
    mid_ref[...] = total
    beside.rest()
    left(hid_copies + first0 + first1 + second0 + second1 + [third0, third1] + back)


def attn_forward(x, gain, w_half, bias, cos, sin, rows, views, collective_id):
    views = [view + (rows.shape[2],) for view in views]
    return pl.pallas_call(
        functools.partial(attn_forward_kernel, views),
        out_shape=(
            jax.ShapeDtypeStruct((OWN, D), F32),
            jax.ShapeDtypeStruct((4, OWN, D), BF),
            jax.ShapeDtypeStruct((2, HEADS, TOK, HD), BF),
            jax.ShapeDtypeStruct((2, 2, 4, 4, TOK, 2 * HD), BF),
            jax.ShapeDtypeStruct((2 * TOK, HEADS * HD), BF),
            jax.ShapeDtypeStruct((2, D, QKW), BF),
        )
        + gathered(views),
        in_specs=[VM, VM, ANY, VM, VM, VM, ANY],
        out_specs=(VM,) * 6 + (ANY,) * len(views),
        scratch_shapes=[
            pltpu.VMEM((4, OWN, D), BF),
            pltpu.VMEM((3, OWN, D), BF),
            pltpu.SemaphoreType.DMA,
        ]
        + sems(21, len(views), Gather),
        compiler_params=params(collective_id),
        name="attn_forward",
    )(x, gain, w_half, bias, cos, sin, rows)


def fetch_mlp(w_refs, w_vmem, sems):
    copies = []
    part = 0
    for ref in w_refs:
        for i in range(ref.shape[1] // UNITS):
            copies.append(pltpu.make_async_copy(ref.at[:, i * UNITS : (i + 1) * UNITS], w_vmem.at[part], sems.at[part]))
            copies[-1].start()
            part += 1
    return copies


def gather_yc(net, me, buf):
    sent = [net.go(buf.at[me.c, me.y], buf.at[me.c, me.y], me.yp(k)) for k in ORDER]
    crossed = [net.go(buf.at[me.c, me.y], buf.at[me.c, me.y], me.cp())]
    for k, copy in zip(ORDER, sent):
        copy.wait_recv()
        slot = (me.y + 4 - k) % 4
        crossed.append(net.go(buf.at[me.c, slot], buf.at[me.c, slot], me.cp()))
    landed(crossed)
    return sent + crossed


def scatter_yc_start(net, me, part, mate):
    return net.go(part.at[1 - me.c], mate, me.cp())


def scatter_yc_middle(net, me, part, mate, got, swap):
    swap.wait_recv()
    mate[...] = (part[me.c].astype(F32) + mate[...].astype(F32)).astype(BF)
    return [net.go(mate.at[(me.y + k) % 4], got.at[k - 1], me.yp(k)) for k in ORDER]


def scatter_yc_end(me, mate, got, back):
    total = mate[me.y].astype(F32)
    landed(back)
    for k in range(3):
        total = total + got[k].astype(F32)
    return total


def mlp_forward_kernel(weight_count, views, mid_ref, gain_ref, *refs):
    w_refs = refs[:weight_count]
    row_refs = refs[weight_count : weight_count + len(views)]
    refs = refs[weight_count + len(views) :]
    out_ref, hid_ref, gate_ref, up_ref, prod_ref = refs[:5]
    bufs = refs[5 : 5 + len(views)]
    w_vmem, acc, part, mate, got, wsem, lsem, send, recv = refs[5 + len(views) :]
    me = Place()
    weights = fetch_mlp(w_refs, w_vmem, wsem)
    greet([me.yp(1), me.yp(2), me.yp(3), me.cp()] + (xz(me) if views else []))
    net = Links(send, recv)
    beside = gather_jobs(net, me, [view_of(ref, view) for ref, view in zip(row_refs, views)], bufs, lsem)
    normed, _ = unit_rms(mid_ref[...])
    hid_ref[me.c, me.y] = (normed * gain_ref[...]).astype(BF)
    beside.step()
    spread_out = gather_yc(net, me, hid_ref)
    for copy in weights:
        copy.wait()
    beside.step()
    acc[...] = jnp.zeros_like(acc)

    def step(i, _):
        cols = pl.ds(pl.multiple_of(i * CHUNK, CHUNK), CHUNK)
        gate = dot(hid_ref[...].reshape(256, D), w_vmem[0, :, cols])
        up = dot(hid_ref[...].reshape(256, D), w_vmem[1, :, cols])
        product = (gate * jax.nn.sigmoid(gate) * up).astype(BF)
        gate_ref[:, cols] = gate
        up_ref[:, cols] = up
        prod_ref[:, cols] = product
        acc[...] += dot(product, w_vmem[2, :, cols], 1, 1)
        return 0

    lax.fori_loop(0, UNITS // CHUNK, step, 0)
    part[...] = acc[...].astype(BF).reshape(2, 4, OWN, D)
    swap = scatter_yc_start(net, me, part, mate)
    beside.step()
    back = scatter_yc_middle(net, me, part, mate, got, swap)
    beside.step()
    out_ref[...] = mid_ref[...] + scatter_yc_end(me, mate, got, back)
    beside.rest()
    left(spread_out + [swap] + back)


def mlp_forward(mid, gain, weights, rows, views, collective_id):
    views = [view + (ref.shape[2],) for ref, view in zip(rows, views)]
    return pl.pallas_call(
        functools.partial(mlp_forward_kernel, len(weights), views),
        out_shape=(
            jax.ShapeDtypeStruct((OWN, D), F32),
            jax.ShapeDtypeStruct((2, 4, OWN, D), BF),
            jax.ShapeDtypeStruct((256, UNITS), F32),
            jax.ShapeDtypeStruct((256, UNITS), F32),
            jax.ShapeDtypeStruct((256, UNITS), BF),
        )
        + gathered(views),
        in_specs=[VM, VM] + [ANY] * (len(weights) + len(rows)),
        out_specs=(VM,) * 5 + (ANY,) * len(views),
        scratch_shapes=[
            pltpu.VMEM((3, D, UNITS), BF),
            pltpu.VMEM((256, D), F32),
            pltpu.VMEM((2, 4, OWN, D), BF),
            pltpu.VMEM((4, OWN, D), BF),
            pltpu.VMEM((3, OWN, D), BF),
            pltpu.SemaphoreType.DMA((3,)),
        ]
        + sems(11, len(views), Gather),
        compiler_params=params(collective_id),
        name="mlp_forward",
    )(mid, gain, *weights, *rows)


def mlp_backward_kernel(weight_count, jobs, g_ref, mid_ref, gain_ref, hid_ref, gate_ref, up_ref, prod_ref, *refs):
    w_refs = refs[:weight_count]
    srcs = refs[weight_count : weight_count + jobs]
    refs = refs[weight_count + jobs :]
    gmid_ref, ggain_ref, dgu_ref, dd_ref = refs[:4]
    outs = refs[4 : 4 + jobs]
    w_vmem, low, dgate, dup, acc, part, mate, got, wsem = refs[4 + jobs : 13 + jobs]
    job_scratch = refs[13 + jobs : 13 + 7 * jobs]
    lsem, send, recv = refs[13 + 7 * jobs :]
    me = Place()
    weights = fetch_mlp(w_refs, w_vmem, wsem)
    greet([me.yp(1), me.yp(2), me.yp(3), me.cp()] + (xz(me) if jobs else []))
    net = Links(send, recv)
    beside = scatter_jobs(net, me, srcs, outs, job_scratch, lsem)
    low[me.c, me.y] = g_ref[...].astype(BF)
    beside.step()
    spread_out = gather_yc(net, me, low)
    for copy in weights:
        copy.wait()
    acc[...] = jnp.zeros_like(acc)

    def step(i, _):
        cols = pl.ds(pl.multiple_of(i * CHUNK, CHUNK), CHUNK)
        dprod = dot(low[...].reshape(256, D), w_vmem[2, :, cols])
        gate, up = gate_ref[:, cols], up_ref[:, cols]
        sigma = jax.nn.sigmoid(gate)
        dg = (dprod * up * sigma * (1.0 + gate * (1.0 - sigma))).astype(BF)
        du = (dprod * gate * sigma).astype(BF)
        dgate[:, cols] = dg
        dup[:, cols] = du
        acc[...] += dot(dg, w_vmem[0, :, cols], 1, 1) + dot(du, w_vmem[1, :, cols], 1, 1)
        return 0

    lax.fori_loop(0, UNITS // CHUNK, step, 0)
    part[...] = acc[...].astype(BF).reshape(2, 4, OWN, D)
    swap = scatter_yc_start(net, me, part, mate)

    beside.step()

    def weight_grads(dw_ref, index, left_ref, right_ref):
        def step_w(i, _):
            cols = pl.ds(pl.multiple_of(i * CHUNK, CHUNK), CHUNK)
            where = pl.ds(pl.multiple_of(index * UNITS + i * CHUNK, CHUNK), CHUNK)
            dw_ref[:, where] = dot(left_ref[...].reshape(256, D), right_ref[:, cols], 0, 0).astype(BF)
            return 0

        lax.fori_loop(0, UNITS // CHUNK, step_w, 0)

    back = scatter_yc_middle(net, me, part, mate, got, swap)
    weight_grads(dgu_ref, 0, hid_ref, dgate)
    beside.step()
    weight_grads(dgu_ref, 1, hid_ref, dup)
    beside.step()
    weight_grads(dd_ref, 0, low, prod_ref)
    dy = scatter_yc_end(me, mate, got, back)
    du, ggain_ref[...] = norm_back(mid_ref[...], gain_ref[...], dy)
    gmid_ref[...] = g_ref[...] + du
    beside.rest()
    left(spread_out + [swap] + back)


def job_outs(jobs):
    return tuple(jax.ShapeDtypeStruct((2, job.shape[0] // 32, job.shape[1]), BF) for job in jobs)


def job_scratch(jobs):
    return [ref for job in jobs for ref in Scatter.scratch(job.shape[0] // 32, job.shape[1])]


def mlp_backward(g, mid, gain, weights, hid, gate, up, prod, jobs, collective_id):
    return pl.pallas_call(
        functools.partial(mlp_backward_kernel, len(weights), len(jobs)),
        out_shape=(
            jax.ShapeDtypeStruct((OWN, D), F32),
            jax.ShapeDtypeStruct((1, D), F32),
            jax.ShapeDtypeStruct((D, 2 * UNITS), BF),
            jax.ShapeDtypeStruct((D, UNITS), BF),
        )
        + job_outs(jobs),
        in_specs=[VM] * 7 + [ANY] * (len(weights) + len(jobs)),
        out_specs=(VM,) * (4 + len(jobs)),
        scratch_shapes=[
            pltpu.VMEM((3, D, UNITS), BF),
            pltpu.VMEM((2, 4, OWN, D), BF),
            pltpu.VMEM((256, UNITS), BF),
            pltpu.VMEM((256, UNITS), BF),
            pltpu.VMEM((256, D), F32),
            pltpu.VMEM((2, 4, OWN, D), BF),
            pltpu.VMEM((4, OWN, D), BF),
            pltpu.VMEM((3, OWN, D), BF),
            pltpu.SemaphoreType.DMA((3,)),
        ]
        + job_scratch(jobs)
        + sems(11, len(jobs), Scatter),
        compiler_params=params(collective_id),
        name="mlp_backward",
    )(g, mid, gain, hid, gate, up, prod, *weights, *[by_blocks(job) for job in jobs])


def attn_backward_kernel(
    jobs, gm_ref, x_ref, gain_ref, w_ref, hid_ref, q_ref, kv_ref, att_ref, cos_ref, sin_ref, *refs
):
    srcs = refs[:jobs]
    gin_ref, ggain_ref, gbias_ref, dw_ref = refs[jobs : jobs + 4]
    outs = refs[jobs + 4 : 2 * jobs + 4]
    refs = refs[2 * jobs + 4 :]
    low, dkv, kmate, kz, kx, k2, k3, kpair, kpair_got, dqs, dws, dw_got, part, got = refs[:14]
    job_refs = refs[14 : 14 + 6 * jobs]
    lsem, send, recv = refs[14 + 6 * jobs :]
    me = Place()
    greet([me.yp(1), me.yp(2), me.yp(3), me.cp()] + xz(me))
    net = Links(send, recv)
    beside = scatter_jobs(net, me, srcs, outs, job_refs, lsem)
    low[me.y] = gm_ref[...].astype(BF)
    spread_out = [net.go(low.at[me.y], low.at[me.y], me.yp(k)) for k in ORDER]
    beside.step()
    cos, sin = twice(cos_ref[...]), twice(sin_ref[...])
    landed(spread_out)
    grad_mid = low[...].reshape(2 * TOK, D)
    grad_att = dot(grad_mid, w_ref[1, :, :384]).astype(BF)
    for m in range(2):
        rows = slice(m * TOK, (m + 1) * TOK)
        queries = q_ref[m].reshape(HEADS * TOK, HD)
        keys = kv_ref[:, m, :, :, :, :HD].reshape(2048, HD)
        values = kv_ref[:, m, :, :, :, HD:].reshape(2048, HD)
        grad_out = jnp.concatenate([grad_att[rows, h * HD : (h + 1) * HD] for h in range(HEADS)], axis=0)
        scores = masked(dot(queries, keys, 1, 1), me.ctx)
        weight = jnp.exp(scores - jnp.max(scores, axis=1, keepdims=True))
        soft = weight / jnp.sum(weight, axis=1, keepdims=True)
        grad_soft = dot(grad_out, values, 1, 1)
        delta = jnp.sum(soft * grad_soft, axis=1, keepdims=True)
        grad_scores = (soft * (grad_soft - delta)).astype(BF)
        grad_values = dot(soft.astype(BF), grad_out, 0, 0)
        grad_keys = dot(grad_scores, queries, 0, 0) * (HD**-0.5)
        dkv[:, m] = jnp.concatenate([grad_keys, grad_values], axis=1).astype(BF).reshape(2, 4, 4, TOK, 2 * HD)
        dq = dot(grad_scores, keys) * (HD**-0.5)
        for h in range(HEADS):
            dqs[rows, h * HD : (h + 1) * HD] = dq[h * TOK : (h + 1) * TOK]
    swap = net.go(dkv.at[1 - me.c], kmate, me.cp())
    beside.step()
    dq_low = jnp.concatenate(
        [turned_back(dqs[:, h * HD : (h + 1) * HD], cos, sin).astype(BF) for h in range(HEADS)], axis=1
    )
    hidden = hid_ref[...].reshape(2 * TOK, D)
    swap.wait_recv()
    kmate[...] = (kmate[...].astype(F32) + dkv[me.c].astype(F32)).astype(BF)
    first0 = [net.go(kmate.at[0, (me.z + k) % 4], kz.at[k - 1], me.zp(k)) for k in ORDER]
    first1 = [net.go(kmate.at[1, :, (me.x + k) % 4], kx.at[k - 1], me.xp(k)) for k in ORDER]
    dws[0, :, :384] = dot(hidden, dq_low, 0, 0).astype(BF)
    dws[1, :, :384] = dot(grad_mid, att_ref[...], 0, 0).astype(BF)
    dws[1, :, 384:] = jnp.zeros((D, HD), BF)
    beside.step()
    landed(first0)
    total0 = kmate[0, me.z].astype(F32)
    for k in range(3):
        total0 = total0 + kz[k].astype(F32)
    k2[0] = total0.astype(BF)
    second0 = [net.go(k2.at[0, (me.x + k) % 4], k3.at[0, k - 1], me.xp(k)) for k in ORDER]
    landed(first1)
    total1 = kmate[1, :, me.x].astype(F32)
    for k in range(3):
        total1 = total1 + kx[k].astype(F32)
    k2[1] = total1.astype(BF)
    second1 = [net.go(k2.at[1, (me.z + k) % 4], k3.at[1, k - 1], me.zp(k)) for k in ORDER]
    landed(second0 + second1)
    for m, place in ((0, me.x), (1, me.z)):
        total = k2[m, place].astype(F32)
        for k in range(3):
            total = total + k3[m, k].astype(F32)
        kpair[0, m * TOK : (m + 1) * TOK] = total[:, :HD].astype(BF)
        kpair[1, m * TOK : (m + 1) * TOK] = total[:, HD:].astype(BF)
    pair = net.go(kpair.at[1 - me.s], kpair_got, {"section": 1 - me.s})
    pair.wait_recv()
    total = kpair[me.s].astype(F32) + kpair_got[...].astype(F32)
    dk_low = jnp.where(me.s == 0, turned_back(total, cos, sin), total).astype(BF)
    part[...] = (
        (dot(dq_low, w_ref[0, :, :384], 1, 1) + dot(dk_low, w_ref[me.s, :, 384:], 1, 1)).astype(BF).reshape(4, OWN, D)
    )
    back = [net.go(part.at[(me.y + k) % 4], got.at[k - 1], me.yp(k)) for k in ORDER]
    beside.step()
    dws[0, :, 384:] = dot(hidden, dk_low, 0, 0).astype(BF)
    dw_swap = net.go(dws.at[1 - me.c], dw_got, me.cp())
    gbias_ref[:, :384] = jnp.sum(dq_low.astype(F32), axis=0, keepdims=True)
    gbias_ref[:, 384:] = jnp.sum(dk_low.astype(F32), axis=0, keepdims=True)
    dy = part[me.y].astype(F32)
    landed(back)
    for k in range(3):
        dy = dy + got[k].astype(F32)
    dx, ggain_ref[...] = norm_back(x_ref[...], gain_ref[...], dy)
    gin_ref[...] = gm_ref[...] + dx
    dw_swap.wait_recv()
    dw_ref[...] = (dws[me.c].astype(F32) + dw_got[...].astype(F32)).astype(BF)
    beside.rest()
    left(spread_out + [swap] + first0 + first1 + second0 + second1 + [pair] + back + [dw_swap])


def attn_backward(gm, x, gain, w, hid, q, kv, att, cos, sin, jobs, collective_id):
    return pl.pallas_call(
        functools.partial(attn_backward_kernel, len(jobs)),
        out_shape=(
            jax.ShapeDtypeStruct((OWN, D), F32),
            jax.ShapeDtypeStruct((1, D), F32),
            jax.ShapeDtypeStruct((1, QKW), F32),
            jax.ShapeDtypeStruct((D, QKW), BF),
        )
        + job_outs(jobs),
        in_specs=[VM] * 10 + [ANY] * len(jobs),
        out_specs=(VM,) * (4 + len(jobs)),
        scratch_shapes=[
            pltpu.VMEM((4, OWN, D), BF),
            pltpu.VMEM((2, 2, 4, 4, TOK, 2 * HD), BF),
            pltpu.VMEM((2, 4, 4, TOK, 2 * HD), BF),
            pltpu.VMEM((3, 4, TOK, 2 * HD), BF),
            pltpu.VMEM((3, 4, TOK, 2 * HD), BF),
            pltpu.VMEM((2, 4, TOK, 2 * HD), BF),
            pltpu.VMEM((2, 3, TOK, 2 * HD), BF),
            pltpu.VMEM((2, 2 * TOK, HD), BF),
            pltpu.VMEM((2 * TOK, HD), BF),
            pltpu.VMEM((2 * TOK, HEADS * HD), F32),
            pltpu.VMEM((2, D, QKW), BF),
            pltpu.VMEM((D, QKW), BF),
            pltpu.VMEM((4, OWN, D), BF),
            pltpu.VMEM((3, OWN, D), BF),
        ]
        + job_scratch(jobs)
        + sems(21, len(jobs), Scatter),
        compiler_params=params(collective_id),
        name="attn_backward",
    )(gm, x, gain, w, hid, q, kv, att, cos, sin, *[by_blocks(job) for job in jobs])


def quad(me):
    return (
        (me.c, 1 - me.s, {"section": 1 - me.s}),
        (1 - me.c, me.s, me.cp()),
        (1 - me.c, 1 - me.s, {"section": 1 - me.s, "ctx": me.ctx + 1 - 2 * me.c}),
    )


def open_kernel(
    attn_ref, mlp_ref, tiny_ref, ends_ref,
    attn_out, mlp_out, tiny_out, ends_out, tiny_all, attn_buf,
    hsem, lsem, send, recv,
):
    me = Place()
    peers = quad(me)
    greet([peer for _, _, peer in peers] + xz(me))
    net = Links(send, recv)
    away = pl.ds(pl.multiple_of((1 - me.s) * OWN, OWN), OWN)
    home = pl.ds(pl.multiple_of(me.s * OWN, OWN), OWN)
    early, late = [], []
    for core, section, peer in peers:
        early.append(net.go(attn_ref.at[section, core], attn_out.at[me.s, me.c], peer))
        early.append(net.go(tiny_ref, tiny_out.at[me.s, me.c], peer))
    late.append(net.go(ends_ref.at[me.h, away], ends_out.at[me.s], {"section": 1 - me.s}))
    for core, section, peer in peers:
        late.append(net.go(mlp_ref.at[section, core], mlp_out.at[me.s, me.c], peer))
    pairs = (
        (attn_ref.at[me.s, me.c], attn_out.at[me.s, me.c]),
        (tiny_ref, tiny_out.at[me.s, me.c]),
        (ends_ref.at[me.h, home], ends_out.at[me.s]),
        (mlp_ref.at[me.s, me.c], mlp_out.at[me.s, me.c]),
    )
    here = []
    for i, (src, dst) in enumerate(pairs):
        here.append(pltpu.make_async_copy(src, dst, hsem.at[i]))
        here[-1].start()
    here[0].wait()
    here[1].wait()
    landed(early)
    here.append(pltpu.make_async_copy(tiny_out, tiny_all.at[me.z, me.x], hsem.at[4]))
    here[4].start()
    one = [net.go(tiny_out, tiny_all.at[me.z, me.x], me.xp(k)) for k in ORDER]
    attn = Gather(net, me, attn_out.at[0], attn_buf, lsem.at[0])
    attn.start()
    here[4].wait()
    landed(one)
    two = [net.go(tiny_all.at[me.z], tiny_all.at[me.z], me.zp(k)) for k in ORDER]
    attn.second()
    attn.third()
    attn.fourth()
    attn.finish()
    landed(two)
    here[2].wait()
    here[3].wait()
    landed(late)
    left(early + late + one + two)


def open_up(attn, mlp, tiny, ends):
    return pl.pallas_call(
        open_kernel,
        out_shape=(
            jax.ShapeDtypeStruct(attn.shape, BF),
            jax.ShapeDtypeStruct(mlp.shape, BF),
            jax.ShapeDtypeStruct((2, 2) + tiny.shape, BF),
            jax.ShapeDtypeStruct((2, OWN, D), F32),
            jax.ShapeDtypeStruct((4, 4, 2, 2) + tiny.shape, BF),
            jax.ShapeDtypeStruct((4, 4) + attn.shape[1:], BF),
        ),
        in_specs=[ANY] * 4,
        out_specs=(ANY,) * 6,
        scratch_shapes=[pltpu.SemaphoreType.DMA((5,))] + sems(16, 1, Gather),
        compiler_params=params(8),
        name="open_up",
    )(attn, mlp, tiny, ends)


def deposit_kernel(
    a0, a1, d0, d1, gu0, gu1, small, ends,
    attn_out, gu_out, d_out, small_out, ends_out,
    *scratch,
):
    me = Place()
    peers = quad(me)
    greet([me.yp(1), me.yp(2), me.yp(3), me.cp(), peers[2][2]] + xz(me))
    res_a, res_gu, res_d, sum_c, sum_got, hsem, lsem, send, recv = scratch[12:]
    net = Links(send, recv)
    beside = scatter_jobs(net, me, (d0, a0), (res_d.at[0], res_a.at[0]), scratch[:12], lsem)
    beside.step()
    here = []
    for i, (src, dst) in enumerate(
        ((gu0, res_gu.at[0]), (gu1, res_gu.at[1]), (d1, res_d.at[1]), (a1, res_a.at[1]), (ends.at[me.s], ends_out.at[me.y]))
    ):
        here.append(pltpu.make_async_copy(src, dst, hsem.at[i]))
        here[-1].start()
    copies = []
    sum_c[0] = small[...]
    rounds = ((me.yp, ORDER), (lambda k: me.cp(), (1,)), (me.xp, ORDER), (me.zp, ORDER))

    def small_round(turn, slot):
        peer, ks = rounds[turn]
        sent = [net.go(sum_c.at[turn], sum_got.at[slot + k - 1], peer(k)) for k in ks]
        copies.extend(sent)
        landed(sent)
        total = sum_c[turn]
        for k in ks:
            total = total + sum_got[slot + k - 1]
        sum_c[turn + 1] = total

    small_round(0, 0)
    small_round(1, 3)
    last = [net.go(ends.at[((me.y + k) % 4) % 2], ends_out.at[me.y], me.yp(k)) for k in ORDER]

    def go_home(res, out, sem):
        for core, section, peer in peers:
            last.append(net.go(res.at[section, core], out.at[me.s, me.c], peer))
        here.append(pltpu.make_async_copy(res.at[me.s, me.c], out.at[me.s, me.c], hsem.at[sem]))
        here[-1].start()

    here[0].wait()
    here[1].wait()
    go_home(res_gu, gu_out, 5)
    beside.step()
    small_round(2, 4)
    small_round(3, 7)
    beside.step()
    beside.step()
    beside.step()
    here[2].wait()
    here[3].wait()
    go_home(res_d, d_out, 6)
    go_home(res_a, attn_out, 7)
    small_out[...] = sum_c[4]
    for copy in here[4:]:
        copy.wait()
    landed(last)
    left(copies + last)
    beside.rest()


def deposit(a0, a1, d0, d1, gu0, gu1, small, ends):
    rows = a1.shape[1]
    return pl.pallas_call(
        deposit_kernel,
        out_shape=(
            jax.ShapeDtypeStruct((2,) + a1.shape, BF),
            jax.ShapeDtypeStruct((2,) + gu1.shape, BF),
            jax.ShapeDtypeStruct((2,) + d1.shape, BF),
            jax.ShapeDtypeStruct(small.shape, F32),
            jax.ShapeDtypeStruct((4, OWN, D), F32),
        ),
        in_specs=[ANY] * 6 + [VM, ANY],
        out_specs=(ANY, ANY, ANY, VM, ANY),
        scratch_shapes=job_scratch((d0, a0))
        + [
            pltpu.VMEM((2,) + a1.shape, BF),
            pltpu.VMEM((2,) + gu1.shape, BF),
            pltpu.VMEM((2,) + d1.shape, BF),
            pltpu.VMEM((5,) + small.shape, F32),
            pltpu.VMEM((10,) + small.shape, F32),
            pltpu.SemaphoreType.DMA((8,)),
        ]
        + sems(22, 2, Scatter),
        compiler_params=params(9),
        name="deposit",
    )(by_blocks(a0), a1, by_blocks(d0), d1, gu0, gu1, small, ends)


def unit_slices(w):
    padded = jnp.pad(w, ((0, 0), (0, 4 * UNITS - w.shape[1])))
    return padded.reshape(w.shape[0], 2, 2, UNITS).transpose(1, 2, 0, 3)


def body(ends, w_query, w_kv, w_out, w_gate_up, w_down, gains, bias_query, bias_kv):
    me = Place()
    rows = w_query.shape[1]
    wq = w_query[0].reshape(rows, 2, 384)
    wo = w_out[0].reshape(rows, 2, 384)
    attn_pieces = jnp.stack(
        [
            jnp.stack(
                [
                    jnp.concatenate([wq[:, s], w_kv[0, :, 0]], axis=1),
                    jnp.concatenate([wo[:, s], w_kv[0, :, 1]], axis=1),
                ]
            )
            for s in range(2)
        ]
    )
    mlp_pieces = jnp.concatenate(
        [unit_slices(w_gate_up[0, :, 0]), unit_slices(w_gate_up[0, :, 1]), unit_slices(w_down[0])], axis=3
    )
    packed = jnp.concatenate([gains[0].reshape(-1), bias_query[0].reshape(-1), bias_kv[0].reshape(-1)])[None]
    attn_rows, mlp_rows, _, tokens, tiny_all, attn_w0 = open_up(
        attn_pieces, mlp_pieces, jnp.pad(packed, ((0, 15), (0, 0))), ends[0]
    )

    everything = tiny_all[:, :, :, :, 0].reshape(16, 2, 2, 128).astype(F32)
    gain_all = everything[..., :96].reshape(16, 2, 2, 2, 48).transpose(1, 3, 0, 2, 4).reshape(2, 2, 1, D)
    bias_here = everything[..., 96:].reshape(16, 2, 2, 8, 4).transpose(1, 3, 0, 2, 4).reshape(2, 8, 128)
    bias_q = lax.dynamic_slice(bias_here, (0, me.s * HEADS, 0), (2, HEADS, 128)).reshape(2, 1, 384)
    bias = jnp.concatenate([bias_q, bias_here[:, 6:8].reshape(2, 1, 256)], axis=2)

    positions = (me.ctx * TOK + jnp.arange(TOK, dtype=jnp.int32)).astype(F32)
    inverse = 1.0 / THETA ** (jnp.arange(0, HD, 2, dtype=F32) / HD)
    angles = positions[:, None] * inverse[None, :]
    cos = jnp.concatenate([jnp.cos(angles), jnp.cos(angles)], axis=1)
    sin = jnp.concatenate([-jnp.sin(angles), jnp.sin(angles)], axis=1)

    def whole(blocks):
        return blocks.reshape(D, -1)

    gate, up_down, every = slice(0, UNITS), slice(UNITS, 3 * UNITS), slice(0, 3 * UNITS)
    x0 = tokens[0]
    mid0, hid, q, kv, att, wf, mlp_w0 = attn_forward(
        x0, gain_all[0, 0], whole(attn_w0), bias[0], cos, sin, mlp_rows, [(0, every)], 0
    )
    kept0 = (hid, q, kv, att)
    wf0 = wf
    mlp_w0 = [whole(mlp_w0)]
    out, *mlp0, attn_w1, gate_w1 = mlp_forward(
        mid0, gain_all[0, 1], mlp_w0, [attn_rows, mlp_rows], [(1, slice(0, QKW)), (1, gate)], 1
    )
    x1 = out.astype(BF).astype(F32)
    mid1, hid, q, kv, att, wf, up_down_w1 = attn_forward(
        x1, gain_all[1, 0], whole(attn_w1), bias[1], cos, sin, mlp_rows, [(1, up_down)], 2
    )
    kept1 = (hid, q, kv, att)
    mlp_w1 = [whole(gate_w1), whole(up_down_w1)]
    out, *mlp1 = mlp_forward(mid1, gain_all[1, 1], mlp_w1, [], [], 3)

    gmid, ggain11, dgu1, dd1 = mlp_backward(tokens[1], mid1, gain_all[1, 1], mlp_w1, *mlp1, [], 4)
    gin, ggain10, gbias1, da1, dgu1 = attn_backward(
        gmid, x1, gain_all[1, 0], wf, *kept1, cos, sin, [dgu1], 5
    )
    g = gin.astype(BF).astype(F32)
    gmid, ggain01, dgu0, dd0, dd1, da1 = mlp_backward(g, mid0, gain_all[0, 1], mlp_w0, *mlp0, [dd1, da1], 6)
    gin, ggain00, gbias0, da0, dgu0 = attn_backward(
        gmid, x0, gain_all[0, 0], wf0, *kept0, cos, sin, [dgu0], 7
    )
    bias_g = [gbias0, gbias1]
    gain_g = [ggain00, ggain01, ggain10, ggain11]

    small = jnp.stack(bias_g)
    small = jnp.where(jnp.arange(4)[None, :, None] == me.y, small, 0.0)
    small = jnp.concatenate([jnp.stack(gain_g).reshape(-1), small.reshape(-1)]).reshape(-1, 128)
    attn_home, gu_home, d_home, small, boundary = deposit(
        da0, da1, dd0, dd1, dgu0, dgu1, small, jnp.stack([gin, out])
    )
    small = small.reshape(-1)
    gain_sum = small[: 4 * D].reshape(2, 2, 32, 48)
    bias_sum = small[4 * D :].reshape(2, 2, 2, 4, 32, 4)
    gain_sum = lax.dynamic_index_in_dim(gain_sum, me.s, 0, keepdims=False)
    gain_sum = lax.dynamic_index_in_dim(gain_sum, me.ctx, 1, keepdims=False)
    bias_sum = lax.dynamic_index_in_dim(bias_sum, me.s, 0, keepdims=False)
    bias_sum = lax.dynamic_index_in_dim(bias_sum, me.h, 0, keepdims=False)
    bias_sum = lax.dynamic_index_in_dim(bias_sum, me.ctx, 2, keepdims=False)

    attn_home = attn_home.astype(F32)
    gu_home = gu_home.astype(F32).reshape(2, 2, rows, 2, UNITS).transpose(2, 3, 0, 1, 4).reshape(rows, 2, 4 * UNITS)
    d_home = d_home.astype(F32).transpose(2, 0, 1, 3).reshape(rows, 4 * UNITS)
    return (
        boundary.reshape(1, 2, TOK, D),
        attn_home[:, 0, :, :384].transpose(1, 0, 2).reshape(1, rows, 768),
        attn_home[:, 0, :, 384:].transpose(1, 0, 2)[None],
        attn_home[:, 1, :, :384].transpose(1, 0, 2).reshape(1, rows, 768),
        gu_home[:, :, : w_down.shape[2]][None],
        d_home[:, : w_down.shape[2]][None],
        gain_sum[None],
        bias_sum[:, :HEADS].reshape(1, 6, 4),
        bias_sum[:, HEADS].reshape(1, 2, 1, 4),
    )


def solution(mesh):
    placed = (
        P("section", None, "ctx", None),
        P("section", "ctx", "shard"),
        P("section", "ctx", None, "shard"),
        P("section", "ctx", "shard"),
        P("section", "ctx", None, "shard"),
        P("section", "ctx", "shard"),
        P("section", None, "ctx"),
        P("section", "shard", "ctx"),
        P("section", None, "shard", "ctx"),
    )
    return jax.shard_map(
        body,
        mesh=mesh,
        in_specs=placed,
        out_specs=(
            P("section", None, "ctx", None),
            P("section", "ctx", "shard"),
            P("section", "ctx", None, "shard"),
            P("section", "ctx", "shard"),
            P("section", "ctx", None, "shard"),
            P("section", "ctx", "shard"),
            P("section", None, "ctx"),
            P("section", "shard", "ctx"),
            P("section", None, "shard", "ctx"),
        ),
        check_vma=False,
    )
```

```python
import functools
import types

import jax
import jax.numpy as jnp
from jax import lax
from jax.experimental import pallas as pl
from jax.experimental.pallas import tpu as pltpu
from jax.sharding import PartitionSpec as P

MESH = pl.DeviceIdType.MESH
BF = jnp.bfloat16
F32 = jnp.float32
EPS = 1e-06
THETA = 1000000.0
D = 1536
HD = 128
HEADS = 3
UNITS = 1152
CHUNK = 384
TOK = 64
OWN = 32
ROWS = 48
QKW = 512
ORDER = (1, 3, 2)
SIDES = (1, 3)


class Place:
    def __init__(self):
        self.ctx = lax.axis_index("ctx")
        self.s = lax.axis_index("section")
        self.h = lax.axis_index("shard")
        self.z = self.ctx // 8
        self.x = (self.ctx // 2) % 4
        self.c = self.ctx % 2
        self.y = self.h * 2 + self.s

    def yp(self, k):
        other = (self.y + k) % 4
        return {"section": other % 2, "shard": other // 2}

    def xp(self, k):
        return {"ctx": self.z * 8 + ((self.x + k) % 4) * 2 + self.c}

    def zp(self, k):
        return {"ctx": (self.ctx + 8 * k) % 32}

    def cp(self):
        return {"ctx": self.ctx + 1 - 2 * self.c}

    def quad(self):
        return (
            (self.c, 1 - self.s, {"section": 1 - self.s}),
            (1 - self.c, self.s, self.cp()),
            (1 - self.c, 1 - self.s, {"section": 1 - self.s, "ctx": self.ctx + 1 - 2 * self.c}),
        )

    def greet(self):
        peers = [self.yp(k) for k in ORDER] + [self.cp(), self.quad()[2][2]]
        peers += [self.xp(k) for k in ORDER] + [self.zp(k) for k in ORDER]
        barrier = pltpu.get_barrier_semaphore()
        for peer in peers:
            pl.semaphore_signal(barrier, 1, device_id=peer, device_id_type=MESH)
        pl.semaphore_wait(barrier, len(peers))


class Links:
    def __init__(self, send, recv):
        self.send, self.recv, self.count = send, recv, 0
        self.free = list(range(send.shape[0]))

    def go(self, src, dst, peer):
        index = self.count
        self.count += 1
        slot = self.free.pop(0)
        copy = pltpu.make_async_remote_copy(
            src, dst, self.send.at[slot], self.recv.at[index], device_id=peer, device_id_type=MESH
        )
        copy.start()
        return copy, slot

    def left(self, copies):
        for copy, slot in copies:
            copy.wait_send()
            self.free.append(slot)


def landed(copies):
    for copy, _ in copies:
        copy.wait_recv()


class Local:
    def __init__(self, sems):
        self.sems, self.count = sems, 0

    def go(self, src, dst):
        copy = pltpu.make_async_copy(src, dst, self.sems.at[self.count])
        self.count += 1
        copy.start()
        return copy


def cuts(columns):
    cut = (columns // 256) * 128
    return (slice(0, cut), slice(cut, columns))


class Gather:
    copies = 40

    def __init__(self, me, net, local, src, buf, ready=()):
        self.me, self.net, self.local, self.src, self.buf, self.ready = me, net, local, src, buf, ready
        self.cuts = cuts(src.shape[-1])
        self.sent = []

    def steps(self):
        return [self.start, self.second, self.third, self.fourth, self.finish]

    def at(self, half, p, q):
        return self.buf.at[q, p, 0] if half == 0 else self.buf.at[p, q, 1]

    def axes(self, half):
        me = self.me
        return (me.x, me.z, me.xp, me.zp) if half == 0 else (me.z, me.x, me.zp, me.xp)

    def go(self, src, dst, peer):
        copy = self.net.go(src, dst, peer)
        self.sent.append(copy)
        return copy

    def start(self):
        me = self.me
        for wait in self.ready:
            wait()
        self.own = self.local.go(self.src, self.buf.at[me.z, me.x])
        self.a, self.c = [None, None], [[None] * 4, [None] * 4]
        for half in range(2):
            p, q, pp, qp = self.axes(half)
            self.a[half] = [self.go(self.src.at[half], self.at(half, p, q), pp(k)) for k in SIDES]
        for half in range(2):
            p, q, pp, qp = self.axes(half)
            self.c[half][0] = [self.go(self.src.at[half], self.at(half, p, q), qp(k)) for k in SIDES]

    def second(self):
        self.f = [[], []]
        for half in range(2):
            p, q, pp, qp = self.axes(half)
            for i, k in enumerate(SIDES):
                landed([self.a[half][i]])
                piece = self.at(half, (p + 4 - k) % 4, q).at[:, self.cuts[i]]
                self.f[half].append(self.go(piece, piece, pp(k)))
        for half in range(2):
            p, q, pp, qp = self.axes(half)
            for i, k in enumerate(SIDES):
                block = self.at(half, (p + 4 - k) % 4, q)
                self.c[half][i + 1] = [self.go(block, block, qp(kk)) for kk in SIDES]

    def third(self):
        for half in range(2):
            p, q, pp, qp = self.axes(half)
            landed(self.f[half])
            block = self.at(half, (p + 2) % 4, q)
            self.c[half][3] = [self.go(block, block, qp(kk)) for kk in SIDES]
        self.last = []
        self.onward((0,))

    def fourth(self):
        self.onward((1, 2, 3))

    def onward(self, turns):
        for j in turns:
            shift = (0, 3, 1, 2)[j]
            for half in range(2):
                p, q, pp, qp = self.axes(half)
                for i, k in enumerate(SIDES):
                    landed([self.c[half][j][i]])
                    piece = self.at(half, (p + shift) % 4, (q + 4 - k) % 4).at[:, self.cuts[i]]
                    self.last.append(self.go(piece, piece, qp(k)))

    def finish(self):
        landed(self.last)
        self.own.wait()
        self.net.left(self.sent)


class Scatter:
    copies = 16

    def __init__(self, me, net, part, scratch, out, then=None):
        self.me, self.net, self.part, self.out, self.then = me, net, part, out, then
        self.r1, self.r2, self.u1, self.u2 = scratch
        self.cuts = cuts(part.shape[-1])
        self.sent = []

    def steps(self):
        return [self.start, self.second, self.third, self.fourth, self.finish]

    @staticmethod
    def scratch(columns):
        wide = columns - (columns // 256) * 128
        return [
            pltpu.VMEM((2, 2, 4, ROWS, wide), BF),
            pltpu.VMEM((2, 2, 4, ROWS, columns), BF),
            pltpu.VMEM((2, 2, ROWS, wide), BF),
            pltpu.VMEM((2, 2, ROWS, columns), BF),
        ]

    def group(self, half, q):
        return self.part.at[q, :, 0] if half == 0 else self.part.at[:, q, 1]

    def axes(self, half):
        me = self.me
        return (me.x, me.z, me.xp, me.zp) if half == 0 else (me.z, me.x, me.zp, me.xp)

    def go(self, src, dst, peer):
        copy = self.net.go(src, dst, peer)
        self.sent.append(copy)
        return copy

    def wide(self, i):
        return slice(0, self.cuts[i].stop - self.cuts[i].start)

    def start(self):
        self.one = [[], []]
        for half in range(2):
            p, q, pp, qp = self.axes(half)
            for i, k in enumerate(SIDES):
                piece = self.group(half, (q + 2) % 4).at[:, :, self.cuts[i]]
                self.one[half].append(self.go(piece, self.r1.at[half, i, :, :, self.wide(i)], qp(k)))

    def second(self):
        self.two = [[], []]
        for i, k in enumerate(SIDES):
            for half in range(2):
                p, q, pp, qp = self.axes(half)
                landed([self.one[half][i]])
                mine = self.group(half, (q + k) % 4)

                def add(j, _):
                    mine[j, :, self.cuts[i]] = (
                        mine[j, :, self.cuts[i]].astype(F32) + self.r1[half, i, j, :, self.wide(i)].astype(F32)
                    ).astype(BF)
                    return 0

                lax.fori_loop(0, 4, add, 0)
                self.two[half].append(self.go(mine, self.r2.at[half, i], qp(k)))

    def third(self):
        self.three = [[], []]
        for half in range(2):
            p, q, pp, qp = self.axes(half)
            landed(self.two[half])
            mine = self.group(half, q)

            def add(j, _):
                mine[j] = (
                    mine[j].astype(F32) + self.r2[half, 0, j].astype(F32) + self.r2[half, 1, j].astype(F32)
                ).astype(BF)
                return 0

            lax.fori_loop(0, 4, add, 0)
            for i, k in enumerate(SIDES):
                self.three[half].append(
                    self.go(mine.at[(p + 2) % 4, :, self.cuts[i]], self.u1.at[half, i, :, self.wide(i)], pp(k))
                )

    def fourth(self):
        self.four = [[], []]
        for half in range(2):
            p, q, pp, qp = self.axes(half)
            for i, k in enumerate(SIDES):
                landed([self.three[half][i]])
                block = self.group(half, q).at[(p + k) % 4]
                block[:, self.cuts[i]] = (
                    block[:, self.cuts[i]].astype(F32) + self.u1[half, i, :, self.wide(i)].astype(F32)
                ).astype(BF)
                self.four[half].append(self.go(block, self.u2.at[half, i], pp(k)))

    def finish(self):
        for half in range(2):
            p, q, pp, qp = self.axes(half)
            landed(self.four[half])
            self.out[half] = (
                self.group(half, q)[p].astype(F32) + self.u2[half, 0].astype(F32) + self.u2[half, 1].astype(F32)
            ).astype(BF)
        self.net.left(self.sent)
        if self.then is not None:
            self.then()


class Beside:
    def __init__(self, lag):
        self.lag, self.turn, self.jobs = lag, 0, []

    def add(self, job):
        first = self.turn
        if self.jobs:
            first = max(first, self.jobs[-1][0] + self.lag)
        self.jobs.append((first, list(job.steps()), job))
        return job

    def step(self, count=1):
        for _ in range(count):
            for first, steps, _ in reversed(self.jobs):
                if self.turn >= first and steps:
                    steps.pop(0)()
            self.turn += 1

    def until(self, *jobs):
        while any(steps for _, steps, job in self.jobs if job in jobs):
            self.step()

    def rest(self):
        while any(steps for _, steps, _ in self.jobs):
            self.step()


def dot(a, b, ca=1, cb=0):
    return lax.dot_general(a, b, (((ca,), (cb,)), ((), ())), preferred_element_type=F32)


def unit_rms(u):
    scale = lax.rsqrt(jnp.mean(u * u, axis=1, keepdims=True) + EPS)
    return u * scale, scale


def norm_back(u, gain, dy):
    n, scale = unit_rms(u)
    sd = dy * gain
    return scale * (sd - n * jnp.mean(sd * n, axis=1, keepdims=True)), jnp.sum(dy * n, axis=0, keepdims=True)


def turned(u, cos, sin):
    return u * cos + pltpu.roll(u, 64, 1) * sin


def turned_back(w, cos, sin):
    return w * cos - pltpu.roll(w, 64, 1) * sin


def twice(table):
    return jnp.concatenate([table, table], axis=0)


def key_places(rows):
    j = lax.broadcasted_iota(jnp.int32, (rows, 2048), 1)
    core = j // 1024
    chip = (j % 1024) // TOK
    return chip * (2 * TOK) + core * TOK + j % TOK


def masked(raw, ctx):
    rows = raw.shape[0]
    query = ctx * TOK + lax.broadcasted_iota(jnp.int32, (rows, 2048), 0) % TOK
    return jnp.where(key_places(rows) <= query, raw * (HD**-0.5), -1e30)


def columns_of(i, base=0):
    return pl.ds(pl.multiple_of(base + i * CHUNK, CHUNK), CHUNK)


def attn_forward(me, net, beside, x_ref, gain, bias, cos_ref, sin_ref, wf, weights, hid, q, kv, att, part, got, mid):
    x = x_ref[...]
    normed, _ = unit_rms(x)
    hid[me.y] = (normed * gain).astype(BF)
    hid_copies = [net.go(hid.at[me.y], hid.at[me.y], me.yp(k)) for k in ORDER]
    cos, sin = twice(cos_ref[...]), twice(sin_ref[...])
    weights()
    landed(hid_copies)
    hidden = hid[...].reshape(2 * TOK, D)
    proj = dot(hidden, whole(wf.at[0], slice(0, QKW))) + bias[:, :QKW]
    key = turned(proj[:, 384:], cos, sin).astype(BF)
    value = (dot(hidden, whole(wf.at[1], slice(384, QKW))) + bias[:, QKW:]).astype(BF)
    keyval = jnp.concatenate([key, value], axis=1)
    for m in range(2):
        kv[me.c, m, me.z, me.x] = keyval[m * TOK : (m + 1) * TOK]
    mine0, mine1 = kv.at[me.c, 0, me.z, me.x], kv.at[me.c, 1, me.z, me.x]
    first0 = [net.go(mine0, mine0, me.xp(k)) for k in ORDER]
    first1 = [net.go(mine1, mine1, me.zp(k)) for k in ORDER]
    for head in range(HEADS):
        query = turned(proj[:, head * HD : (head + 1) * HD], cos, sin).astype(BF)
        for m in range(2):
            q[m, head] = query[m * TOK : (m + 1) * TOK]
    beside.step()
    landed(first0)
    second0 = [net.go(kv.at[me.c, 0, me.z], kv.at[me.c, 0, me.z], me.zp(k)) for k in ORDER]
    landed(first1)
    second1 = [net.go(kv.at[me.c, 1, :, me.x], kv.at[me.c, 1, :, me.x], me.xp(k)) for k in ORDER]
    beside.step()
    landed(second0)
    third0 = net.go(kv.at[me.c, 0], kv.at[me.c, 0], me.cp())
    landed(second1)
    third1 = net.go(kv.at[me.c, 1], kv.at[me.c, 1], me.cp())
    for m, third in ((0, third0), (1, third1)):
        beside.step()
        landed([third])
        queries = q[m].reshape(HEADS * TOK, HD)
        keys = kv[:, m, :, :, :, :HD].reshape(2048, HD)
        values = kv[:, m, :, :, :, HD:].reshape(2048, HD)
        scores = masked(dot(queries, keys, 1, 1), me.ctx)
        weight = jnp.exp(scores - jnp.max(scores, axis=1, keepdims=True))
        total = jnp.sum(weight, axis=1, keepdims=True)
        out = (dot(weight.astype(BF), values) / total).astype(BF)
        for head in range(HEADS):
            att[m * TOK : (m + 1) * TOK, head * HD : (head + 1) * HD] = out[head * TOK : (head + 1) * TOK]
    beside.step()
    part[...] = dot(att[...], whole(wf.at[1], slice(0, 384)), 1, 1).astype(BF).reshape(4, OWN, D)
    back = [net.go(part.at[(me.y + k) % 4], got.at[k - 1], me.yp(k)) for k in ORDER]
    beside.step()
    total = x + part[me.y].astype(F32)
    landed(back)
    for k in range(3):
        total = total + got[k].astype(F32)
    mid[...] = total
    net.left(hid_copies + first0 + first1 + second0 + second1 + [third0, third1] + back)


def gather_yc(me, net, buf):
    own = buf.at[me.c, me.y]
    sent = [net.go(own, own, me.yp(k)) for k in ORDER]
    crossed = [net.go(own, own, me.cp())]

    def rest():
        for k, copy in zip(ORDER, sent):
            landed([copy])
            block = buf.at[me.c, (me.y + 4 - k) % 4]
            crossed.append(net.go(block, block, me.cp()))
        landed(crossed)
        return sent + crossed

    return rest


class ScatterYC:
    def __init__(self, me, net, part, mate, got):
        self.me, self.net, self.part, self.mate, self.got = me, net, part, mate, got
        self.swap = net.go(part.at[1 - me.c], mate, me.cp())

    def middle(self):
        me, mate = self.me, self.mate
        landed([self.swap])
        mate[...] = (self.part[me.c].astype(F32) + mate[...].astype(F32)).astype(BF)
        self.back = [self.net.go(mate.at[(me.y + k) % 4], self.got.at[k - 1], me.yp(k)) for k in ORDER]

    def end(self):
        total = self.mate[self.me.y].astype(F32)
        landed(self.back)
        for k in range(3):
            total = total + self.got[k].astype(F32)
        self.net.left([self.swap] + self.back)
        return total


def whole(ref, columns):
    return ref[:, :, :, :, columns].reshape(D, -1)


def mlp_forward(me, net, beside, mid, gain, wg, wu, wd, weights, hid, gate, up, prod, acc, part, mate, got, out):
    normed, _ = unit_rms(mid[...])
    hid[me.c, me.y] = (normed * gain).astype(BF)
    rest = gather_yc(me, net, hid)
    beside.step()
    copies = rest()
    weights(0)
    weights(1)

    def first(i, _):
        cols = columns_of(i)
        gate_part = dot(hid[...].reshape(256, D), whole(wg, cols))
        up_part = dot(hid[...].reshape(256, D), whole(wu, cols))
        gate[:, cols] = gate_part
        up[:, cols] = up_part
        prod[:, cols] = (gate_part * jax.nn.sigmoid(gate_part) * up_part).astype(BF)
        return 0

    lax.fori_loop(0, UNITS // CHUNK, first, 0)
    beside.step()
    weights(2)
    acc[...] = jnp.zeros_like(acc)

    def second(i, _):
        cols = columns_of(i)
        acc[...] += dot(prod[:, cols], whole(wd, cols), 1, 1)
        return 0

    lax.fori_loop(0, UNITS // CHUNK, second, 0)
    part[...] = acc[...].astype(BF).reshape(2, 4, OWN, D)
    scatter = ScatterYC(me, net, part, mate, got)
    beside.step()
    scatter.middle()
    beside.step()
    out[...] = mid[...] + scatter.end()
    return copies


def call(kernel, name, collective_id, ins, outs, scratch):
    names = list(ins) + list(outs) + list(scratch)

    def body(*refs):
        kernel(types.SimpleNamespace(**dict(zip(names, refs))))

    def spec(here):
        return pl.BlockSpec(memory_space=pltpu.VMEM if here else pl.ANY)

    results = pl.pallas_call(
        body,
        out_shape=tuple(jax.ShapeDtypeStruct(shape, dtype) for shape, dtype, _ in outs.values()),
        in_specs=[spec(here) for _, here in ins.values()],
        out_specs=tuple(spec(here) for _, _, here in outs.values()),
        scratch_shapes=list(scratch.values()),
        compiler_params=pltpu.CompilerParams(
            collective_id=collective_id, has_side_effects=True, vmem_limit_bytes=63 << 20
        ),
        name=name,
    )(*[array for array, _ in ins.values()])
    return dict(zip(outs, results))


def sems(local, send, recv):
    return {
        "lsem": pltpu.SemaphoreType.DMA((local,)),
        "send": pltpu.SemaphoreType.DMA((send,)),
        "recv": pltpu.SemaphoreType.DMA((recv,)),
    }


KEPT = {
    "hid": ((4, OWN, D), BF),
    "q": ((2, HEADS, TOK, HD), BF),
    "kv": ((2, 2, 4, 4, TOK, 2 * HD), BF),
    "att": ((2 * TOK, HEADS * HD), BF),
    "wf": ((2, 4, 4, 2, ROWS, QKW), BF),
    "x": ((OWN, D), F32),
    "mid": ((OWN, D), F32),
    "hid2": ((2, 4, OWN, D), BF),
    "gate": ((256, UNITS), F32),
    "up": ((256, UNITS), F32),
    "prod": ((256, UNITS), BF),
    "wg": ((4, 4, 2, ROWS, UNITS), BF),
    "wu": ((4, 4, 2, ROWS, UNITS), BF),
    "wd": ((4, 4, 2, ROWS, UNITS), BF),
}
MLP_PARTS = ("wg", "wu", "wd")


def vmem(shape_dtype):
    return pltpu.VMEM(*shape_dtype)


def forward_kernel(r):
    me = Place()
    me.greet()
    net, local = Links(r.send, r.recv), Local(r.lsem)
    peers = me.quad()
    early, late, arrivals = [], [], []
    for core, section, peer in peers:
        early.append(net.go(r.attn_pieces.at[section, core], r.attn_rows.at[me.s, me.c], peer))
        early.append(net.go(r.tiny, r.tiny_quad.at[me.s, me.c], peer))
    here = [
        local.go(r.attn_pieces.at[me.s, me.c], r.attn_rows.at[me.s, me.c]),
        local.go(r.tiny, r.tiny_quad.at[me.s, me.c]),
    ]
    away = pl.ds(pl.multiple_of((1 - me.s) * OWN, OWN), OWN)
    home = pl.ds(pl.multiple_of(me.s * OWN, OWN), OWN)
    tokens_over = net.go(r.ends.at[me.h, away], r.tokens.at[me.s], {"section": 1 - me.s})
    tokens_here = local.go(r.ends.at[me.h, home], r.tokens.at[me.s])
    for part in range(3):
        over = [
            net.go(r.mlp_pieces.at[part, section, core], r.mlp_rows.at[part, me.s, me.c], peer)
            for core, section, peer in peers
        ]
        kept = local.go(r.mlp_pieces.at[part, me.s, me.c], r.mlp_rows.at[part, me.s, me.c])
        arrivals.append((functools.partial(landed, over), kept.wait))
        late.extend(over)

    beside = Beside(2)
    attn_jobs = [None, None]
    mlp_jobs = [[None] * 3, [None] * 3]

    def add_attn(l):
        buf = getattr(r, f"wf{l}").at[me.c]
        attn_jobs[l] = beside.add(Gather(me, net, local, r.attn_rows.at[l], buf))

    def add_mlp(l, part):
        ready = arrivals[part] if l == 0 else ()
        buf = getattr(r, MLP_PARTS[part] + str(l))
        mlp_jobs[l][part] = beside.add(Gather(me, net, local, r.mlp_rows.at[part, l], buf, ready))

    for copy in here:
        copy.wait()
    landed(early)
    r.tiny_mine[...] = (r.tiny_quad[:, 0].astype(F32) + r.tiny_quad[:, 1].astype(F32)).astype(BF)
    one = [net.go(r.tiny_mine, r.tiny_x.at[k - 1], me.xp(k)) for k in ORDER]
    for l in range(2):
        add_attn(l)
        for part in range(3):
            add_mlp(l, part)
    beside.step()
    landed(one)
    r.tiny_row[...] = (
        r.tiny_mine[...].astype(F32) + r.tiny_x[0].astype(F32) + r.tiny_x[1].astype(F32) + r.tiny_x[2].astype(F32)
    ).astype(BF)
    two = [net.go(r.tiny_row, r.tiny_z.at[k - 1], me.zp(k)) for k in ORDER]
    beside.step()
    landed(two)
    r.small[...] = (
        r.tiny_row[...].astype(F32) + r.tiny_z[0].astype(F32) + r.tiny_z[1].astype(F32) + r.tiny_z[2].astype(F32)
    )

    def gain(l, which):
        return jnp.concatenate([r.small[l, 12 * which + i : 12 * which + i + 1, :] for i in range(12)], axis=1)

    def bias(l):
        rows = [r.small[l, pl.ds(24 + HEADS * me.s + i, 1), :] for i in range(HEADS)]
        rows += [r.small[l, 30 + i : 31 + i, :] for i in range(2)]
        return jnp.concatenate(rows, axis=1)

    for l in range(2):
        for which in range(2):
            r.gains[l, which] = gain(l, which)
    tokens_here.wait()
    landed([tokens_over])
    r.low[me.c, me.y] = r.tokens[1].astype(BF)
    low_rest = []

    saved = []

    def save(l, *names):
        for name in names:
            saved.append(local.go(getattr(r, name + str(l)), getattr(r, "out_" + name + str(l))))

    done = []
    for l in range(2):
        kept = types.SimpleNamespace(**{name: getattr(r, name + str(l)) for name in KEPT})
        if l == 0:
            kept.x[...] = r.tokens[0]

        def attn_weights():
            if l == 0:
                low_rest.append(gather_yc(me, net, r.low))
            beside.until(attn_jobs[l])
            swap = net.go(kept.wf.at[me.c], kept.wf.at[me.c], me.cp())
            landed([swap])
            done.append(swap)

        attn_forward(
            me, net, beside, kept.x, r.gains[l, 0], bias(l), r.cos, r.sin, kept.wf, attn_weights,
            kept.hid, kept.q, kept.kv, kept.att, getattr(r, f"part{l}"), getattr(r, f"got{l}"), kept.mid,
        )
        if l == 0:
            done += low_rest[0]()
        save(l, "hid", "q", "kv", "att", "wf", "x", "mid")
        out = r.out1 if l == 1 else r.out0
        done += mlp_forward(
            me, net, beside, kept.mid, r.gains[l, 1], kept.wg, kept.wu, kept.wd,
            lambda part: beside.until(mlp_jobs[l][part]),
            kept.hid2, kept.gate, kept.up, kept.prod, r.acc, getattr(r, f"wide{l}"), getattr(r, f"mate{l}"),
            getattr(r, f"got2{l}"), out,
        )
        save(l, "hid2", "gate", "up", "prod", "wg", "wu", "wd")
        if l == 0:
            r.x1[...] = out[...].astype(BF).astype(F32)
    beside.rest()
    for copy in saved:
        copy.wait()
    net.left(early + late + [tokens_over] + one + two + done)


def forward(attn_pieces, mlp_pieces, tiny, ends, cos, sin):
    ins = {
        "attn_pieces": (attn_pieces, False), "mlp_pieces": (mlp_pieces, False), "tiny": (tiny, False), "ends": (ends, False),
        "cos": (cos, True), "sin": (sin, True),
    }
    outs = {f"out_{name}{l}": (*KEPT[name], False) for l in range(2) for name in KEPT}
    outs["gains"] = ((2, 2, 1, D), F32, True)
    outs["out1"] = ((OWN, D), F32, True)
    outs["low"] = ((2, 4, OWN, D), BF, True)
    outs["tokens"] = ((2, OWN, D), F32, True)
    scratch = {f"{name}{l}": vmem(KEPT[name]) for l in range(2) for name in KEPT}
    scratch |= {
        "attn_rows": pltpu.VMEM((2, 2, ROWS, QKW), BF),
        "mlp_rows": pltpu.VMEM((3, 2, 2, ROWS, UNITS), BF),
        "tiny_quad": pltpu.VMEM((2, 2, 32, 128), BF),
        "tiny_mine": pltpu.VMEM((2, 32, 128), BF),
        "tiny_x": pltpu.VMEM((3, 2, 32, 128), BF),
        "tiny_row": pltpu.VMEM((2, 32, 128), BF),
        "tiny_z": pltpu.VMEM((3, 2, 32, 128), BF),
        "small": pltpu.VMEM((2, 32, 128), F32),
        "out0": pltpu.VMEM((OWN, D), F32),
        "acc": pltpu.VMEM((256, D), F32),
    }
    for l in range(2):
        scratch |= {
            f"part{l}": pltpu.VMEM((4, OWN, D), BF),
            f"got{l}": pltpu.VMEM((3, OWN, D), BF),
            f"wide{l}": pltpu.VMEM((2, 4, OWN, D), BF),
            f"mate{l}": pltpu.VMEM((4, OWN, D), BF),
            f"got2{l}": pltpu.VMEM((3, OWN, D), BF),
        }
    return call(forward_kernel, "forward", 0, ins, outs, scratch | sems(48, 200, 413))


def attn_backward(me, net, beside, r, gm, load_weights):
    wf, dws = r.wg, r.wu
    r.low2[me.y] = gm.astype(BF)
    own = r.low2.at[me.y]
    gathered = [net.go(own, own, me.yp(k)) for k in ORDER]
    beside.step()
    cos, sin = twice(r.cos[...]), twice(r.sin[...])
    load_weights()
    landed(gathered)
    grad_mid = r.low2[...].reshape(2 * TOK, D)
    grad_att = dot(grad_mid, whole(wf, slice(512, 896))).astype(BF)
    for m in range(2):
        rows = slice(m * TOK, (m + 1) * TOK)
        queries = r.q[m].reshape(HEADS * TOK, HD)
        keys = r.kv[:, m, :, :, :, :HD].reshape(2048, HD)
        values = r.kv[:, m, :, :, :, HD:].reshape(2048, HD)
        grad_out = jnp.concatenate([grad_att[rows, h * HD : (h + 1) * HD] for h in range(HEADS)], axis=0)
        scores = masked(dot(queries, keys, 1, 1), me.ctx)
        weight = jnp.exp(scores - jnp.max(scores, axis=1, keepdims=True))
        soft = weight / jnp.sum(weight, axis=1, keepdims=True)
        grad_soft = dot(grad_out, values, 1, 1)
        delta = jnp.sum(soft * grad_soft, axis=1, keepdims=True)
        grad_scores = (soft * (grad_soft - delta)).astype(BF)
        grad_values = dot(soft.astype(BF), grad_out, 0, 0)
        grad_keys = dot(grad_scores, queries, 0, 0) * (HD**-0.5)
        r.dkv[:, m] = jnp.concatenate([grad_keys, grad_values], axis=1).astype(BF).reshape(2, 4, 4, TOK, 2 * HD)
        dq = dot(grad_scores, keys) * (HD**-0.5)
        for h in range(HEADS):
            r.dqs[rows, h * HD : (h + 1) * HD] = dq[h * TOK : (h + 1) * TOK]
        beside.step()
    swap = net.go(r.dkv.at[1 - me.c], r.kmate, me.cp())
    dq_low = jnp.concatenate(
        [turned_back(r.dqs[:, h * HD : (h + 1) * HD], cos, sin).astype(BF) for h in range(HEADS)], axis=1
    )
    hidden = r.hid[...].reshape(2 * TOK, D)
    landed([swap])
    kmate, kz, kx, k2, k3 = r.kmate, r.kz, r.kx, r.k2, r.k3
    kmate[...] = (kmate[...].astype(F32) + r.dkv[me.c].astype(F32)).astype(BF)
    first0 = [net.go(kmate.at[0, (me.z + k) % 4], kz.at[k - 1], me.zp(k)) for k in ORDER]
    first1 = [net.go(kmate.at[1, :, (me.x + k) % 4], kx.at[k - 1], me.xp(k)) for k in ORDER]

    def blocks(value):
        return value.astype(BF).reshape(4, 4, 2, ROWS, -1)

    dws[:, :, :, :, :384] = blocks(dot(hidden, dq_low, 0, 0))
    dws[:, :, :, :, 512:896] = blocks(dot(grad_mid, r.att[...], 0, 0))
    dws[:, :, :, :, 896:1024] = jnp.zeros((4, 4, 2, ROWS, HD), BF)
    beside.step()
    landed(first0)
    total0 = kmate[0, me.z].astype(F32)
    for k in range(3):
        total0 = total0 + kz[k].astype(F32)
    k2[0] = total0.astype(BF)
    second0 = [net.go(k2.at[0, (me.x + k) % 4], k3.at[0, k - 1], me.xp(k)) for k in ORDER]
    landed(first1)
    total1 = kmate[1, :, me.x].astype(F32)
    for k in range(3):
        total1 = total1 + kx[k].astype(F32)
    k2[1] = total1.astype(BF)
    second1 = [net.go(k2.at[1, (me.z + k) % 4], k3.at[1, k - 1], me.zp(k)) for k in ORDER]
    beside.step()
    landed(second0 + second1)
    for m, place in ((0, me.x), (1, me.z)):
        total = k2[m, place].astype(F32)
        for k in range(3):
            total = total + k3[m, k].astype(F32)
        r.kpair[0, m * TOK : (m + 1) * TOK] = total[:, :HD].astype(BF)
        r.kpair[1, m * TOK : (m + 1) * TOK] = total[:, HD:].astype(BF)
    pair = net.go(r.kpair.at[1 - me.s], r.kpair_got, {"section": 1 - me.s})
    landed([pair])
    total = r.kpair[me.s].astype(F32) + r.kpair_got[...].astype(F32)
    dk_low = jnp.where(me.s == 0, turned_back(total, cos, sin), total).astype(BF)
    w_own = jnp.where(me.s == 0, whole(wf, slice(384, 512)), whole(wf, slice(896, 1024)))
    r.part[...] = (
        (dot(dq_low, whole(wf, slice(0, 384)), 1, 1) + dot(dk_low, w_own, 1, 1)).astype(BF).reshape(4, OWN, D)
    )
    back = [net.go(r.part.at[(me.y + k) % 4], r.got.at[k - 1], me.yp(k)) for k in ORDER]
    dws[:, :, :, :, 384:512] = blocks(dot(hidden, dk_low, 0, 0))

    def half(core):
        return pl.ds(pl.multiple_of(core * QKW, QKW), QKW)

    dw_swap = net.go(dws.at[:, :, :, :, half(1 - me.c)], r.da, me.cp())
    beside.step()
    gbias = jnp.concatenate(
        [jnp.sum(dq_low.astype(F32), axis=0, keepdims=True), jnp.sum(dk_low.astype(F32), axis=0, keepdims=True)], axis=1
    )
    dy = r.part[me.y].astype(F32)
    landed(back)
    for k in range(3):
        dy = dy + r.got[k].astype(F32)
    dx, ggain = norm_back(r.x[...], r.gains[0], dy)
    r.gin[...] = gm + dx
    landed([dw_swap])

    def add(j, _):
        r.da[j] = (dws[j, :, :, :, half(me.c)].astype(F32) + r.da[j].astype(F32)).astype(BF)
        return 0

    lax.fori_loop(0, 4, add, 0)
    net.left(gathered + [swap] + first0 + first1 + second0 + second1 + [pair] + back + [dw_swap])
    return ggain, gbias


def mlp_backward(me, net, beside, r, g, loaded, scatter):
    loaded("prod")

    def weight_grad(dw, left_ref, right_ref):
        def step(i, _):
            cols = columns_of(i)
            dw[:, :, :, :, cols] = (
                dot(left_ref[...].reshape(256, D), right_ref[:, cols], 0, 0).astype(BF).reshape(4, 4, 2, ROWS, CHUNK)
            )
            return 0

        lax.fori_loop(0, UNITS // CHUNK, step, 0)

    weight_grad(r.dd, r.low, r.prod)
    scatter(2)
    beside.step()
    loaded("gate", "up", "wd", "wg", "wu", "hid2")
    r.acc[...] = jnp.zeros_like(r.acc)

    def step(i, _):
        cols = columns_of(i)
        dprod = dot(r.low[...].reshape(256, D), whole(r.wd, cols))
        gate, up = r.gate[:, cols], r.up[:, cols]
        sigma = jax.nn.sigmoid(gate)
        dg = (dprod * up * sigma * (1.0 + gate * (1.0 - sigma))).astype(BF)
        du = (dprod * gate * sigma).astype(BF)
        r.dgate[:, cols] = dg
        r.dup[:, cols] = du
        r.acc[...] += dot(dg, whole(r.wg, cols), 1, 1) + dot(du, whole(r.wu, cols), 1, 1)
        return 0

    lax.fori_loop(0, UNITS // CHUNK, step, 0)
    r.wide[...] = r.acc[...].astype(BF).reshape(2, 4, OWN, D)
    sums = ScatterYC(me, net, r.wide, r.mate, r.got2)
    beside.step()
    weight_grad(r.dg, r.hid2, r.dgate)
    sums.middle()
    scatter(0)
    beside.step()
    weight_grad(r.du, r.hid2, r.dup)
    scatter(1)
    beside.step()
    dy = sums.end()
    du, ggain = norm_back(r.mid[...], r.gains[1], dy)
    return g + du, ggain


def put_small(r, base, y, ggain0, ggain1, gbias):
    r.sums[0, base + 24 : base + 40] = jnp.zeros((16, 128), F32)
    for which, ggain in enumerate((ggain0, ggain1)):
        for i in range(12):
            r.sums[0, base + 12 * which + i : base + 12 * which + i + 1] = ggain[:, i * 128 : (i + 1) * 128]
    for i in range(4):
        r.sums[0, pl.ds(base + 24 + 4 * y + i, 1)] = gbias[:, i * 128 : (i + 1) * 128]


def backward_kernel(last, r):
    me = Place()
    local = Local(r.lsem)
    names = ("prod", "low", "gate", "up", "wd", "wg", "wu", "hid2", "mid", "hid", "q", "kv", "att", "x")
    pending = {}

    def load(name):
        pending[name] = local.go(getattr(r, "in_" + name), getattr(r, name))

    def loaded(*wanted):
        for name in wanted:
            pending.pop(name).wait()

    for name in names:
        if not (last and name == "low"):
            load(name)
    me.greet()
    net = Links(r.send, r.recv)
    beside = Beside(2)
    extra = []
    g = r.g[...]
    if last:
        g = g.astype(BF).astype(F32)
        r.low[me.c, me.y] = g.astype(BF)
        rest = gather_yc(me, net, r.low)
        res = [local.go(r.in_sums1, r.res_m.at[:, 1]), local.go(r.in_out1, r.ends2.at[1])]
        da1 = local.go(r.in_da1, r.da1)
        crossed = []

        def go_home(src, dst):
            for core, section, peer in me.quad():
                crossed.append(net.go(src.at[section, core], dst.at[me.s, me.c], peer))
            extra.append(local.go(src.at[me.s, me.c], dst.at[me.s, me.c]))

        da1.wait()
        beside.add(Scatter(me, net, r.da1, (r.a1_r1, r.a1_r2, r.a1_u1, r.a1_u2), r.res_a.at[1]))
        beside.step()

    def scatter(part):
        dw = (r.dg, r.du, r.dd)[part]
        job = tuple(getattr(r, f"m{part}_{name}") for name in ("r1", "r2", "u1", "u2"))
        if last:
            out = r.res_m.at[part, 0]
            beside.add(Scatter(me, net, dw, job, out, lambda: go_home(r.res_m.at[part], r.m_home.at[part])))
        else:
            beside.add(Scatter(me, net, dw, job, r.sums1.at[part]))

    if last:
        low_copies = rest()
        for copy in res:
            copy.wait()
    loaded("mid", *(() if last else ("low",)))
    gm, ggain1 = mlp_backward(me, net, beside, r, g, loaded, scatter)

    wf_copies = [
        local.go(r.in_wf.at[0], r.wg.at[:, :, :, :, :QKW]), local.go(r.in_wf.at[1], r.wg.at[:, :, :, :, QKW : 2 * QKW])
    ]

    def load_weights():
        for copy in wf_copies:
            copy.wait()
        loaded("hid", "q", "kv", "att", "x")

    ggain0, gbias = attn_backward(me, net, beside, r, gm, load_weights)
    if not last:
        put_small(r, 0, me.y, ggain0, ggain1, gbias)
        r.small1[...] = r.sums[0]
        da_out = local.go(r.da, r.out_da)
        beside.rest()
        da_out.wait()
        return
    beside.add(
        Scatter(
            me, net, r.da, (r.a0_r1, r.a0_r2, r.a0_u1, r.a0_u2), r.res_a.at[0],
            lambda: go_home(r.res_a, r.a_home),
        )
    )
    beside.step()
    r.ends2[0] = r.gin[...]
    for k in ORDER:
        crossed.append(net.go(r.ends2.at[((me.y + k) % 4) % 2], r.boundary.at[me.y], me.yp(k)))
    r.boundary[me.y] = r.ends2[me.s]
    put_small(r, 0, me.y, ggain0, ggain1, gbias)
    r.sums[0, 40:] = r.small1[...]
    rounds = ((me.yp, ORDER, 0), (lambda k: me.cp(), (1,), 3), (me.xp, ORDER, 4), (me.zp, ORDER, 7))
    small = []
    for turn, (peer, ks, slot) in enumerate(rounds):
        sent = [net.go(r.sums.at[turn], r.sums_got.at[slot + k - 1], peer(k)) for k in ks]
        beside.step()
        landed(sent)
        total = r.sums[turn]
        for k in ks:
            total = total + r.sums_got[slot + k - 1]
        r.sums[turn + 1] = total
        small.extend(sent)
    r.small[...] = r.sums[4]
    beside.rest()
    landed(crossed)
    for copy in extra:
        copy.wait()
    net.left(low_copies + crossed + small)


def backward(last, kept, g, gains, cos, sin, more):
    ins = {"in_" + name: (kept[name], False) for name in KEPT}
    ins |= {"g": (g, True), "gains": (gains, True), "cos": (cos, True), "sin": (sin, True)}
    if last:
        ins |= {
            "in_sums1": (more["sums1"], False), "in_out1": (more["out1"], False), "in_da1": (more["out_da"], False),
            "small1": (more["small1"], True),
        }
        outs = {
            "m_home": ((3, 2, 2, ROWS, UNITS), BF, False),
            "a_home": ((2, 2, ROWS, QKW), BF, False),
            "boundary": ((4, OWN, D), F32, True),
            "small": ((80, 128), F32, True),
        }
    else:
        ins["in_low"] = (more["low"], False)
        outs = {
            "sums1": ((3, 2, ROWS, UNITS), BF, True),
            "out_da": ((4, 4, 2, ROWS, QKW), BF, False),
            "small1": ((40, 128), F32, True),
            "gin": ((OWN, D), F32, True),
        }
    scratch = {name: vmem(KEPT[name]) for name in KEPT if name != "wf"}
    blocks = (4, 4, 2, ROWS, UNITS)
    scratch |= {
        "low": pltpu.VMEM((2, 4, OWN, D), BF),
        "dgate": pltpu.VMEM((256, UNITS), BF),
        "dup": pltpu.VMEM((256, UNITS), BF),
        "acc": pltpu.VMEM((256, D), F32),
        "wide": pltpu.VMEM((2, 4, OWN, D), BF),
        "mate": pltpu.VMEM((4, OWN, D), BF),
        "got2": pltpu.VMEM((3, OWN, D), BF),
        "dg": pltpu.VMEM(blocks, BF),
        "du": pltpu.VMEM(blocks, BF),
        "dd": pltpu.VMEM(blocks, BF),
        "low2": pltpu.VMEM((4, OWN, D), BF),
        "dkv": pltpu.VMEM((2, 2, 4, 4, TOK, 2 * HD), BF),
        "kmate": pltpu.VMEM((2, 4, 4, TOK, 2 * HD), BF),
        "kz": pltpu.VMEM((3, 4, TOK, 2 * HD), BF),
        "kx": pltpu.VMEM((3, 4, TOK, 2 * HD), BF),
        "k2": pltpu.VMEM((2, 4, TOK, 2 * HD), BF),
        "k3": pltpu.VMEM((2, 3, TOK, 2 * HD), BF),
        "kpair": pltpu.VMEM((2, 2 * TOK, HD), BF),
        "kpair_got": pltpu.VMEM((2 * TOK, HD), BF),
        "dqs": pltpu.VMEM((2 * TOK, HEADS * HD), F32),
        "da": pltpu.VMEM((4, 4, 2, ROWS, QKW), BF),
        "part": pltpu.VMEM((4, OWN, D), BF),
        "got": pltpu.VMEM((3, OWN, D), BF),
        "sums": pltpu.VMEM((5, 80, 128) if last else (1, 40, 128), F32),
    }
    jobs = {f"m{part}": UNITS for part in range(3)}
    if last:
        jobs |= {"a0": QKW, "a1": QKW}
        scratch |= {
            "gin": pltpu.VMEM((OWN, D), F32),
            "da1": pltpu.VMEM((4, 4, 2, ROWS, QKW), BF),
            "res_m": pltpu.VMEM((3, 2, 2, ROWS, UNITS), BF),
            "res_a": pltpu.VMEM((2, 2, ROWS, QKW), BF),
            "ends2": pltpu.VMEM((2, OWN, D), F32),
            "sums_got": pltpu.VMEM((10, 80, 128), F32),
        }
    for job, columns in jobs.items():
        for name, ref in zip(("r1", "r2", "u1", "u2"), Scatter.scratch(columns)):
            scratch[f"{job}_{name}"] = ref
    return call(
        functools.partial(backward_kernel, last), "backward", 1 + last, ins, outs,
        scratch | (sems(28, 140, 144) if last else sems(28, 80, 84)),
    )


def unit_slices(w):
    padded = jnp.pad(w, ((0, 0), (0, 4 * UNITS - w.shape[1])))
    return padded.reshape(w.shape[0], 2, 2, UNITS).transpose(1, 2, 0, 3)


def body(ends, w_query, w_kv, w_out, w_gate_up, w_down, gains, bias_query, bias_kv):
    me = Place()
    rows = w_query.shape[1]
    wq = w_query[0].reshape(rows, 2, 384)
    wo = w_out[0].reshape(rows, 2, 384)
    attn_pieces = jnp.stack(
        [
            jnp.stack(
                [
                    jnp.concatenate([wq[:, s], w_kv[0, :, 0]], axis=1),
                    jnp.concatenate([wo[:, s], w_kv[0, :, 1]], axis=1),
                ]
            )
            for s in range(2)
        ]
    )
    mlp_pieces = jnp.stack(
        [unit_slices(w_gate_up[0, :, 0]), unit_slices(w_gate_up[0, :, 1]), unit_slices(w_down[0])]
    )
    tiny = jnp.concatenate(
        [
            lax.dynamic_update_slice(jnp.zeros((2, D), BF), gains[0], (0, me.ctx * 48)).reshape(24, 128),
            lax.dynamic_update_slice(
                jnp.zeros((8, 128), BF),
                jnp.concatenate([bias_query[0], bias_kv[0].reshape(2, 4)], axis=0),
                (0, me.ctx * 4),
            ),
        ],
        axis=0,
    )
    positions = (me.ctx * TOK + jnp.arange(TOK, dtype=jnp.int32)).astype(F32)
    inverse = 1.0 / THETA ** (jnp.arange(0, HD, 2, dtype=F32) / HD)
    angles = positions[:, None] * inverse[None, :]
    cos = jnp.concatenate([jnp.cos(angles), jnp.cos(angles)], axis=1)
    sin = jnp.concatenate([-jnp.sin(angles), jnp.sin(angles)], axis=1)

    ahead = forward(attn_pieces, mlp_pieces, tiny, ends[0], cos, sin)
    kept = [{name: ahead[f"out_{name}{l}"] for name in KEPT} for l in range(2)]
    gain_all = ahead["gains"]
    upper = backward(False, kept[1], ahead["tokens"][1], gain_all[1], cos, sin, ahead)
    done = backward(True, kept[0], upper["gin"], gain_all[0], cos, sin, upper | {"out1": ahead["out1"]})

    small = done["small"].reshape(2, 40, 128)
    small = lax.dynamic_index_in_dim(small, me.s, 0, keepdims=False)
    gain_sum = lax.dynamic_index_in_dim(small[:24].reshape(2, 32, 48), me.ctx, 1, keepdims=False)
    bias_sum = small[24:].reshape(2, 2, 4, 32, 4)
    bias_sum = lax.dynamic_index_in_dim(bias_sum, me.h, 0, keepdims=False)
    bias_sum = lax.dynamic_index_in_dim(bias_sum, me.ctx, 2, keepdims=False)

    attn_home = done["a_home"].astype(F32)
    mlp_home = done["m_home"].astype(F32).transpose(3, 0, 1, 2, 4).reshape(rows, 3, 4 * UNITS)
    mlp_home = mlp_home[:, :, : w_down.shape[2]]
    return (
        done["boundary"].reshape(1, 2, TOK, D),
        attn_home[:, 0, :, :384].transpose(1, 0, 2).reshape(1, rows, 768),
        attn_home[:, 0, :, 384:].transpose(1, 0, 2)[None],
        attn_home[:, 1, :, :384].transpose(1, 0, 2).reshape(1, rows, 768),
        mlp_home[:, :2][None],
        mlp_home[:, 2][None],
        gain_sum[None],
        bias_sum[:, :HEADS].reshape(1, 6, 4),
        bias_sum[:, HEADS].reshape(1, 2, 1, 4),
    )


def solution(mesh):
    placed = (
        P("section", None, "ctx", None),
        P("section", "ctx", "shard"),
        P("section", "ctx", None, "shard"),
        P("section", "ctx", "shard"),
        P("section", "ctx", None, "shard"),
        P("section", "ctx", "shard"),
        P("section", None, "ctx"),
        P("section", "shard", "ctx"),
        P("section", None, "shard", "ctx"),
    )
    return jax.shard_map(
        body,
        mesh=mesh,
        in_specs=placed,
        out_specs=(
            P("section", None, "ctx", None),
            P("section", "ctx", "shard"),
            P("section", "ctx", None, "shard"),
            P("section", "ctx", "shard"),
            P("section", "ctx", None, "shard"),
            P("section", "ctx", "shard"),
            P("section", None, "ctx"),
            P("section", "shard", "ctx"),
            P("section", None, "shard", "ctx"),
        ),
        check_vma=False,
    )
```

```python
import functools
import types

import jax
import jax.numpy as jnp
from jax import lax
from jax.experimental import pallas as pl
from jax.experimental.pallas import tpu as pltpu
from jax.sharding import PartitionSpec as P

MESH = pl.DeviceIdType.MESH
BF = jnp.bfloat16
F32 = jnp.float32
EPS = 1e-06
THETA = 1000000.0
D = 1536
HD = 128
HEADS = 3
UNITS = 1152
CHUNK = 384
TOK = 64
OWN = 32
ROWS = 48
QKW = 512
ORDER = (1, 3, 2)
SIDES = (1, 3)
OTHERS = tuple((dz, dx) for dz in range(4) for dx in range(4) if (dz, dx) != (0, 0))


class Place:
    def __init__(self):
        self.ctx = lax.axis_index("ctx")
        self.s = lax.axis_index("section")
        self.h = lax.axis_index("shard")
        self.z = self.ctx // 8
        self.x = (self.ctx // 2) % 4
        self.c = self.ctx % 2
        self.y = self.h * 2 + self.s

    def yp(self, k):
        other = (self.y + k) % 4
        return dict(section=other % 2, shard=other // 2)

    def xp(self, k):
        return dict(ctx=self.z * 8 + ((self.x + k) % 4) * 2 + self.c)

    def zp(self, k):
        return dict(ctx=(self.ctx + 8 * k) % 32)

    def cp(self):
        return dict(ctx=self.ctx + 1 - 2 * self.c)

    def quad(self):
        return (
            (self.c, 1 - self.s, dict(section=1 - self.s)),
            (1 - self.c, self.s, self.cp()),
            (1 - self.c, 1 - self.s, dict(section=1 - self.s, ctx=self.ctx + 1 - 2 * self.c)),
        )

    def chip(self, dz, dx):
        return dict(ctx=((self.z + dz) % 4) * 8 + ((self.x + dx) % 4) * 2 + self.c)

    def greet(self, far=False):
        peers = [self.yp(k) for k in ORDER] + [self.cp(), self.quad()[2][2]]
        peers += [self.xp(k) for k in ORDER] + [self.zp(k) for k in ORDER]
        if far:
            peers += [self.chip(dz, dx) for dz, dx in OTHERS if dz and dx]
        barrier = pltpu.get_barrier_semaphore()
        for peer in peers:
            pl.semaphore_signal(barrier, 1, device_id=peer, device_id_type=MESH)
        pl.semaphore_wait(barrier, len(peers))


class Links:
    def __init__(self, send, recv):
        self.send, self.recv, self.count = send, recv, 0
        self.free = list(range(send.shape[0]))

    def go(self, src, dst, peer):
        index = self.count
        self.count += 1
        slot = self.free.pop(0)
        copy = pltpu.make_async_remote_copy(
            src, dst, self.send.at[slot], self.recv.at[index], device_id=peer, device_id_type=MESH
        )
        copy.start()
        return copy, slot

    def left(self, copies):
        for copy, slot in copies:
            copy.wait_send()
            self.free.append(slot)


def landed(copies):
    for copy, _ in copies:
        copy.wait_recv()


class Local:
    def __init__(self, sems):
        self.sems, self.count = sems, 0

    def go(self, src, dst):
        copy = pltpu.make_async_copy(src, dst, self.sems.at[self.count])
        self.count += 1
        copy.start()
        return copy


def cuts(columns):
    cut = (columns // 256) * 128
    return (slice(0, cut), slice(cut, columns))


class Gather:
    copies = 40

    def __init__(self, me, net, local, src, buf, ready=(), then=None):
        self.me, self.net, self.local, self.src, self.buf, self.ready = me, net, local, src, buf, ready
        self.then = then
        self.cuts = cuts(src.shape[-1])
        self.sent = []

    def steps(self):
        by_half = [functools.partial(f, half) for f in (self.second, self.third, self.fourth) for half in range(2)]
        return [self.start, *by_half, self.finish]

    def at(self, half, p, q):
        return self.buf.at[q, p, 0] if half == 0 else self.buf.at[p, q, 1]

    def axes(self, half):
        me = self.me
        return (me.x, me.z, me.xp, me.zp) if half == 0 else (me.z, me.x, me.zp, me.xp)

    def go(self, src, dst, peer):
        copy = self.net.go(src, dst, peer)
        self.sent.append(copy)
        return copy

    def start(self):
        me = self.me
        for wait in self.ready:
            wait()
        self.own = self.local.go(self.src, self.buf.at[me.z, me.x])
        self.a, self.c = [None, None], [[None] * 4, [None] * 4]
        self.f, self.last = [[], []], []
        for half in range(2):
            p, q, pp, qp = self.axes(half)
            self.a[half] = [self.go(self.src.at[half], self.at(half, p, q), pp(k)) for k in SIDES]
        for half in range(2):
            p, q, pp, qp = self.axes(half)
            self.c[half][0] = [self.go(self.src.at[half], self.at(half, p, q), qp(k)) for k in SIDES]

    def second(self, half):
        p, q, pp, qp = self.axes(half)
        for i, k in enumerate(SIDES):
            landed([self.a[half][i]])
            piece = self.at(half, (p + 4 - k) % 4, q).at[:, self.cuts[i]]
            self.f[half].append(self.go(piece, piece, pp(k)))
        for i, k in enumerate(SIDES):
            block = self.at(half, (p + 4 - k) % 4, q)
            self.c[half][i + 1] = [self.go(block, block, qp(kk)) for kk in SIDES]

    def third(self, half):
        p, q, pp, qp = self.axes(half)
        landed(self.f[half])
        block = self.at(half, (p + 2) % 4, q)
        self.c[half][3] = [self.go(block, block, qp(kk)) for kk in SIDES]
        self.onward(half, (0,))

    def fourth(self, half):
        self.onward(half, (1, 2, 3))

    def onward(self, half, turns):
        p, q, pp, qp = self.axes(half)
        for j in turns:
            shift = (0, 3, 1, 2)[j]
            for i, k in enumerate(SIDES):
                landed([self.c[half][j][i]])
                piece = self.at(half, (p + shift) % 4, (q + 4 - k) % 4).at[:, self.cuts[i]]
                self.last.append(self.go(piece, piece, qp(k)))

    def finish(self):
        landed(self.last)
        self.own.wait()
        self.net.left(self.sent)
        if self.then is not None:
            self.then()


class Scatter:
    copies = 16

    def __init__(self, me, net, part, scratch, out, then=None):
        self.me, self.net, self.part, self.out, self.then = me, net, part, out, then
        self.r1, self.r2, self.u1, self.u2 = scratch
        self.cuts = cuts(part.shape[-1])
        self.sent = []

    def steps(self):
        by_half = [functools.partial(f, half) for f in (self.second, self.third, self.fourth) for half in range(2)]
        return [self.start, *by_half, self.finish]

    @staticmethod
    def scratch(columns):
        wide = columns - (columns // 256) * 128
        return [
            pltpu.VMEM((2, 2, 4, ROWS, wide), BF),
            pltpu.VMEM((2, 2, 4, ROWS, columns), BF),
            pltpu.VMEM((2, 2, ROWS, wide), BF),
            pltpu.VMEM((2, 2, ROWS, columns), BF),
        ]

    def group(self, half, q):
        return self.part.at[q, :, 0] if half == 0 else self.part.at[:, q, 1]

    def axes(self, half):
        me = self.me
        return (me.x, me.z, me.xp, me.zp) if half == 0 else (me.z, me.x, me.zp, me.xp)

    def go(self, src, dst, peer):
        copy = self.net.go(src, dst, peer)
        self.sent.append(copy)
        return copy

    def wide(self, i):
        return slice(0, self.cuts[i].stop - self.cuts[i].start)

    def start(self):
        self.one, self.two, self.three, self.four = ([[], []] for _ in range(4))
        for half in range(2):
            p, q, pp, qp = self.axes(half)
            for i, k in enumerate(SIDES):
                piece = self.group(half, (q + 2) % 4).at[:, :, self.cuts[i]]
                self.one[half].append(self.go(piece, self.r1.at[half, i, :, :, self.wide(i)], qp(k)))

    def second(self, half):
        p, q, pp, qp = self.axes(half)
        for i, k in enumerate(SIDES):
            landed([self.one[half][i]])
            mine = self.group(half, (q + k) % 4)

            def add(j, _):
                mine[j, :, self.cuts[i]] = (
                    mine[j, :, self.cuts[i]].astype(F32) + self.r1[half, i, j, :, self.wide(i)].astype(F32)
                ).astype(BF)
                return 0

            lax.fori_loop(0, 4, add, 0)
            self.two[half].append(self.go(mine, self.r2.at[half, i], qp(k)))

    def third(self, half):
        p, q, pp, qp = self.axes(half)
        landed(self.two[half])
        mine = self.group(half, q)

        def add(j, _):
            mine[j] = (
                mine[j].astype(F32) + self.r2[half, 0, j].astype(F32) + self.r2[half, 1, j].astype(F32)
            ).astype(BF)
            return 0

        lax.fori_loop(0, 4, add, 0)
        for i, k in enumerate(SIDES):
            self.three[half].append(
                self.go(mine.at[(p + 2) % 4, :, self.cuts[i]], self.u1.at[half, i, :, self.wide(i)], pp(k))
            )

    def fourth(self, half):
        p, q, pp, qp = self.axes(half)
        for i, k in enumerate(SIDES):
            landed([self.three[half][i]])
            block = self.group(half, q).at[(p + k) % 4]
            block[:, self.cuts[i]] = (
                block[:, self.cuts[i]].astype(F32) + self.u1[half, i, :, self.wide(i)].astype(F32)
            ).astype(BF)
            self.four[half].append(self.go(block, self.u2.at[half, i], pp(k)))

    def finish(self):
        for half in range(2):
            p, q, pp, qp = self.axes(half)
            landed(self.four[half])
            self.out[half] = (
                self.group(half, q)[p].astype(F32) + self.u2[half, 0].astype(F32) + self.u2[half, 1].astype(F32)
            ).astype(BF)
        self.net.left(self.sent)
        if self.then is not None:
            self.then()


class DirectScatter:
    def __init__(self, me, net, part, got, out):
        self.me, self.net, self.part, self.got, self.out = me, net, part, got, out
        self.sent = []
        for i, (dz, dx) in enumerate(OTHERS):
            src = part.at[(me.z + dz) % 4, (me.x + dx) % 4]
            self.sent.append(net.go(src, got.at[i], me.chip(dz, dx)))

    def finish(self):
        total = self.part[self.me.z, self.me.x].astype(F32)
        landed(self.sent)
        for i in range(len(OTHERS)):
            total = total + self.got[i].astype(F32)
        self.out[...] = total.astype(BF)
        self.net.left(self.sent)


class Beside:
    def __init__(self, lags, turns):
        self.lags, self.turns, self.turn, self.jobs = lags, list(turns), 0, []

    def add(self, job):
        first = self.turn
        if self.jobs:
            first = max(first, self.jobs[-1][0] + self.lags[len(self.jobs)])
        self.jobs.append((first, list(job.steps()), job))
        return job

    def step(self):
        for _ in range(self.turns.pop(0) if self.turns else 0):
            self.take()

    def take(self):
        for first, steps, _ in reversed(self.jobs):
            if self.turn >= first and steps:
                steps.pop(0)()
        self.turn += 1

    def until(self, *jobs):
        while any(steps for _, steps, job in self.jobs if job in jobs):
            self.take()

    def rest(self):
        while any(steps for _, steps, _ in self.jobs):
            self.take()


def dot(a, b, ca=1, cb=0):
    return lax.dot_general(a, b, (((ca,), (cb,)), ((), ())), preferred_element_type=F32)


def unit_rms(u):
    scale = lax.rsqrt(jnp.mean(u * u, axis=1, keepdims=True) + EPS)
    return u * scale, scale


def norm_back(u, gain, dy):
    n, scale = unit_rms(u)
    sd = dy * gain
    return scale * (sd - n * jnp.mean(sd * n, axis=1, keepdims=True)), jnp.sum(dy * n, axis=0, keepdims=True)


def turned(u, cos, sin):
    return u * cos + pltpu.roll(u, 64, 1) * sin


def turned_back(w, cos, sin):
    return w * cos - pltpu.roll(w, 64, 1) * sin


def twice(table):
    return jnp.concatenate([table, table], axis=0)


def key_places(rows):
    j = lax.broadcasted_iota(jnp.int32, (rows, 2048), 1)
    core = j // 1024
    chip = (j % 1024) // TOK
    return chip * (2 * TOK) + core * TOK + j % TOK


def masked(raw, ctx):
    rows = raw.shape[0]
    query = ctx * TOK + lax.broadcasted_iota(jnp.int32, (rows, 2048), 0) % TOK
    return jnp.where(key_places(rows) <= query, raw * (HD**-0.5), -1e30)


def columns_of(i, base=0):
    return pl.ds(pl.multiple_of(base + i * CHUNK, CHUNK), CHUNK)


def attn_forward(me, net, beside, x_ref, gain, bias, turns, wf, weights, hid, q, kv, att, part, got, mid):
    x = x_ref[...]
    normed, _ = unit_rms(x)
    hid[me.y] = (normed * gain).astype(BF)
    hid_copies = [net.go(hid.at[me.y], hid.at[me.y], me.yp(k)) for k in ORDER]
    cos, sin = twice(turns[0]), twice(turns[1])
    weights()
    landed(hid_copies)
    hidden = hid[...].reshape(2 * TOK, D)
    proj = dot(hidden, whole(wf.at[0], slice(0, QKW))) + bias[:, :QKW]
    key = turned(proj[:, 384:], cos, sin).astype(BF)
    value = (dot(hidden, whole(wf.at[1], slice(384, QKW))) + bias[:, QKW:]).astype(BF)
    keyval = jnp.concatenate([key, value], axis=1)
    for m in range(2):
        kv[me.c, m, me.z, me.x] = keyval[m * TOK : (m + 1) * TOK]
    mine0, mine1 = kv.at[me.c, 0, me.z, me.x], kv.at[me.c, 1, me.z, me.x]
    first0 = [net.go(mine0, mine0, me.xp(k)) for k in ORDER]
    first1 = [net.go(mine1, mine1, me.zp(k)) for k in ORDER]
    for head in range(HEADS):
        query = turned(proj[:, head * HD : (head + 1) * HD], cos, sin).astype(BF)
        for m in range(2):
            q[m, head] = query[m * TOK : (m + 1) * TOK]
    beside.step()
    landed(first0)
    second0 = [net.go(kv.at[me.c, 0, me.z], kv.at[me.c, 0, me.z], me.zp(k)) for k in ORDER]
    landed(first1)
    second1 = [net.go(kv.at[me.c, 1, :, me.x], kv.at[me.c, 1, :, me.x], me.xp(k)) for k in ORDER]
    beside.step()
    landed(second0)
    third0 = net.go(kv.at[me.c, 0], kv.at[me.c, 0], me.cp())
    landed(second1)
    third1 = net.go(kv.at[me.c, 1], kv.at[me.c, 1], me.cp())
    for m, third in ((0, third0), (1, third1)):
        beside.step()
        landed([third])
        queries = q[m].reshape(HEADS * TOK, HD)
        keys = kv[:, m, :, :, :, :HD].reshape(2048, HD)
        values = kv[:, m, :, :, :, HD:].reshape(2048, HD)
        scores = masked(dot(queries, keys, 1, 1), me.ctx)
        weight = jnp.exp(scores - jnp.max(scores, axis=1, keepdims=True))
        total = jnp.sum(weight, axis=1, keepdims=True)
        out = (dot(weight.astype(BF), values) / total).astype(BF)
        for head in range(HEADS):
            att[m * TOK : (m + 1) * TOK, head * HD : (head + 1) * HD] = out[head * TOK : (head + 1) * TOK]
    beside.step()
    part[...] = dot(att[...], whole(wf.at[1], slice(0, 384)), 1, 1).astype(BF).reshape(4, OWN, D)
    back = [net.go(part.at[(me.y + k) % 4], got.at[k - 1], me.yp(k)) for k in ORDER]
    beside.step()
    total = x + part[me.y].astype(F32)
    landed(back)
    for k in range(3):
        total = total + got[k].astype(F32)
    mid[...] = total
    net.left(hid_copies + first0 + first1 + second0 + second1 + [third0, third1] + back)


def gather_yc(me, net, buf):
    own = buf.at[me.c, me.y]
    sent = [net.go(own, own, me.yp(k)) for k in ORDER]
    crossed = [net.go(own, own, me.cp())]

    def rest():
        for k, copy in zip(ORDER, sent):
            landed([copy])
            block = buf.at[me.c, (me.y + 4 - k) % 4]
            crossed.append(net.go(block, block, me.cp()))
        landed(crossed)
        return sent + crossed

    return rest


class ScatterYC:
    def __init__(self, me, net, part, mate, got):
        self.me, self.net, self.part, self.mate, self.got = me, net, part, mate, got
        self.swap = net.go(part.at[1 - me.c], mate, me.cp())

    def middle(self):
        me, mate = self.me, self.mate
        landed([self.swap])
        mate[...] = (self.part[me.c].astype(F32) + mate[...].astype(F32)).astype(BF)
        self.back = [self.net.go(mate.at[(me.y + k) % 4], self.got.at[k - 1], me.yp(k)) for k in ORDER]

    def end(self):
        total = self.mate[self.me.y].astype(F32)
        landed(self.back)
        for k in range(3):
            total = total + self.got[k].astype(F32)
        self.net.left([self.swap] + self.back)
        return total


def whole(ref, columns):
    return ref[:, :, :, :, columns].reshape(D, -1)


def mlp_product(me, net, beside, mid, gain, wm, weights, hid, gate, up, prod):
    normed, _ = unit_rms(mid[...])
    hid[me.c, me.y] = (normed * gain).astype(BF)
    rest = gather_yc(me, net, hid)
    beside.step()
    copies = rest()
    weights(GATE, UP)

    def first(i, _):
        cols = columns_of(i)
        gate_part = dot(hid[...].reshape(256, D), whole(wm, cols))
        up_part = dot(hid[...].reshape(256, D), whole(wm, columns_of(i, UNITS)))
        gate[:, cols] = gate_part
        up[:, cols] = up_part
        prod[:, cols] = (gate_part * jax.nn.sigmoid(gate_part) * up_part).astype(BF)
        return 0

    lax.fori_loop(0, UNITS // CHUNK, first, 0)
    net.left(copies)


def mlp_down(me, net, wm, prod, part, mate, got):
    part[...] = dot(prod[...], whole(wm, DOWN), 1, 1).astype(BF).reshape(2, 4, OWN, D)
    return ScatterYC(me, net, part, mate, got)


def call(kernel, name, collective_id, ins, outs, scratch):
    names = list(ins) + list(outs) + list(scratch)

    def body(*refs):
        kernel(types.SimpleNamespace(**dict(zip(names, refs))))

    def spec(here):
        return pl.BlockSpec(memory_space=pltpu.VMEM if here else pl.ANY)

    results = pl.pallas_call(
        body,
        out_shape=tuple(jax.ShapeDtypeStruct(shape, dtype) for shape, dtype, _ in outs.values()),
        in_specs=[spec(here) for _, here in ins.values()],
        out_specs=tuple(spec(here) for _, _, here in outs.values()),
        scratch_shapes=list(scratch.values()),
        compiler_params=pltpu.CompilerParams(
            collective_id=collective_id, has_side_effects=True, vmem_limit_bytes=63 << 20
        ),
        name=name,
    )(*[array for array, _ in ins.values()])
    return dict(zip(outs, results))


def sems(local, send, recv):
    return dict(
        lsem=pltpu.SemaphoreType.DMA((local,)),
        send=pltpu.SemaphoreType.DMA((send,)),
        recv=pltpu.SemaphoreType.DMA((recv,)),
    )


KEPT = dict(
    hid=((4, OWN, D), BF),
    q=((2, HEADS, TOK, HD), BF),
    kv=((2, 2, 4, 4, TOK, 2 * HD), BF),
    att=((2 * TOK, HEADS * HD), BF),
    wf=((2, 4, 4, 2, ROWS, QKW), BF),
    x=((OWN, D), F32),
    mid=((OWN, D), F32),
    hid2=((2, 4, OWN, D), BF),
    gate=((256, UNITS), F32),
    up=((256, UNITS), F32),
    prod=((256, UNITS), BF),
    wm=((4, 4, 2, ROWS, 3 * UNITS), BF),
)
GATE, UP, DOWN = (slice(part * UNITS, (part + 1) * UNITS) for part in range(3))
FORWARD_LAGS, FORWARD_TURNS = (5, 4, 3, 0, 6, 1, 6, 3), (4, 3, 1, 1, 1, 1, 0, 2, 2, 0, 0, 4, 1, 2, 1, 2, 0, 0, 1, 3, 0)
UPPER_LAGS, UPPER_TURNS = (5, 1, 1), (1, 0, 0, 2, 0, 0, 0, 2, 2, 2)
LOWER_LAGS, LOWER_TURNS = (5, 2, 1, 3, 3), (3, 0, 1, 0, 1, 1, 0, 0, 2, 2, 2, 2)


def vmem(shape_dtype):
    return pltpu.VMEM(*shape_dtype)


def forward_kernel(r):
    me = Place()
    me.greet()
    net, local = Links(r.send, r.recv), Local(r.lsem)
    peers = me.quad()
    early, late, arrivals = [], [], []
    everyone = me.quad() + ((me.c, me.s, None),)

    def hand_out(copies, src, dst):
        waits = []
        for core, section, peer in everyone:
            if peer is None:
                waits.append(local.go(src(core, section), dst).wait)
            else:
                copies.append(net.go(src(core, section), dst, peer))
                waits.append(functools.partial(landed, copies[-1:]))
        return waits

    def columns_for(width, core_and_section, base=0):
        return pl.ds(pl.multiple_of(core_and_section * width + base, 128), width)

    attn_dst = r.attn_rows.at[me.s, me.c]
    waits = hand_out(early, lambda c, s: r.attn_flat.at[c, :, columns_for(384, s)], attn_dst.at[:, :384])
    waits += hand_out(early, lambda c, s: r.attn_flat.at[c, :, 768:], attn_dst.at[:, 384:])
    spots = pltpu.roll(r.gains_here[...], me.ctx * 48, 1)
    for which in range(2):
        for i in range(12):
            r.tiny_f32[12 * which + i : 12 * which + i + 1] = spots[which : which + 1, i * 128 : (i + 1) * 128]
    r.tiny_f32[24:] = pltpu.roll(r.bias_here[...], me.ctx * 4, 1)
    r.tiny[...] = r.tiny_f32[...].astype(BF)
    waits += hand_out(early, lambda c, s: r.tiny, r.tiny_quad.at[me.s, me.c])
    away = pl.ds(pl.multiple_of((1 - me.s) * OWN, OWN), OWN)
    home = pl.ds(pl.multiple_of(me.s * OWN, OWN), OWN)
    tokens_over = net.go(r.ends.at[me.h, away], r.tokens.at[me.s], dict(section=1 - me.s))
    tokens_here = local.go(r.ends.at[me.h, home], r.tokens.at[me.s])
    for part, columns in enumerate((GATE, UP, DOWN)):
        src = r.down_flat if part == 2 else r.gate_up_flat.at[part]
        arrivals.append(
            hand_out(
                late, lambda c, s: src.at[:, columns_for(UNITS, 2 * s + c)], r.mlp_rows.at[me.s, me.c, :, columns]
            )
        )

    beside = Beside(FORWARD_LAGS, FORWARD_TURNS)
    saved, done, swaps = [], [], [None, None]
    attn_jobs, mlp_jobs = [None, None], [[], []]

    def save(l, *names):
        for name in names:
            saved.append(local.go(getattr(r, name + str(l)), getattr(r, "out_" + name + str(l))))

    def add_attn(l):
        own = getattr(r, f"wf{l}").at[me.c]

        def swap():
            swaps[l] = net.go(own, own, me.cp())

        attn_jobs[l] = beside.add(Gather(me, net, local, r.attn_rows.at[l], own, (), swap))

    def add_mlp(l, columns):
        buf, out = (getattr(r, f"{name}{l}").at[:, :, :, :, columns] for name in ("wm", "out_wm"))
        ready = arrivals[columns.start // UNITS] if l == 0 else ()
        job = Gather(
            me, net, local, r.mlp_rows.at[l, :, :, columns], buf, ready, lambda: saved.append(local.go(buf, out))
        )
        mlp_jobs[l].append((columns, beside.add(job)))

    for wait in waits:
        wait()
    r.tiny_mine[...] = (r.tiny_quad[:, 0].astype(F32) + r.tiny_quad[:, 1].astype(F32)).astype(BF)
    one = [net.go(r.tiny_mine, r.tiny_x.at[k - 1], me.xp(k)) for k in ORDER]
    for l in range(2):
        add_attn(l)
        for columns in (GATE, UP, DOWN):
            add_mlp(l, columns)
    beside.step()
    landed(one)
    r.tiny_row[...] = (
        r.tiny_mine[...].astype(F32) + r.tiny_x[0].astype(F32) + r.tiny_x[1].astype(F32) + r.tiny_x[2].astype(F32)
    ).astype(BF)
    two = [net.go(r.tiny_row, r.tiny_z.at[k - 1], me.zp(k)) for k in ORDER]
    beside.step()
    landed(two)
    r.small[...] = (
        r.tiny_row[...].astype(F32) + r.tiny_z[0].astype(F32) + r.tiny_z[1].astype(F32) + r.tiny_z[2].astype(F32)
    )

    def gain(l, which):
        return jnp.concatenate([r.small[l, 12 * which + i : 12 * which + i + 1, :] for i in range(12)], axis=1)

    def bias(l):
        rows = [r.small[l, pl.ds(24 + HEADS * me.s + i, 1), :] for i in range(HEADS)]
        rows += [r.small[l, 30 + i : 31 + i, :] for i in range(2)]
        return jnp.concatenate(rows, axis=1)

    for l in range(2):
        for which in range(2):
            r.gains[l, which] = gain(l, which)
    tokens_here.wait()
    landed([tokens_over])
    r.low[me.c, me.y] = r.tokens[1].astype(BF)
    low_rest = []

    for l in range(2):
        kept = types.SimpleNamespace(**{name: getattr(r, name + str(l)) for name in KEPT})
        if l == 0:
            kept.x[...] = r.tokens[0]

        def attn_weights():
            if l == 0:
                low_rest.append(gather_yc(me, net, r.low))
            else:
                beside.step()
            beside.until(attn_jobs[l])
            landed([swaps[l]])
            done.append(swaps[l])

        attn_forward(
            me, net, beside, kept.x, r.gains[l, 0], bias(l), r.turns, kept.wf, attn_weights,
            kept.hid, kept.q, kept.kv, kept.att, getattr(r, f"part{l}"), getattr(r, f"got{l}"), kept.mid,
        )
        if l == 0:
            done += low_rest[0]()
        save(l, "hid", "q", "kv", "att", "wf", "x", "mid")
        weights = lambda *wanted: beside.until(*[job for columns, job in mlp_jobs[l] if columns in wanted])
        mlp_product(
            me, net, beside, kept.mid, r.gains[l, 1], kept.wm, weights, kept.hid2, kept.gate, kept.up, kept.prod
        )
        save(l, "hid2", "gate", "up", "prod")
        beside.step()
        if l == 0:
            weights(DOWN)
            scatter = mlp_down(me, net, kept.wm, kept.prod, r.wide0, r.mate0, r.got20)
            beside.step()
            scatter.middle()
            beside.step()
            r.x1[...] = (kept.mid[...] + scatter.end()).astype(BF).astype(F32)
    beside.rest()
    for copy in saved:
        copy.wait()
    net.left(early + late + [tokens_over] + one + two + done)


def forward(attn_flat, gate_up_flat, down_flat, gains_here, bias_here, ends, turns):
    ins = dict(
        attn_flat=(attn_flat, False), gate_up_flat=(gate_up_flat, False), down_flat=(down_flat, False),
        gains_here=(gains_here, True), bias_here=(bias_here, True), ends=(ends, False), turns=(turns, True),
    )
    outs = {f"out_{name}{l}": (*KEPT[name], False) for l in range(2) for name in KEPT}
    outs["gains"] = ((2, 2, 1, D), F32, True)
    outs["low"] = ((2, 4, OWN, D), BF, True)
    outs["tokens"] = ((2, OWN, D), F32, True)
    scratch = {f"{name}{l}": vmem(KEPT[name]) for l in range(2) for name in KEPT}
    scratch |= dict(
        attn_rows=pltpu.VMEM((2, 2, ROWS, QKW), BF),
        mlp_rows=pltpu.VMEM((2, 2, ROWS, 3 * UNITS), BF),
        tiny_f32=pltpu.VMEM((32, 128), F32),
        tiny=pltpu.VMEM((32, 128), BF),
        tiny_quad=pltpu.VMEM((2, 2, 32, 128), BF),
        tiny_mine=pltpu.VMEM((2, 32, 128), BF),
        tiny_x=pltpu.VMEM((3, 2, 32, 128), BF),
        tiny_row=pltpu.VMEM((2, 32, 128), BF),
        tiny_z=pltpu.VMEM((3, 2, 32, 128), BF),
        small=pltpu.VMEM((2, 32, 128), F32),
        acc=pltpu.VMEM((256, D), F32),
    )
    for l in range(2):
        scratch["part" + str(l)] = pltpu.VMEM((4, OWN, D), BF)
        scratch["got" + str(l)] = pltpu.VMEM((3, OWN, D), BF)
    scratch |= dict(
        wide0=pltpu.VMEM((2, 4, OWN, D), BF), mate0=pltpu.VMEM((4, OWN, D), BF), got20=pltpu.VMEM((3, OWN, D), BF)
    )
    return call(forward_kernel, "forward", 0, ins, outs, scratch | sems(48, 200, 413 + 3))


def attn_backward(me, net, beside, r, gm, load_weights, asides, early_done):
    wf, dws = r.wm.at[:, :, :, :, : 2 * QKW], r.wm.at[:, :, :, :, UNITS : UNITS + 2 * QKW]
    r.low2[me.y] = gm.astype(BF)
    own = r.low2.at[me.y]
    gathered = [net.go(own, own, me.yp(k)) for k in ORDER]
    beside.step()
    cos, sin = twice(r.turns[0]), twice(r.turns[1])
    load_weights()
    landed(gathered)
    grad_mid = r.low2[...].reshape(2 * TOK, D)
    grad_att = dot(grad_mid, whole(wf, slice(512, 896))).astype(BF)
    for m in range(2):
        rows = slice(m * TOK, (m + 1) * TOK)
        queries = r.q[m].reshape(HEADS * TOK, HD)
        keys = r.kv[:, m, :, :, :, :HD].reshape(2048, HD)
        values = r.kv[:, m, :, :, :, HD:].reshape(2048, HD)
        grad_out = jnp.concatenate([grad_att[rows, h * HD : (h + 1) * HD] for h in range(HEADS)], axis=0)
        scores = masked(dot(queries, keys, 1, 1), me.ctx)
        weight = jnp.exp(scores - jnp.max(scores, axis=1, keepdims=True))
        soft = weight / jnp.sum(weight, axis=1, keepdims=True)
        grad_soft = dot(grad_out, values, 1, 1)
        delta = jnp.sum(soft * grad_soft, axis=1, keepdims=True)
        grad_scores = (soft * (grad_soft - delta)).astype(BF)
        grad_values = dot(soft.astype(BF), grad_out, 0, 0)
        grad_keys = dot(grad_scores, queries, 0, 0) * (HD**-0.5)
        r.dkv[:, m] = jnp.concatenate([grad_keys, grad_values], axis=1).astype(BF).reshape(2, 4, 4, TOK, 2 * HD)
        dq = dot(grad_scores, keys) * (HD**-0.5)
        for h in range(HEADS):
            r.dqs[rows, h * HD : (h + 1) * HD] = dq[h * TOK : (h + 1) * TOK]
        beside.step()
    swap = net.go(r.dkv.at[1 - me.c], r.kmate, me.cp())
    dq_low = jnp.concatenate(
        [turned_back(r.dqs[:, h * HD : (h + 1) * HD], cos, sin).astype(BF) for h in range(HEADS)], axis=1
    )
    hidden = r.hid[...].reshape(2 * TOK, D)
    landed([swap])
    kmate, kz, kx, k2, k3 = r.kmate, r.kz, r.kx, r.k2, r.k3
    kmate[...] = (kmate[...].astype(F32) + r.dkv[me.c].astype(F32)).astype(BF)
    first0 = [net.go(kmate.at[0, (me.z + k) % 4], kz.at[k - 1], me.zp(k)) for k in ORDER]
    first1 = [net.go(kmate.at[1, :, (me.x + k) % 4], kx.at[k - 1], me.xp(k)) for k in ORDER]

    def blocks(value):
        return value.astype(BF).reshape(4, 4, 2, ROWS, -1)

    dws[:, :, :, :, :384] = blocks(dot(hidden, dq_low, 0, 0))
    dws[:, :, :, :, 512:896] = blocks(dot(grad_mid, r.att[...], 0, 0))
    dws[:, :, :, :, 896:1024] = jnp.zeros((4, 4, 2, ROWS, HD), BF)

    def half(core, base=0, width=384):
        return pl.ds(pl.multiple_of(core * QKW + base, 128), width)

    early_swap = net.go(dws.at[:, :, :, :, half(1 - me.c)], r.da, me.cp())
    asides[0]()
    beside.step()
    landed(first0)
    total0 = kmate[0, me.z].astype(F32)
    for k in range(3):
        total0 = total0 + kz[k].astype(F32)
    k2[0] = total0.astype(BF)
    second0 = [net.go(k2.at[0, (me.x + k) % 4], k3.at[0, k - 1], me.xp(k)) for k in ORDER]
    landed(first1)
    total1 = kmate[1, :, me.x].astype(F32)
    for k in range(3):
        total1 = total1 + kx[k].astype(F32)
    k2[1] = total1.astype(BF)
    second1 = [net.go(k2.at[1, (me.z + k) % 4], k3.at[1, k - 1], me.zp(k)) for k in ORDER]
    landed([early_swap])

    def add_early(j, _):
        r.da[j] = (dws[j, :, :, :, half(me.c)].astype(F32) + r.da[j].astype(F32)).astype(BF)
        return 0

    lax.fori_loop(0, 4, add_early, 0)
    early_done()
    asides[1]()
    beside.step()
    landed(second0 + second1)
    for m, place in ((0, me.x), (1, me.z)):
        total = k2[m, place].astype(F32)
        for k in range(3):
            total = total + k3[m, k].astype(F32)
        r.kpair[0, m * TOK : (m + 1) * TOK] = total[:, :HD].astype(BF)
        r.kpair[1, m * TOK : (m + 1) * TOK] = total[:, HD:].astype(BF)
    pair = net.go(r.kpair.at[1 - me.s], r.kpair_got, dict(section=1 - me.s))
    landed([pair])
    total = r.kpair[me.s].astype(F32) + r.kpair_got[...].astype(F32)
    dk_low = jnp.where(me.s == 0, turned_back(total, cos, sin), total).astype(BF)
    w_own = jnp.where(me.s == 0, whole(wf, slice(384, 512)), whole(wf, slice(896, 1024)))
    r.part[...] = (
        (dot(dq_low, whole(wf, slice(0, 384)), 1, 1) + dot(dk_low, w_own, 1, 1)).astype(BF).reshape(4, OWN, D)
    )
    back = [net.go(r.part.at[(me.y + k) % 4], r.got.at[k - 1], me.yp(k)) for k in ORDER]
    dws[:, :, :, :, 384:512] = blocks(dot(hidden, dk_low, 0, 0))

    late_swap = net.go(dws.at[:, :, :, :, half(1 - me.c, 384, HD)], r.dakv, me.cp())
    asides[2]()
    beside.step()
    gbias = jnp.concatenate(
        [jnp.sum(dq_low.astype(F32), axis=0, keepdims=True), jnp.sum(dk_low.astype(F32), axis=0, keepdims=True)], axis=1
    )
    dy = r.part[me.y].astype(F32)
    landed(back)
    for k in range(3):
        dy = dy + r.got[k].astype(F32)
    dx, ggain = norm_back(r.x[...], r.gains[r.layer, 0], dy)
    r.gin[...] = gm + dx
    landed([late_swap])
    r.dakv[...] = (dws[:, :, :, :, half(me.c, 384, HD)].astype(F32) + r.dakv[...].astype(F32)).astype(BF)
    net.left(gathered + [swap] + first0 + first1 + second0 + second1 + [pair] + back + [early_swap, late_swap])
    return ggain, gbias


def mlp_backward(me, net, beside, r, g, loaded, scatter):
    loaded("prod")

    def weight_grad(base, left_ref, right_ref):
        def step(i, _):
            r.dm[:, :, :, :, columns_of(i, base)] = (
                dot(left_ref[...].reshape(256, D), right_ref[:, columns_of(i)], 0, 0)
                .astype(BF)
                .reshape(4, 4, 2, ROWS, CHUNK)
            )
            return 0

        lax.fori_loop(0, UNITS // CHUNK, step, 0)

    weight_grad(2 * UNITS, r.low, r.prod)
    scatter(DOWN)
    beside.step()
    loaded("gate", "up", "wm", "hid2")
    r.acc[...] = jnp.zeros_like(r.acc)

    def step(i, _):
        cols = columns_of(i)
        dprod = dot(r.low[...].reshape(256, D), whole(r.wm, columns_of(i, 2 * UNITS)))
        gate, up = r.gate[:, cols], r.up[:, cols]
        sigma = jax.nn.sigmoid(gate)
        dg = (dprod * up * sigma * (1.0 + gate * (1.0 - sigma))).astype(BF)
        du = (dprod * gate * sigma).astype(BF)
        r.dgate[:, cols] = dg
        r.dup[:, cols] = du
        r.acc[...] += dot(dg, whole(r.wm, cols), 1, 1) + dot(du, whole(r.wm, columns_of(i, UNITS)), 1, 1)
        return 0

    lax.fori_loop(0, UNITS // CHUNK, step, 0)
    r.wide[...] = r.acc[...].astype(BF).reshape(2, 4, OWN, D)
    sums = ScatterYC(me, net, r.wide, r.mate, r.got2)
    beside.step()
    weight_grad(0, r.hid2, r.dgate)
    sums.middle()
    scatter(GATE)
    beside.step()
    weight_grad(UNITS, r.hid2, r.dup)
    scatter(UP)
    beside.step()
    dy = sums.end()
    du, ggain = norm_back(r.mid[...], r.gains[r.layer, 1], dy)
    return g + du, ggain


def put_small(r, base, y, ggain0, ggain1, gbias):
    r.sums[0, base + 24 : base + 40] = jnp.zeros((16, 128), F32)
    for which, ggain in enumerate((ggain0, ggain1)):
        for i in range(12):
            r.sums[0, base + 12 * which + i : base + 12 * which + i + 1] = ggain[:, i * 128 : (i + 1) * 128]
    for i in range(4):
        r.sums[0, pl.ds(base + 24 + 4 * y + i, 1)] = gbias[:, i * 128 : (i + 1) * 128]


def backward_kernel(last, r):
    me = Place()
    local = Local(r.lsem)
    names = ("prod", "low", "gate", "up", "wm", "hid2", "mid", "hid", "q", "kv", "att", "x")
    pending = {}

    def load(name):
        pending[name] = local.go(getattr(r, "in_" + name), getattr(r, name))

    def loaded(*wanted):
        for name in wanted:
            pending.pop(name).wait()

    for name in names:
        if not (last and name == "low"):
            load(name)
    me.greet(last)
    net = Links(r.send, r.recv)
    beside = Beside(LOWER_LAGS, LOWER_TURNS) if last else Beside(UPPER_LAGS, UPPER_TURNS)
    extra = []

    def job_refs(columns):
        return tuple(getattr(r, "m" + str(columns.start) + name) for name in ("_r1", "_r2", "_u1", "_u2"))

    r.layer = 0 if last else 1
    g = r.g[...] if last else r.tokens[1]
    if last:
        g = g.astype(BF).astype(F32)
        r.low[me.c, me.y] = g.astype(BF)
        rest = gather_yc(me, net, r.low)
        res = [local.go(r.in_sums1, r.res_m.at[1])]
        da1 = local.go(r.in_da1, r.da1)
        crossed = []

        def go_home(src, dst):
            for core, section, peer in me.quad():
                crossed.append(net.go(src.at[section, core], dst, peer))
            extra.append(local.go(src.at[me.s, me.c], dst))

        def place_of(width, index):
            return pl.ds(pl.multiple_of(index * width, 128), width)

        def attn_home():
            go_home(r.res_a.at[:, :, :, :384], r.attn_home.at[me.c, :, place_of(384, me.s)])
            go_home(r.res_a.at[:, :, :, 384:], r.kv_home.at[me.c, :, place_of(HD, me.s)])

        da1.wait()
        beside.add(Scatter(me, net, r.da1, (r.a1_r1, r.a1_r2, r.a1_u1, r.a1_u2), r.res_a.at[1]))
        beside.step()

    def scatter(columns):
        dw = r.dm.at[:, :, :, :, columns]
        if last:
            dst = r.down_home if columns == DOWN else r.gate_up_home.at[columns.start // UNITS]
            dst = dst.at[:, place_of(UNITS, 2 * me.s + me.c)]
            then = functools.partial(go_home, r.res_m.at[:, :, :, columns], dst)
            beside.add(Scatter(me, net, dw, job_refs(columns), r.res_m.at[0, :, :, columns], then))
        else:
            beside.add(Scatter(me, net, dw, job_refs(columns), r.sums1.at[:, :, columns]))

    if last:
        low_copies = rest()
        for copy in res:
            copy.wait()
    loaded("mid", *(() if last else ("low",)))
    gm, ggain1 = mlp_backward(me, net, beside, r, g, loaded, scatter)

    wf_copies = [
        local.go(r.in_wf.at[0], r.wm.at[:, :, :, :, :QKW]), local.go(r.in_wf.at[1], r.wm.at[:, :, :, :, QKW : 2 * QKW])
    ]

    def load_weights():
        for copy in wf_copies:
            copy.wait()
        loaded("hid", "q", "kv", "att", "x")

    nothing = lambda: None
    if not last:
        down = []
        asides = (
            lambda: down.append(mlp_down(me, net, r.wm, r.prod, r.wide2, r.mate2, r.got3)),
            lambda: down[0].middle(),
            lambda: down.append(down[0].end()),
        )
        ggain0, gbias = attn_backward(me, net, beside, r, gm, load_weights, asides, nothing)
        r.out1[...] = r.mid[...] + down[1]
        put_small(r, 0, me.y, ggain0, ggain1, gbias)
        r.small1[...] = r.sums[0]
        extra.append(local.go(r.da, r.out_da.at[:, :, :, :, :384]))
        extra.append(local.go(r.dakv, r.out_da.at[:, :, :, :, 384:]))
        beside.rest()
        for copy in extra:
            copy.wait()
        return

    def attn_job():
        job = (r.a0_r1, r.a0_r2, r.a0_u1, r.a0_u2)
        beside.add(Scatter(me, net, r.da, job, r.res_a.at[0, :, :, :384]))

    ggain0, gbias = attn_backward(me, net, beside, r, gm, load_weights, (nothing,) * 3, attn_job)
    last_scatter = DirectScatter(me, net, r.dakv, r.kv_got, r.res_a.at[0, :, :, 384:])
    beside.step()
    put_small(r, 0, me.y, ggain0, ggain1, gbias)
    r.sums[0, 40:] = r.small1[...]
    rounds = ((me.yp, ORDER, 0), (lambda k: me.cp(), (1,), 3), (me.xp, ORDER, 4), (me.zp, ORDER, 7))
    small = []
    for turn, (peer, ks, slot) in enumerate(rounds):
        sent = [net.go(r.sums.at[turn], r.sums_got.at[slot + k - 1], peer(k)) for k in ks]
        if turn == 0:
            r.ends2[0] = r.gin[...].astype(BF)
            r.ends2[1] = r.out1[...].astype(BF)
            edges = [net.go(r.ends2.at[((me.y + k) % 4) % 2], r.ends_got.at[k - 1], me.yp(k)) for k in ORDER]
        if turn == 2:
            last_scatter.finish()
            beside.rest()
            attn_home()
        landed(sent)
        total = r.sums[turn]
        for k in ks:
            total = total + r.sums_got[slot + k - 1]
        r.sums[turn + 1] = total
        small.extend(sent)
    total = r.sums.at[4]
    spots = [r.sums[4, pl.ds(40 * me.s + i, 1)] for i in range(24)]
    spots = jnp.concatenate(
        [jnp.concatenate(spots[12 * which : 12 * which + 12], axis=1) for which in range(2)]
        + [jnp.zeros((6, D), F32)],
        axis=0,
    )
    r.gain_home[...] = pltpu.roll(spots, ((32 - me.ctx) % 32) * 48, 1)[:, :128]
    rows = [total[pl.ds(40 * me.s + 24 + 8 * me.h + i, 1)] for i in range(8)]
    r.bias_home[...] = pltpu.roll(jnp.concatenate(rows, axis=0), ((32 - me.ctx) % 32) * 4, 1)
    r.boundary[me.y] = jnp.where(me.s == 0, r.gin[...], r.out1[...])
    landed(edges)
    for k in ORDER:
        r.boundary[(me.y + 4 - k) % 4] = r.ends_got[k - 1].astype(F32)
    beside.rest()
    landed(crossed)
    for copy in extra:
        copy.wait()
    net.left(low_copies + crossed + edges + small)


def backward(last, kept, gains, turns, more):
    ins = {"in_" + name: (kept[name], False) for name in KEPT}
    ins |= dict(gains=(gains, True), turns=(turns, True))
    if last:
        ins["g"] = (more["gin"], True)
        ins |= dict(
            in_sums1=(more["sums1"], False), out1=(more["out1"], True), in_da1=(more["out_da"], False),
            small1=(more["small1"], True),
        )
        outs = dict(
            gate_up_home=((2, ROWS, 4 * UNITS), BF, False),
            down_home=((ROWS, 4 * UNITS), BF, False),
            attn_home=((2, ROWS, 768), BF, False),
            kv_home=((2, ROWS, 2 * HD), BF, False),
            boundary=((4, OWN, D), F32, True),
            gain_home=((8, 128), F32, True),
            bias_home=((8, 128), F32, True),
        )
    else:
        ins |= dict(in_low=(more["low"], False), tokens=(more["tokens"], True))
        outs = dict(
            sums1=((2, ROWS, 3 * UNITS), BF, True),
            out1=((OWN, D), F32, True),
            out_da=((4, 4, 2, ROWS, QKW), BF, False),
            small1=((40, 128), F32, True),
            gin=((OWN, D), F32, True),
        )
    scratch = {name: vmem(KEPT[name]) for name in KEPT if name != "wf"}
    scratch |= dict(
        low=pltpu.VMEM((2, 4, OWN, D), BF),
        dgate=pltpu.VMEM((256, UNITS), BF),
        dup=pltpu.VMEM((256, UNITS), BF),
        acc=pltpu.VMEM((256, D), F32),
        wide=pltpu.VMEM((2, 4, OWN, D), BF),
        mate=pltpu.VMEM((4, OWN, D), BF),
        got2=pltpu.VMEM((3, OWN, D), BF),
        dm=pltpu.VMEM((4, 4, 2, ROWS, 3 * UNITS), BF),
        low2=pltpu.VMEM((4, OWN, D), BF),
        dkv=pltpu.VMEM((2, 2, 4, 4, TOK, 2 * HD), BF),
        kmate=pltpu.VMEM((2, 4, 4, TOK, 2 * HD), BF),
        kz=pltpu.VMEM((3, 4, TOK, 2 * HD), BF),
        kx=pltpu.VMEM((3, 4, TOK, 2 * HD), BF),
        k2=pltpu.VMEM((2, 4, TOK, 2 * HD), BF),
        k3=pltpu.VMEM((2, 3, TOK, 2 * HD), BF),
        kpair=pltpu.VMEM((2, 2 * TOK, HD), BF),
        kpair_got=pltpu.VMEM((2 * TOK, HD), BF),
        dqs=pltpu.VMEM((2 * TOK, HEADS * HD), F32),
        da=pltpu.VMEM((4, 4, 2, ROWS, 384), BF),
        dakv=pltpu.VMEM((4, 4, 2, ROWS, HD), BF),
        part=pltpu.VMEM((4, OWN, D), BF),
        got=pltpu.VMEM((3, OWN, D), BF),
        sums=pltpu.VMEM((5, 80, 128) if last else (1, 40, 128), F32),
    )
    jobs = {"m" + str(columns.start): UNITS for columns in (GATE, UP, DOWN)}
    if last:
        jobs |= dict(a0=384, a1=QKW)
        scratch |= dict(
            gin=pltpu.VMEM((OWN, D), F32),
            da1=pltpu.VMEM((4, 4, 2, ROWS, QKW), BF),
            res_m=pltpu.VMEM((2, 2, ROWS, 3 * UNITS), BF),
            res_a=pltpu.VMEM((2, 2, ROWS, QKW), BF),
            kv_got=pltpu.VMEM((15, 2, ROWS, HD), BF),
            ends2=pltpu.VMEM((2, OWN, D), BF),
            ends_got=pltpu.VMEM((3, OWN, D), BF),
            sums_got=pltpu.VMEM((10, 80, 128), F32),
        )
    if not last:
        scratch |= dict(
            wide2=pltpu.VMEM((2, 4, OWN, D), BF), mate2=pltpu.VMEM((4, OWN, D), BF), got3=pltpu.VMEM((3, OWN, D), BF)
        )
    for job, columns in jobs.items():
        for name, ref in zip(("r1", "r2", "u1", "u2"), Scatter.scratch(columns)):
            scratch[f"{job}_{name}"] = ref
    return call(
        functools.partial(backward_kernel, last), "backward", 1 + last, ins, outs,
        scratch | (sems(32, 160, 200) if last else sems(32, 80, 84)),
    )


def body(ends, w_query, w_kv, w_out, w_gate_up, w_down, gains, bias_query, bias_kv):
    me = Place()
    kv = w_kv[0].transpose(1, 0, 2)
    attn_flat = jnp.concatenate([jnp.stack([w_query[0], w_out[0]]), kv], axis=2)
    missing = 4 * UNITS - w_down.shape[2]
    gate_up_flat = jnp.pad(w_gate_up[0].transpose(1, 0, 2), ((0, 0), (0, 0), (0, missing)))
    down_flat = jnp.pad(w_down[0], ((0, 0), (0, missing)))
    gains_here = jnp.pad(gains[0].astype(F32), ((0, 6), (0, D - 48)))
    bias_here = jnp.concatenate([bias_query[0], bias_kv[0].reshape(2, 4)], axis=0).astype(F32)
    bias_here = jnp.pad(bias_here, ((0, 0), (0, 124)))
    lane = jnp.arange(HD, dtype=jnp.int32)
    inverse = 1.0 / THETA ** ((lane % 64).astype(F32) * (2.0 / HD))
    positions = (me.ctx * TOK + jnp.arange(TOK, dtype=jnp.int32)).astype(F32)
    angles = positions[:, None] * inverse[None, :]
    turns = jnp.stack([jnp.cos(angles), jnp.where(lane < 64, -1.0, 1.0) * jnp.sin(angles)])

    ahead = forward(attn_flat, gate_up_flat, down_flat, gains_here, bias_here, ends[0], turns)
    kept = [{name: ahead[f"out_{name}{l}"] for name in KEPT} for l in range(2)]
    upper = backward(False, kept[1], ahead["gains"], turns, ahead)
    done = backward(True, kept[0], ahead["gains"], turns, upper)

    units = w_down.shape[2]
    bias = done["bias_home"][:, :4].reshape(2, 4, 4)
    return (
        done["boundary"].reshape(1, 2, TOK, D),
        done["attn_home"][0].astype(F32)[None],
        done["kv_home"][0].astype(F32).reshape(1, ROWS, 2, HD),
        done["attn_home"][1].astype(F32)[None],
        done["gate_up_home"][:, :, :units].astype(F32).transpose(1, 0, 2)[None],
        done["down_home"][:, :units].astype(F32)[None],
        done["gain_home"][:2, :48][None],
        bias[:, :HEADS].reshape(1, 6, 4),
        bias[:, HEADS].reshape(1, 2, 1, 4),
    )


def solution(mesh):
    placed = (
        P("section", None, "ctx", None),
        P("section", "ctx", "shard"),
        P("section", "ctx", None, "shard"),
        P("section", "ctx", "shard"),
        P("section", "ctx", None, "shard"),
        P("section", "ctx", "shard"),
        P("section", None, "ctx"),
        P("section", "shard", "ctx"),
        P("section", None, "shard", "ctx"),
    )
    return jax.shard_map(
        body,
        mesh=mesh,
        in_specs=placed,
        out_specs=(
            P("section", None, "ctx", None),
            P("section", "ctx", "shard"),
            P("section", "ctx", None, "shard"),
            P("section", "ctx", "shard"),
            P("section", "ctx", None, "shard"),
            P("section", "ctx", "shard"),
            P("section", None, "ctx"),
            P("section", "shard", "ctx"),
            P("section", None, "shard", "ctx"),
        ),
        check_vma=False,
    )
```

```python
import functools
import types

import jax
import jax.numpy as jnp
from jax import lax
from jax.experimental import pallas as pl
from jax.experimental.pallas import tpu as pltpu
from jax.sharding import PartitionSpec as P

MESH = pl.DeviceIdType.MESH
BF = jnp.bfloat16
F32 = jnp.float32
EPS = 1e-06
THETA = 1000000.0
D = 1536
HD = 128
HEADS = 3
UNITS = 1152
CHUNK = 384
TOK = 64
OWN = 32
ROWS = 48
QKW = 512
ORDER = (1, 3, 2)
SIDES = (1, 3)
OTHERS = tuple((dz, dx) for dz in range(4) for dx in range(4) if (dz, dx) != (0, 0))


class Place:
    def __init__(self):
        self.ctx = lax.axis_index("ctx")
        self.s = lax.axis_index("section")
        self.h = lax.axis_index("shard")
        self.z = self.ctx // 8
        self.x = (self.ctx // 2) % 4
        self.c = self.ctx % 2
        self.y = self.h * 2 + self.s

    def yp(self, k):
        other = (self.y + k) % 4
        return dict(section=other % 2, shard=other // 2)

    def xp(self, k):
        return dict(ctx=self.z * 8 + ((self.x + k) % 4) * 2 + self.c)

    def zp(self, k):
        return dict(ctx=(self.ctx + 8 * k) % 32)

    def cp(self):
        return dict(ctx=self.ctx + 1 - 2 * self.c)

    def quad(self):
        return (
            (self.c, 1 - self.s, dict(section=1 - self.s)),
            (1 - self.c, self.s, self.cp()),
            (1 - self.c, 1 - self.s, dict(section=1 - self.s, ctx=self.ctx + 1 - 2 * self.c)),
        )

    def chip(self, dz, dx):
        return dict(ctx=((self.z + dz) % 4) * 8 + ((self.x + dx) % 4) * 2 + self.c)

    def greet(self, far=False):
        peers = [self.yp(k) for k in ORDER] + [self.cp(), self.quad()[2][2]]
        peers += [self.xp(k) for k in ORDER] + [self.zp(k) for k in ORDER]
        if far:
            peers += [self.chip(dz, dx) for dz, dx in OTHERS if dz and dx]
        barrier = pltpu.get_barrier_semaphore()
        for peer in peers:
            pl.semaphore_signal(barrier, 1, device_id=peer, device_id_type=MESH)
        pl.semaphore_wait(barrier, len(peers))


class Links:
    def __init__(self, send, recv):
        self.send, self.recv, self.count = send, recv, 0
        self.free = list(range(send.shape[0]))

    def go(self, src, dst, peer):
        index = self.count
        self.count += 1
        slot = self.free.pop(0)
        copy = pltpu.make_async_remote_copy(
            src, dst, self.send.at[slot], self.recv.at[index], device_id=peer, device_id_type=MESH
        )
        copy.start()
        return copy, slot

    def left(self, copies):
        for copy, slot in copies:
            copy.wait_send()
            self.free.append(slot)


def landed(copies):
    for copy, _ in copies:
        copy.wait_recv()


class Local:
    def __init__(self, sems):
        self.sems, self.count = sems, 0

    def go(self, src, dst):
        copy = pltpu.make_async_copy(src, dst, self.sems.at[self.count])
        self.count += 1
        copy.start()
        return copy


def cuts(columns, flip):
    cut = (columns // 256) * 128
    both = (slice(0, cut), slice(cut, columns))
    return both[::-1] if flip else both


class Gather:
    copies = 40

    def __init__(self, me, net, local, src, buf, ready=(), then=None, flip=False):
        self.me, self.net, self.local, self.src, self.buf, self.ready = me, net, local, src, buf, ready
        self.then = then
        self.cuts = cuts(src.shape[-1], flip)
        self.sent = []

    def steps(self):
        by_half = [functools.partial(f, half) for f in (self.second, self.third, self.fourth) for half in range(2)]
        return [self.start, *by_half, self.finish]

    def at(self, half, p, q):
        return self.buf.at[q, p, 0] if half == 0 else self.buf.at[p, q, 1]

    def axes(self, half):
        me = self.me
        return (me.x, me.z, me.xp, me.zp) if half == 0 else (me.z, me.x, me.zp, me.xp)

    def go(self, src, dst, peer):
        copy = self.net.go(src, dst, peer)
        self.sent.append(copy)
        return copy

    def start(self):
        me = self.me
        for wait in self.ready:
            wait()
        self.own = self.local.go(self.src, self.buf.at[me.z, me.x])
        self.a, self.c = [None, None], [[None] * 4, [None] * 4]
        self.f, self.last = [[], []], []
        for half in range(2):
            p, q, pp, qp = self.axes(half)
            self.a[half] = [self.go(self.src.at[half], self.at(half, p, q), pp(k)) for k in SIDES]
        for half in range(2):
            p, q, pp, qp = self.axes(half)
            self.c[half][0] = [self.go(self.src.at[half], self.at(half, p, q), qp(k)) for k in SIDES]

    def second(self, half):
        p, q, pp, qp = self.axes(half)
        for i, k in enumerate(SIDES):
            landed([self.a[half][i]])
            piece = self.at(half, (p + 4 - k) % 4, q).at[:, self.cuts[i]]
            self.f[half].append(self.go(piece, piece, pp(k)))
        for i, k in enumerate(SIDES):
            block = self.at(half, (p + 4 - k) % 4, q)
            self.c[half][i + 1] = [self.go(block, block, qp(kk)) for kk in SIDES]

    def third(self, half):
        p, q, pp, qp = self.axes(half)
        landed(self.f[half])
        block = self.at(half, (p + 2) % 4, q)
        self.c[half][3] = [self.go(block, block, qp(kk)) for kk in SIDES]
        self.onward(half, (0,))

    def fourth(self, half):
        self.onward(half, (1, 2, 3))

    def onward(self, half, turns):
        p, q, pp, qp = self.axes(half)
        for j in turns:
            shift = (0, 3, 1, 2)[j]
            for i, k in enumerate(SIDES):
                landed([self.c[half][j][i]])
                piece = self.at(half, (p + shift) % 4, (q + 4 - k) % 4).at[:, self.cuts[i]]
                self.last.append(self.go(piece, piece, qp(k)))

    def finish(self):
        landed(self.last)
        self.own.wait()
        self.net.left(self.sent)
        if self.then is not None:
            self.then()


class Scatter:
    copies = 16

    def __init__(self, me, net, part, scratch, out, then=None, flip=False):
        self.me, self.net, self.part, self.out, self.then = me, net, part, out, then
        self.r1, self.r2, self.u1, self.u2 = scratch
        self.cuts = cuts(part.shape[-1], flip)
        self.sent = []

    def steps(self):
        by_half = [functools.partial(f, half) for f in (self.second, self.third, self.fourth) for half in range(2)]
        return [self.start, *by_half, self.finish]

    @staticmethod
    def shapes(columns):
        wide = columns - (columns // 256) * 128
        return ((2, 2, 4, ROWS, wide), (2, 2, 4, ROWS, columns), (2, 2, ROWS, wide), (2, 2, ROWS, columns))

    def group(self, half, q):
        return self.part.at[q, :, 0] if half == 0 else self.part.at[:, q, 1]

    def axes(self, half):
        me = self.me
        return (me.x, me.z, me.xp, me.zp) if half == 0 else (me.z, me.x, me.zp, me.xp)

    def go(self, src, dst, peer):
        copy = self.net.go(src, dst, peer)
        self.sent.append(copy)
        return copy

    def wide(self, i):
        return slice(0, self.cuts[i].stop - self.cuts[i].start)

    def start(self):
        self.one, self.two, self.three, self.four = ([[], []] for _ in range(4))
        for half in range(2):
            p, q, pp, qp = self.axes(half)
            for i, k in enumerate(SIDES):
                piece = self.group(half, (q + 2) % 4).at[:, :, self.cuts[i]]
                self.one[half].append(self.go(piece, self.r1.at[half, i, :, :, self.wide(i)], qp(k)))

    def second(self, half):
        p, q, pp, qp = self.axes(half)
        for i, k in enumerate(SIDES):
            landed([self.one[half][i]])
            mine = self.group(half, (q + k) % 4)

            def add(j, _):
                mine[j, :, self.cuts[i]] = (
                    mine[j, :, self.cuts[i]].astype(F32) + self.r1[half, i, j, :, self.wide(i)].astype(F32)
                ).astype(BF)
                return 0

            lax.fori_loop(0, 4, add, 0)
            self.two[half].append(self.go(mine, self.r2.at[half, i], qp(k)))

    def third(self, half):
        p, q, pp, qp = self.axes(half)
        landed(self.two[half])
        mine = self.group(half, q)

        def add(j, _):
            mine[j] = (
                mine[j].astype(F32) + self.r2[half, 0, j].astype(F32) + self.r2[half, 1, j].astype(F32)
            ).astype(BF)
            return 0

        lax.fori_loop(0, 4, add, 0)
        for i, k in enumerate(SIDES):
            self.three[half].append(
                self.go(mine.at[(p + 2) % 4, :, self.cuts[i]], self.u1.at[half, i, :, self.wide(i)], pp(k))
            )

    def fourth(self, half):
        p, q, pp, qp = self.axes(half)
        for i, k in enumerate(SIDES):
            landed([self.three[half][i]])
            block = self.group(half, q).at[(p + k) % 4]
            block[:, self.cuts[i]] = (
                block[:, self.cuts[i]].astype(F32) + self.u1[half, i, :, self.wide(i)].astype(F32)
            ).astype(BF)
            self.four[half].append(self.go(block, self.u2.at[half, i], pp(k)))

    def finish(self):
        for half in range(2):
            p, q, pp, qp = self.axes(half)
            landed(self.four[half])
            self.out[half] = (
                self.group(half, q)[p].astype(F32) + self.u2[half, 0].astype(F32) + self.u2[half, 1].astype(F32)
            ).astype(BF)
        self.net.left(self.sent)
        if self.then is not None:
            self.then()


class DirectScatter:
    def __init__(self, me, net, part, got, out):
        self.me, self.net, self.part, self.got, self.out = me, net, part, got, out
        self.sent = []
        for i, (dz, dx) in enumerate(OTHERS):
            src = part.at[(me.z + dz) % 4, (me.x + dx) % 4]
            self.sent.append(net.go(src, got.at[i], me.chip(dz, dx)))

    def finish(self):
        total = self.part[self.me.z, self.me.x].astype(F32)
        landed(self.sent)
        for i in range(len(OTHERS)):
            total = total + self.got[i].astype(F32)
        self.out[...] = total.astype(BF)
        self.net.left(self.sent)


class Beside:
    def __init__(self, lags, turns):
        self.lags, self.turns, self.turn, self.jobs = lags, list(turns), 0, []

    def add(self, job):
        first = self.turn
        if self.jobs:
            first = max(first, self.jobs[-1][0] + self.lags[len(self.jobs)])
        self.jobs.append((first, list(job.steps()), job))
        return job

    def step(self):
        for _ in range(self.turns.pop(0) if self.turns else 0):
            self.take()

    def take(self):
        for first, steps, _ in reversed(self.jobs):
            if self.turn >= first and steps:
                steps.pop(0)()
        self.turn += 1

    def until(self, *jobs):
        while any(steps for _, steps, job in self.jobs if job in jobs):
            self.take()

    def rest(self):
        while any(steps for _, steps, _ in self.jobs):
            self.take()


def dot(a, b, ca=1, cb=0):
    return lax.dot_general(a, b, (((ca,), (cb,)), ((), ())), preferred_element_type=F32)


def unit_rms(u):
    scale = lax.rsqrt(jnp.mean(u * u, axis=1, keepdims=True) + EPS)
    return u * scale, scale


def norm_back(u, gain, dy):
    n, scale = unit_rms(u)
    sd = dy * gain
    return scale * (sd - n * jnp.mean(sd * n, axis=1, keepdims=True)), jnp.sum(dy * n, axis=0, keepdims=True)


def turned(u, cos, sin):
    return u * cos + pltpu.roll(u, 64, 1) * sin


def turned_back(w, cos, sin):
    return w * cos - pltpu.roll(w, 64, 1) * sin


def twice(table):
    return jnp.concatenate([table, table], axis=0)


def key_places(rows):
    j = lax.broadcasted_iota(jnp.int32, (rows, 2048), 1)
    core = j // 1024
    chip = (j % 1024) // TOK
    return chip * (2 * TOK) + core * TOK + j % TOK


def masked(raw, ctx):
    rows = raw.shape[0]
    query = ctx * TOK + lax.broadcasted_iota(jnp.int32, (rows, 2048), 0) % TOK
    return jnp.where(key_places(rows) <= query, raw * (HD**-0.5), -1e30)


def columns_of(i, base=0):
    return pl.ds(pl.multiple_of(base + i * CHUNK, CHUNK), CHUNK)


def attn_forward(me, net, beside, x_ref, gain, bias, turns, wf, weights, hid, q, kv, att, part, got, mid):
    x = x_ref[...]
    normed, _ = unit_rms(x)
    hid[me.y] = (normed * gain).astype(BF)
    hid_copies = [net.go(hid.at[me.y], hid.at[me.y], me.yp(k)) for k in ORDER]
    cos, sin = twice(turns[0]), twice(turns[1])
    weights()
    beside.step()
    landed(hid_copies)
    hidden = hid[...].reshape(2 * TOK, D)
    proj = dot(hidden, whole(wf.at[0], slice(0, QKW))) + bias[:, :QKW]
    key = turned(proj[:, 384:], cos, sin).astype(BF)
    value = (dot(hidden, whole(wf.at[1], slice(384, QKW))) + bias[:, QKW:]).astype(BF)
    keyval = jnp.concatenate([key, value], axis=1)
    for m in range(2):
        kv[me.c, m, me.z, me.x] = keyval[m * TOK : (m + 1) * TOK]
    mine0, mine1 = kv.at[me.c, 0, me.z, me.x], kv.at[me.c, 1, me.z, me.x]
    first0 = [net.go(mine0, mine0, me.xp(k)) for k in ORDER]
    first1 = [net.go(mine1, mine1, me.zp(k)) for k in ORDER]
    for head in range(HEADS):
        query = turned(proj[:, head * HD : (head + 1) * HD], cos, sin).astype(BF)
        for m in range(2):
            q[m, head] = query[m * TOK : (m + 1) * TOK]
    beside.step()
    landed(first0)
    second0 = [net.go(kv.at[me.c, 0, me.z], kv.at[me.c, 0, me.z], me.zp(k)) for k in ORDER]
    landed(first1)
    second1 = [net.go(kv.at[me.c, 1, :, me.x], kv.at[me.c, 1, :, me.x], me.xp(k)) for k in ORDER]
    beside.step()
    landed(second0)
    third0 = net.go(kv.at[me.c, 0], kv.at[me.c, 0], me.cp())
    landed(second1)
    third1 = net.go(kv.at[me.c, 1], kv.at[me.c, 1], me.cp())
    for m, third in ((0, third0), (1, third1)):
        beside.step()
        landed([third])
        queries = q[m].reshape(HEADS * TOK, HD)
        keys = kv[:, m, :, :, :, :HD].reshape(2048, HD)
        values = kv[:, m, :, :, :, HD:].reshape(2048, HD)
        scores = masked(dot(queries, keys, 1, 1), me.ctx)
        weight = jnp.exp(scores - jnp.max(scores, axis=1, keepdims=True))
        total = jnp.sum(weight, axis=1, keepdims=True)
        out = (dot(weight.astype(BF), values) / total).astype(BF)
        for head in range(HEADS):
            att[m * TOK : (m + 1) * TOK, head * HD : (head + 1) * HD] = out[head * TOK : (head + 1) * TOK]
    beside.step()
    part[...] = dot(att[...], whole(wf.at[1], slice(0, 384)), 1, 1).astype(BF).reshape(4, OWN, D)
    back = [net.go(part.at[(me.y + k) % 4], got.at[k - 1], me.yp(k)) for k in ORDER]
    beside.step()
    total = x + part[me.y].astype(F32)
    landed(back)
    for k in range(3):
        total = total + got[k].astype(F32)
    mid[...] = total
    net.left(hid_copies + first0 + first1 + second0 + second1 + [third0, third1] + back)


def gather_yc(me, net, buf):
    own = buf.at[me.c, me.y]
    sent = [net.go(own, own, me.yp(k)) for k in ORDER]
    crossed = [net.go(own, own, me.cp())]

    def rest():
        for k, copy in zip(ORDER, sent):
            landed([copy])
            block = buf.at[me.c, (me.y + 4 - k) % 4]
            crossed.append(net.go(block, block, me.cp()))
        landed(crossed)
        return sent + crossed

    return rest


class ScatterYC:
    def __init__(self, me, net, part, mate, got):
        self.me, self.net, self.part, self.mate, self.got = me, net, part, mate, got
        self.swap = net.go(part.at[1 - me.c], mate, me.cp())

    def middle(self):
        me, mate = self.me, self.mate
        landed([self.swap])
        mate[...] = (self.part[me.c].astype(F32) + mate[...].astype(F32)).astype(BF)
        self.back = [self.net.go(mate.at[(me.y + k) % 4], self.got.at[k - 1], me.yp(k)) for k in ORDER]

    def end(self):
        total = self.mate[self.me.y].astype(F32)
        landed(self.back)
        for k in range(3):
            total = total + self.got[k].astype(F32)
        self.net.left([self.swap] + self.back)
        return total


def whole(ref, columns):
    return ref[:, :, :, :, columns].reshape(D, -1)


def mlp_product(me, net, beside, mid, gain, wm, weights, hid, gate, up, prod):
    normed, _ = unit_rms(mid[...])
    hid[me.c, me.y] = (normed * gain).astype(BF)
    rest = gather_yc(me, net, hid)
    beside.step()
    copies = rest()
    beside.step()
    weights(GATE, UP)

    def first(i, _):
        cols = columns_of(i)
        gate_part = dot(hid[...].reshape(256, D), whole(wm, cols))
        up_part = dot(hid[...].reshape(256, D), whole(wm, columns_of(i, UNITS)))
        gate[:, cols] = gate_part
        up[:, cols] = up_part
        prod[:, cols] = (gate_part * jax.nn.sigmoid(gate_part) * up_part).astype(BF)
        return 0

    lax.fori_loop(0, UNITS // CHUNK, first, 0)
    net.left(copies)


def mlp_down(me, net, wm, prod, part, mate, got):
    part[...] = dot(prod[...], whole(wm, DOWN), 1, 1).astype(BF).reshape(2, 4, OWN, D)
    return ScatterYC(me, net, part, mate, got)


def call(kernel, name, collective_id, ins, outs, scratch):
    names = list(ins) + list(outs) + list(scratch)

    def body(*refs):
        kernel(types.SimpleNamespace(**dict(zip(names, refs))))

    def spec(here):
        return pl.BlockSpec(memory_space=pltpu.VMEM if here else pl.ANY)

    results = pl.pallas_call(
        body,
        out_shape=tuple(jax.ShapeDtypeStruct(shape, dtype) for shape, dtype, _ in outs.values()),
        in_specs=[spec(here) for _, here in ins.values()],
        out_specs=tuple(spec(here) for _, _, here in outs.values()),
        scratch_shapes=list(scratch.values()),
        compiler_params=pltpu.CompilerParams(
            collective_id=collective_id, has_side_effects=True, vmem_limit_bytes=255 << 18
        ),
        name=name,
    )(*[array for array, _ in ins.values()])
    return dict(zip(outs, results))


def sems(local, send, recv):
    return dict(
        lsem=pltpu.SemaphoreType.DMA((local,)),
        send=pltpu.SemaphoreType.DMA((send,)),
        recv=pltpu.SemaphoreType.DMA((recv,)),
    )


KEPT = dict(
    hid=((4, OWN, D), BF),
    q=((2, HEADS, TOK, HD), BF),
    kv=((2, 2, 4, 4, TOK, 2 * HD), BF),
    att=((2 * TOK, HEADS * HD), BF),
    wf=((2, 4, 4, 2, ROWS, QKW), BF),
    x=((OWN, D), F32),
    mid=((OWN, D), F32),
    hid2=((2, 4, OWN, D), BF),
    gate=((256, UNITS), F32),
    up=((256, UNITS), F32),
    prod=((256, UNITS), BF),
    wm=((4, 4, 2, ROWS, 3 * UNITS), BF),
)
GATE, UP, DOWN = (slice(part * UNITS, (part + 1) * UNITS) for part in range(3))
FORWARD_LAGS = (5, 5, 7, 1, 3, 3, 5, 3)
FORWARD_TURNS = (4, 6, 3, 1, 1, 1, 0, 1, 1, 2, 0, 2, 1, 2, 0, 1, 1, 1, 0, 1, 0, 2, 2, 1, 8)
BACKWARD_LAGS = (5, 0, 3, 3, 1, 0, 3, 3)
BACKWARD_TURNS = (1, 0, 2, 0, 1, 0, 0, 0, 1, 2, 0, 1, 2, 1, 0, 0, 0, 1, 0, 1, 0, 1, 2, 0, 2, 2)


def vmem(shape_dtype):
    return pltpu.VMEM(*shape_dtype)


def forward_kernel(r):
    me = Place()
    me.greet()
    net, local = Links(r.send, r.recv), Local(r.lsem)
    peers = me.quad()
    early, late, arrivals = [], [], []
    everyone = me.quad() + ((me.c, me.s, None),)

    def hand_out(copies, src, dst):
        waits = []
        for core, section, peer in everyone:
            if peer is None:
                waits.append(local.go(src(core, section), dst).wait)
            else:
                copies.append(net.go(src(core, section), dst, peer))
                waits.append(functools.partial(landed, copies[-1:]))
        return waits

    def columns_for(width, core_and_section, base=0):
        return pl.ds(pl.multiple_of(core_and_section * width + base, 128), width)

    attn_dst = r.attn_rows.at[me.s, me.c]
    waits = hand_out(early, lambda c, s: r.attn_flat.at[c, :, columns_for(384, s)], attn_dst.at[:, :384])
    waits += hand_out(early, lambda c, s: r.attn_flat.at[c, :, 768:], attn_dst.at[:, 384:])
    r.padded[...] = jnp.zeros((16, D), F32)
    r.padded[:2, :48] = r.gains_here[...].astype(F32)
    r.padded[8:14, :4] = r.bias_q_here[...].astype(F32)
    r.padded[14:, :4] = r.bias_kv_here[...].astype(F32)
    spots = pltpu.roll(r.padded[:8], me.ctx * 48, 1)
    for which in range(2):
        for i in range(12):
            r.tiny_f32[12 * which + i : 12 * which + i + 1] = spots[which : which + 1, i * 128 : (i + 1) * 128]
    r.tiny_f32[24:] = pltpu.roll(r.padded[8:, :128], me.ctx * 4, 1)
    r.tiny[...] = r.tiny_f32[...].astype(BF)
    waits += hand_out(early, lambda c, s: r.tiny, r.tiny_quad.at[me.s, me.c])
    away = pl.ds(pl.multiple_of((1 - me.s) * OWN, OWN), OWN)
    home = pl.ds(pl.multiple_of(me.s * OWN, OWN), OWN)
    tokens_over = net.go(r.ends.at[me.h, away], r.tokens.at[me.s], dict(section=1 - me.s))
    tokens_here = local.go(r.ends.at[me.h, home], r.tokens.at[me.s])
    for part, columns in enumerate((GATE, UP, DOWN)):
        src = r.down_flat if part == 2 else r.gate_up_flat.at[part]
        arrivals.append(
            hand_out(
                late, lambda c, s: src.at[:, columns_for(UNITS, 2 * s + c)], r.mlp_rows.at[me.s, me.c, :, columns]
            )
        )

    beside = Beside(FORWARD_LAGS, FORWARD_TURNS)
    saved, done, swaps = [], [], [None, None]
    attn_jobs, mlp_jobs = [None, None], [[], []]

    def save(l, *names):
        for name in names:
            saved.append(local.go(getattr(r, name + str(l)), getattr(r, "out_" + name + str(l))))

    def add_attn(l):
        own = getattr(r, f"wf{l}").at[me.c]

        def swap():
            swaps[l] = net.go(own, own, me.cp())

        attn_jobs[l] = beside.add(Gather(me, net, local, r.attn_rows.at[l], own, (), swap))

    def add_mlp(l, columns):
        buf, out = (getattr(r, f"{name}{l}").at[:, :, :, :, columns] for name in ("wm", "out_wm"))
        ready = arrivals[columns.start // UNITS] if l == 0 else ()
        job = Gather(
            me, net, local, r.mlp_rows.at[l, :, :, columns], buf, ready, lambda: saved.append(local.go(buf, out)),
            (l + columns.start // UNITS) % 2 == 1,
        )
        mlp_jobs[l].append((columns, beside.add(job)))

    for wait in waits:
        wait()
    r.tiny_mine[...] = (r.tiny_quad[:, 0].astype(F32) + r.tiny_quad[:, 1].astype(F32)).astype(BF)
    one = [net.go(r.tiny_mine, r.tiny_x.at[k - 1], me.xp(k)) for k in ORDER]
    for l in range(2):
        add_attn(l)
        for columns in (GATE, UP, DOWN):
            add_mlp(l, columns)
    beside.step()
    landed(one)
    r.tiny_row[...] = (
        r.tiny_mine[...].astype(F32) + r.tiny_x[0].astype(F32) + r.tiny_x[1].astype(F32) + r.tiny_x[2].astype(F32)
    ).astype(BF)
    two = [net.go(r.tiny_row, r.tiny_z.at[k - 1], me.zp(k)) for k in ORDER]
    beside.step()
    landed(two)
    r.small[...] = (
        r.tiny_row[...].astype(F32) + r.tiny_z[0].astype(F32) + r.tiny_z[1].astype(F32) + r.tiny_z[2].astype(F32)
    )

    def gain(l, which):
        return jnp.concatenate([r.small[l, 12 * which + i : 12 * which + i + 1, :] for i in range(12)], axis=1)

    def bias(l):
        rows = [r.small[l, pl.ds(24 + HEADS * me.s + i, 1), :] for i in range(HEADS)]
        rows += [r.small[l, 30 + i : 31 + i, :] for i in range(2)]
        return jnp.concatenate(rows, axis=1)

    for l in range(2):
        for which in range(2):
            r.gains[l, which] = gain(l, which)
    tokens_here.wait()
    landed([tokens_over])
    r.low[me.c, me.y] = r.tokens[1].astype(BF)
    low_rest = []

    for l in range(2):
        kept = types.SimpleNamespace(**{name: getattr(r, name + str(l)) for name in KEPT})
        if l == 0:
            kept.x[...] = r.tokens[0]

        def attn_weights():
            if l == 0:
                low_rest.append(gather_yc(me, net, r.low))
            else:
                beside.step()
            beside.until(attn_jobs[l])
            landed([swaps[l]])
            done.append(swaps[l])

        attn_forward(
            me, net, beside, kept.x, r.gains[l, 0], bias(l), r.turns, kept.wf, attn_weights,
            kept.hid, kept.q, kept.kv, kept.att, getattr(r, f"part{l}"), getattr(r, f"got{l}"), kept.mid,
        )
        if l == 0:
            done += low_rest[0]()
        save(l, "hid", "q", "kv", "att", "wf", "x", "mid")
        weights = lambda *wanted: beside.until(*[job for columns, job in mlp_jobs[l] if columns in wanted])
        mlp_product(
            me, net, beside, kept.mid, r.gains[l, 1], kept.wm, weights, kept.hid2, kept.gate, kept.up, kept.prod
        )
        save(l, "hid2", "gate", "up", "prod")
        beside.step()
        if l == 0:
            weights(DOWN)
            scatter = mlp_down(me, net, kept.wm, kept.prod, r.wide0, r.mate0, r.got20)
            beside.step()
            scatter.middle()
            beside.step()
            r.x1[...] = (kept.mid[...] + scatter.end()).astype(BF).astype(F32)
    beside.rest()
    for copy in saved:
        copy.wait()
    net.left(early + late + [tokens_over] + one + two + done)


def forward(attn_flat, gate_up_flat, down_flat, gains_here, bias_q_here, bias_kv_here, ends, turns):
    ins = dict(
        attn_flat=(attn_flat, False), gate_up_flat=(gate_up_flat, False), down_flat=(down_flat, False),
        gains_here=(gains_here, True), bias_q_here=(bias_q_here, True), bias_kv_here=(bias_kv_here, True),
        ends=(ends, False), turns=(turns, True),
    )
    outs = {f"out_{name}{l}": (*KEPT[name], False) for l in range(2) for name in KEPT}
    outs["gains"] = ((2, 2, 1, D), F32, True)
    outs["low"] = ((2, 4, OWN, D), BF, True)
    outs["tokens"] = ((2, OWN, D), F32, True)
    scratch = {f"{name}{l}": vmem(KEPT[name]) for l in range(2) for name in KEPT}
    scratch |= dict(
        attn_rows=pltpu.VMEM((2, 2, ROWS, QKW), BF),
        mlp_rows=pltpu.VMEM((2, 2, ROWS, 3 * UNITS), BF),
        padded=pltpu.VMEM((16, D), F32),
        tiny_f32=pltpu.VMEM((32, 128), F32),
        tiny=pltpu.VMEM((32, 128), BF),
        tiny_quad=pltpu.VMEM((2, 2, 32, 128), BF),
        tiny_mine=pltpu.VMEM((2, 32, 128), BF),
        tiny_x=pltpu.VMEM((3, 2, 32, 128), BF),
        tiny_row=pltpu.VMEM((2, 32, 128), BF),
        tiny_z=pltpu.VMEM((3, 2, 32, 128), BF),
        small=pltpu.VMEM((2, 32, 128), F32),
    )
    for l in range(2):
        scratch["part" + str(l)] = pltpu.VMEM((4, OWN, D), BF)
        scratch["got" + str(l)] = pltpu.VMEM((3, OWN, D), BF)
    scratch |= dict(
        wide0=pltpu.VMEM((2, 4, OWN, D), BF), mate0=pltpu.VMEM((4, OWN, D), BF), got20=pltpu.VMEM((3, OWN, D), BF)
    )
    return call(forward_kernel, "forward", 0, ins, outs, scratch | sems(48, 200, 413 + 3))


def attn_backward(me, net, beside, r, layer, gm, load_weights, asides, early_done):
    da, dakv, got, kpair_got = r.da.at[layer], r.dakv.at[layer], r.got.at[layer], r.kpair_got.at[layer]
    kz, kx, k3 = r.kz.at[layer], r.kx.at[layer], r.k3.at[layer]
    wf, dws = r.wm.at[:, :, :, :, : 2 * QKW], r.wm.at[:, :, :, :, UNITS : UNITS + 2 * QKW]
    r.low2[me.y] = gm.astype(BF)
    own = r.low2.at[me.y]
    gathered = [net.go(own, own, me.yp(k)) for k in ORDER]
    beside.step()
    cos, sin = twice(r.turns[0]), twice(r.turns[1])
    load_weights()
    landed(gathered)
    grad_mid = r.low2[...].reshape(2 * TOK, D)
    grad_att = dot(grad_mid, whole(wf, slice(512, 896))).astype(BF)
    for m in range(2):
        rows = slice(m * TOK, (m + 1) * TOK)
        queries = r.q[m].reshape(HEADS * TOK, HD)
        keys = r.kv[:, m, :, :, :, :HD].reshape(2048, HD)
        values = r.kv[:, m, :, :, :, HD:].reshape(2048, HD)
        grad_out = jnp.concatenate([grad_att[rows, h * HD : (h + 1) * HD] for h in range(HEADS)], axis=0)
        scores = masked(dot(queries, keys, 1, 1), me.ctx)
        weight = jnp.exp(scores - jnp.max(scores, axis=1, keepdims=True))
        soft = weight / jnp.sum(weight, axis=1, keepdims=True)
        grad_soft = dot(grad_out, values, 1, 1)
        delta = jnp.sum(soft * grad_soft, axis=1, keepdims=True)
        grad_scores = (soft * (grad_soft - delta)).astype(BF)
        grad_values = dot(soft.astype(BF), grad_out, 0, 0)
        grad_keys = dot(grad_scores, queries, 0, 0) * (HD**-0.5)
        r.dkv[:, m] = jnp.concatenate([grad_keys, grad_values], axis=1).astype(BF).reshape(2, 4, 4, TOK, 2 * HD)
        dq = dot(grad_scores, keys) * (HD**-0.5)
        for h in range(HEADS):
            r.dqs[rows, h * HD : (h + 1) * HD] = dq[h * TOK : (h + 1) * TOK]
        beside.step()
    swap = net.go(r.dkv.at[1 - me.c], r.kmate, me.cp())
    dq_low = jnp.concatenate(
        [turned_back(r.dqs[:, h * HD : (h + 1) * HD], cos, sin).astype(BF) for h in range(HEADS)], axis=1
    )
    hidden = r.hid[...].reshape(2 * TOK, D)
    beside.step()
    landed([swap])
    kmate, k2 = r.kmate, r.k2
    kmate[...] = (kmate[...].astype(F32) + r.dkv[me.c].astype(F32)).astype(BF)
    first0 = [net.go(kmate.at[0, (me.z + k) % 4], kz.at[k - 1], me.zp(k)) for k in ORDER]
    first1 = [net.go(kmate.at[1, :, (me.x + k) % 4], kx.at[k - 1], me.xp(k)) for k in ORDER]

    def blocks(value):
        return value.astype(BF).reshape(4, 4, 2, ROWS, -1)

    dws[:, :, :, :, :384] = blocks(dot(hidden, dq_low, 0, 0))
    dws[:, :, :, :, 512:896] = blocks(dot(grad_mid, r.att[...], 0, 0))
    dws[:, :, :, :, 896:1024] = jnp.zeros((4, 4, 2, ROWS, HD), BF)

    def half(core, base=0, width=384):
        return pl.ds(pl.multiple_of(core * QKW + base, 128), width)

    early_swap = net.go(dws.at[:, :, :, :, half(1 - me.c)], da, me.cp())
    asides[0]()
    beside.step()
    landed(first0)
    total0 = kmate[0, me.z].astype(F32)
    for k in range(3):
        total0 = total0 + kz[k].astype(F32)
    k2[0] = total0.astype(BF)
    second0 = [net.go(k2.at[0, (me.x + k) % 4], k3.at[0, k - 1], me.xp(k)) for k in ORDER]
    landed(first1)
    total1 = kmate[1, :, me.x].astype(F32)
    for k in range(3):
        total1 = total1 + kx[k].astype(F32)
    k2[1] = total1.astype(BF)
    second1 = [net.go(k2.at[1, (me.z + k) % 4], k3.at[1, k - 1], me.zp(k)) for k in ORDER]
    landed([early_swap])

    def add_early(j, _):
        da[j] = (dws[j, :, :, :, half(me.c)].astype(F32) + da[j].astype(F32)).astype(BF)
        return 0

    lax.fori_loop(0, 4, add_early, 0)
    early_done()
    asides[1]()
    beside.step()
    landed(second0 + second1)
    for m, place in ((0, me.x), (1, me.z)):
        total = k2[m, place].astype(F32)
        for k in range(3):
            total = total + k3[m, k].astype(F32)
        r.kpair[0, m * TOK : (m + 1) * TOK] = total[:, :HD].astype(BF)
        r.kpair[1, m * TOK : (m + 1) * TOK] = total[:, HD:].astype(BF)
    pair = net.go(r.kpair.at[1 - me.s], kpair_got, dict(section=1 - me.s))
    beside.step()
    landed([pair])
    total = r.kpair[me.s].astype(F32) + kpair_got[...].astype(F32)
    dk_low = jnp.where(me.s == 0, turned_back(total, cos, sin), total).astype(BF)
    w_own = jnp.where(me.s == 0, whole(wf, slice(384, 512)), whole(wf, slice(896, 1024)))
    r.part[...] = (
        (dot(dq_low, whole(wf, slice(0, 384)), 1, 1) + dot(dk_low, w_own, 1, 1)).astype(BF).reshape(4, OWN, D)
    )
    back = [net.go(r.part.at[(me.y + k) % 4], got.at[k - 1], me.yp(k)) for k in ORDER]
    dws[:, :, :, :, 384:512] = blocks(dot(hidden, dk_low, 0, 0))

    late_swap = net.go(dws.at[:, :, :, :, half(1 - me.c, 384, HD)], dakv, me.cp())
    asides[2]()
    beside.step()
    gbias = jnp.concatenate(
        [jnp.sum(dq_low.astype(F32), axis=0, keepdims=True), jnp.sum(dk_low.astype(F32), axis=0, keepdims=True)], axis=1
    )
    dy = r.part[me.y].astype(F32)
    landed(back)
    for k in range(3):
        dy = dy + got[k].astype(F32)
    dx, ggain = norm_back(r.x[...], r.gains[layer, 0], dy)
    gin = gm + dx
    landed([late_swap])
    dakv[...] = (dws[:, :, :, :, half(me.c, 384, HD)].astype(F32) + dakv[...].astype(F32)).astype(BF)
    net.left(gathered + [swap] + first0 + first1 + second0 + second1 + [pair] + back + [early_swap, late_swap])
    return gin, ggain, gbias


def mlp_backward(me, net, beside, r, layer, g, loaded, scatter, free):
    mate, got2 = r.mate.at[layer], r.got2.at[layer]
    loaded("prod")

    def weight_grad(base, left_ref, right_ref):
        def step(i, _):
            r.dm[:, :, :, :, columns_of(i, base)] = (
                dot(left_ref[...].reshape(256, D), right_ref[:, columns_of(i)], 0, 0)
                .astype(BF)
                .reshape(4, 4, 2, ROWS, CHUNK)
            )
            return 0

        lax.fori_loop(0, UNITS // CHUNK, step, 0)

    free(DOWN)
    weight_grad(2 * UNITS, r.low, r.prod)
    scatter(DOWN)
    beside.step()
    loaded("gate", "up", "wm", "hid2")

    def step(i, _):
        cols = columns_of(i)
        dprod = dot(r.low[...].reshape(256, D), whole(r.wm, columns_of(i, 2 * UNITS)))
        gate, up = r.gate[:, cols], r.up[:, cols]
        sigma = jax.nn.sigmoid(gate)
        dg = (dprod * up * sigma * (1.0 + gate * (1.0 - sigma))).astype(BF)
        du = (dprod * gate * sigma).astype(BF)
        r.dgate[:, cols] = dg
        r.dup[:, cols] = du
        return 0

    lax.fori_loop(0, UNITS // CHUNK, step, 0)

    def back(i, _):
        w_gate, w_up = (r.wm[i, :, :, :, part].reshape(D // 4, UNITS) for part in (GATE, UP))
        sums = dot(r.dgate[...], w_gate, 1, 1) + dot(r.dup[...], w_up, 1, 1)
        r.wide[:, :, :, columns_of(i)] = sums.astype(BF).reshape(2, 4, OWN, D // 4)
        return 0

    lax.fori_loop(0, 4, back, 0)
    sums = ScatterYC(me, net, r.wide, mate, got2)
    beside.step()
    free(GATE)
    weight_grad(0, r.hid2, r.dgate)
    sums.middle()
    scatter(GATE)
    beside.step()
    free(UP)
    weight_grad(UNITS, r.hid2, r.dup)
    scatter(UP)
    beside.step()
    dy = sums.end()
    du, ggain = norm_back(r.mid[...], r.gains[layer, 1], dy)
    return g + du, ggain


def put_small(r, base, y, ggain0, ggain1, gbias):
    r.sums[0, base + 24 : base + 40] = jnp.zeros((16, 128), F32)
    for which, ggain in enumerate((ggain0, ggain1)):
        for i in range(12):
            r.sums[0, base + 12 * which + i : base + 12 * which + i + 1] = ggain[:, i * 128 : (i + 1) * 128]
    for i in range(4):
        r.sums[0, pl.ds(base + 24 + 4 * y + i, 1)] = gbias[:, i * 128 : (i + 1) * 128]


def backward_kernel(r):
    me = Place()
    local = Local(r.lsem)
    pending = {}

    def load(layer, *names):
        for name in names:
            pending[name] = local.go(getattr(r, "in" + str(layer) + "_" + name), getattr(r, name))

    def loaded(*wanted):
        for name in wanted:
            pending.pop(name).wait()

    attention = ("hid", "q", "kv", "att", "x")
    low_here = local.go(r.in_low, r.low)
    load(1, "prod", "gate", "up", "wm", "hid2", "mid", *attention)
    me.greet(True)
    net = Links(r.send, r.recv)
    beside = Beside(BACKWARD_LAGS, BACKWARD_TURNS)
    crossed, extra = [], []
    jobs = {}

    def go_home(src, dst):
        for core, section, peer in me.quad():
            crossed.append(net.go(src.at[section, core], dst, peer))
        extra.append(local.go(src.at[me.s, me.c], dst))

    def place_of(width, index):
        return pl.ds(pl.multiple_of(index * width, 128), width)

    def attn_home():
        go_home(r.res_a.at[:, :, :, :384], r.attn_home.at[me.c, :, place_of(384, me.s)])
        go_home(r.res_a.at[:, :, :, 384:], r.kv_home.at[me.c, :, place_of(HD, me.s)])

    def scatter(layer, columns):
        dst = r.down_home if columns == DOWN else r.gate_up_home.at[columns.start // UNITS]
        dst = dst.at[:, place_of(UNITS, 2 * me.s + me.c)]
        then = functools.partial(go_home, r.res_m.at[:, :, :, columns], dst) if layer == 0 else None
        refs = tuple(getattr(r, "m" + str(columns.start) + name) for name in ("_r1", "_r2", "_u1", "_u2"))
        flip = (layer + columns.start // UNITS) % 2 == 1
        part = r.dm.at[:, :, :, :, columns]
        jobs[columns.start] = beside.add(Scatter(me, net, part, refs, r.res_m.at[layer, :, :, columns], then, flip))

    def free(columns):
        if columns.start in jobs:
            beside.until(jobs[columns.start])

    def attn_job(layer):
        refs = (r.a_r1.at[layer], r.a_r2.at[layer], r.a_u1.at[layer], r.a_u2.at[layer])
        beside.add(Scatter(me, net, r.da.at[layer], refs, r.res_a.at[layer, :, :, :384], None, layer == 1))

    def attn_weights(layer):
        refs = r.in1_wf if layer else r.in0_wf
        copies = [local.go(refs.at[i], r.wm.at[:, :, :, :, i * QKW : (i + 1) * QKW]) for i in range(2)]

        def wait():
            for copy in copies:
                copy.wait()
            loaded(*attention)

        return wait

    def kv_scatter(layer):
        return DirectScatter(me, net, r.dakv.at[layer], r.kv_got.at[layer], r.res_a.at[layer, :, :, 384:])

    nothing = lambda: None
    low_here.wait()
    loaded("mid")
    gm, ggain11 = mlp_backward(
        me, net, beside, r, 1, r.tokens[1], loaded, functools.partial(scatter, 1), lambda columns: None
    )
    load(0, "gate", "up", "hid2")
    down = []

    def start_down():
        down.append(mlp_down(me, net, r.wm, r.prod, r.wide, r.mate2, r.got3))
        load(0, "prod")

    asides = (start_down, lambda: down[0].middle(), lambda: down.append(down[0].end()))
    gin, ggain10, gbias1 = attn_backward(
        me, net, beside, r, 1, gm, attn_weights(1), asides, functools.partial(attn_job, 1)
    )
    kv_scatter1 = kv_scatter(1)
    r.out1[...] = r.mid[...] + down[1]
    load(0, "wm", "mid", *attention)
    put_small(r, 40, me.y, ggain10, ggain11, gbias1)
    g = gin.astype(BF).astype(F32)
    r.low[me.c, me.y] = g.astype(BF)
    rest = gather_yc(me, net, r.low)
    beside.step()
    low_copies = rest()
    kv_scatter1.finish()
    loaded("mid")
    gm, ggain01 = mlp_backward(me, net, beside, r, 0, g, loaded, functools.partial(scatter, 0), free)
    gin, ggain00, gbias0 = attn_backward(
        me, net, beside, r, 0, gm, attn_weights(0), (nothing,) * 3, functools.partial(attn_job, 0)
    )
    r.gin[...] = gin
    last_scatter = kv_scatter(0)
    beside.step()
    put_small(r, 0, me.y, ggain00, ggain01, gbias0)
    rounds = ((me.yp, ORDER, 0), (lambda k: me.cp(), (1,), 3), (me.xp, ORDER, 4), (me.zp, ORDER, 7))
    small = []
    for turn, (peer, ks, slot) in enumerate(rounds):
        sent = [net.go(r.sums.at[turn], r.sums_got.at[slot + k - 1], peer(k)) for k in ks]
        if turn == 0:
            r.ends2[0] = r.gin[...].astype(BF)
            r.ends2[1] = r.out1[...].astype(BF)
            edges = [net.go(r.ends2.at[((me.y + k) % 4) % 2], r.ends_got.at[k - 1], me.yp(k)) for k in ORDER]
        if turn == 2:
            last_scatter.finish()
            beside.rest()
            attn_home()
        landed(sent)
        total = r.sums[turn]
        for k in ks:
            total = total + r.sums_got[slot + k - 1]
        r.sums[turn + 1] = total
        small.extend(sent)
    total = r.sums.at[4]
    spots = [r.sums[4, pl.ds(40 * me.s + i, 1)] for i in range(24)]
    spots = jnp.concatenate(
        [jnp.concatenate(spots[12 * which : 12 * which + 12], axis=1) for which in range(2)]
        + [jnp.zeros((6, D), F32)],
        axis=0,
    )
    r.gain_home[...] = pltpu.roll(spots, ((32 - me.ctx) % 32) * 48, 1)[:2, :48]
    rows = [total[pl.ds(40 * me.s + 24 + 8 * me.h + i, 1)] for i in range(8)]
    spots = pltpu.roll(jnp.concatenate(rows, axis=0), ((32 - me.ctx) % 32) * 4, 1)[:, :4]
    r.bias_q_home[:HEADS], r.bias_kv_home[:1] = spots[:HEADS], spots[HEADS : HEADS + 1]
    r.bias_q_home[HEADS:], r.bias_kv_home[1:] = spots[HEADS + 1 : 2 * HEADS + 1], spots[2 * HEADS + 1 :]
    r.boundary[me.y] = jnp.where(me.s == 0, r.gin[...], r.out1[...])
    landed(edges)
    for k in ORDER:
        r.boundary[(me.y + 4 - k) % 4] = r.ends_got[k - 1].astype(F32)
    beside.rest()
    landed(crossed)
    for copy in extra:
        copy.wait()
    net.left(low_copies + crossed + edges + small)


def backward(kept, gains, turns, low, tokens):
    ins = {"in" + str(l) + "_" + name: (kept[l][name], False) for l in range(2) for name in KEPT}
    ins |= dict(gains=(gains, True), turns=(turns, True), in_low=(low, False), tokens=(tokens, True))
    outs = dict(
        gate_up_home=((2, ROWS, 4 * UNITS), BF, False),
        down_home=((ROWS, 4 * UNITS), BF, False),
        attn_home=((2, ROWS, 768), BF, False),
        kv_home=((2, ROWS, 2 * HD), BF, False),
        boundary=((4, OWN, D), F32, True),
        gain_home=((2, 48), F32, True),
        bias_q_home=((2 * HEADS, 4), F32, True),
        bias_kv_home=((2, 4), F32, True),
    )
    scratch = {name: vmem(KEPT[name]) for name in KEPT if name != "wf"}
    scratch |= dict(
        low=pltpu.VMEM((2, 4, OWN, D), BF),
        dgate=pltpu.VMEM((256, UNITS), BF),
        dup=pltpu.VMEM((256, UNITS), BF),
        wide=pltpu.VMEM((2, 4, OWN, D), BF),
        mate=pltpu.VMEM((2, 4, OWN, D), BF),
        got2=pltpu.VMEM((2, 3, OWN, D), BF),
        dm=pltpu.VMEM((4, 4, 2, ROWS, 3 * UNITS), BF),
        low2=pltpu.VMEM((4, OWN, D), BF),
        dkv=pltpu.VMEM((2, 2, 4, 4, TOK, 2 * HD), BF),
        kmate=pltpu.VMEM((2, 4, 4, TOK, 2 * HD), BF),
        kz=pltpu.VMEM((2, 3, 4, TOK, 2 * HD), BF),
        kx=pltpu.VMEM((2, 3, 4, TOK, 2 * HD), BF),
        k2=pltpu.VMEM((2, 4, TOK, 2 * HD), BF),
        k3=pltpu.VMEM((2, 2, 3, TOK, 2 * HD), BF),
        kpair=pltpu.VMEM((2, 2 * TOK, HD), BF),
        kpair_got=pltpu.VMEM((2, 2 * TOK, HD), BF),
        dqs=pltpu.VMEM((2 * TOK, HEADS * HD), F32),
        da=pltpu.VMEM((2, 4, 4, 2, ROWS, 384), BF),
        dakv=pltpu.VMEM((2, 4, 4, 2, ROWS, HD), BF),
        part=pltpu.VMEM((4, OWN, D), BF),
        got=pltpu.VMEM((2, 3, OWN, D), BF),
        sums=pltpu.VMEM((5, 80, 128), F32),
        sums_got=pltpu.VMEM((10, 80, 128), F32),
        gin=pltpu.VMEM((OWN, D), F32),
        out1=pltpu.VMEM((OWN, D), F32),
        res_m=pltpu.VMEM((2, 2, ROWS, 3 * UNITS), BF),
        res_a=pltpu.VMEM((2, 2, ROWS, QKW), BF),
        kv_got=pltpu.VMEM((2, 15, 2, ROWS, HD), BF),
        ends2=pltpu.VMEM((2, OWN, D), BF),
        ends_got=pltpu.VMEM((3, OWN, D), BF),
        mate2=pltpu.VMEM((4, OWN, D), BF),
        got3=pltpu.VMEM((3, OWN, D), BF),
    )
    for columns in (GATE, UP, DOWN):
        for name, shape in zip(("_r1", "_r2", "_u1", "_u2"), Scatter.shapes(UNITS)):
            scratch["m" + str(columns.start) + name] = pltpu.VMEM(shape, BF)
    for name, shape in zip(("a_r1", "a_r2", "a_u1", "a_u2"), Scatter.shapes(384)):
        scratch[name] = pltpu.VMEM((2,) + shape, BF)
    return call(backward_kernel, "backward", 1, ins, outs, scratch | sems(60, 160, 260))


def body(ends, w_query, w_kv, w_out, w_gate_up, w_down, gains, bias_query, bias_kv):
    me = Place()
    kv = w_kv[0].transpose(1, 0, 2)
    attn_flat = jnp.concatenate([jnp.stack([w_query[0], w_out[0]]), kv], axis=2)
    missing = 4 * UNITS - w_down.shape[2]
    gate_up_flat = jnp.pad(w_gate_up[0].transpose(1, 0, 2), ((0, 0), (0, 0), (0, missing)))
    down_flat = jnp.pad(w_down[0], ((0, 0), (0, missing)))
    lane = jnp.arange(HD, dtype=jnp.int32)
    inverse = 1.0 / THETA ** ((lane % 64).astype(F32) * (2.0 / HD))
    positions = (me.ctx * TOK + jnp.arange(TOK, dtype=jnp.int32)).astype(F32)
    angles = positions[:, None] * inverse[None, :]
    turns = jnp.stack([jnp.cos(angles), jnp.where(lane < 64, -1.0, 1.0) * jnp.sin(angles)])

    ahead = forward(attn_flat, gate_up_flat, down_flat, gains[0], bias_query[0], bias_kv[0, :, 0], ends[0], turns)
    kept = [{name: ahead[f"out_{name}{l}"] for name in KEPT} for l in range(2)]
    done = backward(kept, ahead["gains"], turns, ahead["low"], ahead["tokens"])

    units = w_down.shape[2]
    return (
        done["boundary"].reshape(1, 2, TOK, D),
        done["attn_home"][0].astype(F32)[None],
        done["kv_home"][0].astype(F32).reshape(1, ROWS, 2, HD),
        done["attn_home"][1].astype(F32)[None],
        done["gate_up_home"][:, :, :units].astype(F32).transpose(1, 0, 2)[None],
        done["down_home"][:, :units].astype(F32)[None],
        done["gain_home"][None],
        done["bias_q_home"][None],
        done["bias_kv_home"].reshape(1, 2, 1, 4),
    )


def solution(mesh):
    placed = (
        P("section", None, "ctx", None),
        P("section", "ctx", "shard"),
        P("section", "ctx", None, "shard"),
        P("section", "ctx", "shard"),
        P("section", "ctx", None, "shard"),
        P("section", "ctx", "shard"),
        P("section", None, "ctx"),
        P("section", "shard", "ctx"),
        P("section", None, "shard", "ctx"),
    )
    return jax.shard_map(
        body,
        mesh=mesh,
        in_specs=placed,
        out_specs=(
            P("section", None, "ctx", None),
            P("section", "ctx", "shard"),
            P("section", "ctx", None, "shard"),
            P("section", "ctx", "shard"),
            P("section", "ctx", None, "shard"),
            P("section", "ctx", "shard"),
            P("section", None, "ctx"),
            P("section", "shard", "ctx"),
            P("section", None, "shard", "ctx"),
        ),
        check_vma=False,
    )
```

```python
import functools
import types

import jax
import jax.numpy as jnp
from jax import lax
from jax.experimental import pallas as pl
from jax.experimental.pallas import tpu as pltpu
from jax.sharding import PartitionSpec as P

MESH = pl.DeviceIdType.MESH
BF = jnp.bfloat16
F32 = jnp.float32
EPS = 1e-06
THETA = 1000000.0
D = 1536
HD = 128
HEADS = 3
UNITS = 1152
CHUNK = 384
TOK = 64
OWN = 32
ROWS = 48
QKW = 512
ORDER = (1, 3, 2)
SIDES = (1, 3)
OTHERS = tuple((dz, dx) for dz in range(4) for dx in range(4) if (dz, dx) != (0, 0))


class Place:
    def __init__(self):
        self.ctx = lax.axis_index("ctx")
        self.s = lax.axis_index("section")
        self.h = lax.axis_index("shard")
        self.z = self.ctx // 8
        self.x = (self.ctx // 2) % 4
        self.c = self.ctx % 2
        self.y = self.h * 2 + self.s

    def yp(self, k):
        other = (self.y + k) % 4
        return dict(section=other % 2, shard=other // 2)

    def xp(self, k):
        return dict(ctx=self.z * 8 + ((self.x + k) % 4) * 2 + self.c)

    def zp(self, k):
        return dict(ctx=(self.ctx + 8 * k) % 32)

    def cp(self):
        return dict(ctx=self.ctx + 1 - 2 * self.c)

    def quad(self):
        return (
            (self.c, 1 - self.s, dict(section=1 - self.s)),
            (1 - self.c, self.s, self.cp()),
            (1 - self.c, 1 - self.s, dict(section=1 - self.s, ctx=self.ctx + 1 - 2 * self.c)),
        )

    def chip(self, dz, dx):
        return dict(ctx=((self.z + dz) % 4) * 8 + ((self.x + dx) % 4) * 2 + self.c)

    def greet(self, far=False):
        peers = [self.yp(k) for k in ORDER] + [self.cp(), self.quad()[2][2]]
        peers += [self.xp(k) for k in ORDER] + [self.zp(k) for k in ORDER]
        if far:
            peers += [self.chip(dz, dx) for dz, dx in OTHERS if dz and dx]
        barrier = pltpu.get_barrier_semaphore()
        for peer in peers:
            pl.semaphore_signal(barrier, 1, device_id=peer, device_id_type=MESH)
        pl.semaphore_wait(barrier, len(peers))


class Links:
    def __init__(self, send, recv):
        self.send, self.recv, self.count = send, recv, 0
        self.free = list(range(send.shape[0]))

    def go(self, src, dst, peer):
        index = self.count
        self.count += 1
        slot = self.free.pop(0)
        copy = pltpu.make_async_remote_copy(
            src, dst, self.send.at[slot], self.recv.at[index], device_id=peer, device_id_type=MESH
        )
        copy.start()
        return copy, slot

    def left(self, copies):
        for copy, slot in copies:
            copy.wait_send()
            self.free.append(slot)


def landed(copies):
    for copy, _ in copies:
        copy.wait_recv()


class Local:
    def __init__(self, sems):
        self.sems, self.count = sems, 0

    def go(self, src, dst):
        copy = pltpu.make_async_copy(src, dst, self.sems.at[self.count])
        self.count += 1
        copy.start()
        return copy


def cuts(columns, flip):
    cut = (columns // 256) * 128
    both = (slice(0, cut), slice(cut, columns))
    return both[::-1] if flip else both


class Gather:
    copies = 40

    def __init__(self, me, net, local, src, buf, ready=(), then=None, flip=False):
        self.me, self.net, self.local, self.src, self.buf, self.ready = me, net, local, src, buf, ready
        self.then = then
        self.cuts = cuts(src.shape[-1], flip)
        self.sent = []

    def steps(self):
        by_half = [functools.partial(f, half) for f in (self.second, self.third, self.fourth) for half in range(2)]
        return [self.start, *by_half, self.finish]

    def at(self, half, p, q):
        return self.buf.at[q, p, 0] if half == 0 else self.buf.at[p, q, 1]

    def axes(self, half):
        me = self.me
        return (me.x, me.z, me.xp, me.zp) if half == 0 else (me.z, me.x, me.zp, me.xp)

    def go(self, src, dst, peer):
        copy = self.net.go(src, dst, peer)
        self.sent.append(copy)
        return copy

    def start(self):
        me = self.me
        for wait in self.ready:
            wait()
        self.own = self.local.go(self.src, self.buf.at[me.z, me.x])
        self.a, self.c = [None, None], [[None] * 4, [None] * 4]
        self.f, self.last = [[], []], []
        for half in range(2):
            p, q, pp, qp = self.axes(half)
            self.a[half] = [self.go(self.src.at[half], self.at(half, p, q), pp(k)) for k in SIDES]
        for half in range(2):
            p, q, pp, qp = self.axes(half)
            self.c[half][0] = [self.go(self.src.at[half], self.at(half, p, q), qp(k)) for k in SIDES]

    def second(self, half):
        p, q, pp, qp = self.axes(half)
        for i, k in enumerate(SIDES):
            landed([self.a[half][i]])
            piece = self.at(half, (p + 4 - k) % 4, q).at[:, self.cuts[i]]
            self.f[half].append(self.go(piece, piece, pp(k)))
        for i, k in enumerate(SIDES):
            block = self.at(half, (p + 4 - k) % 4, q)
            self.c[half][i + 1] = [self.go(block, block, qp(kk)) for kk in SIDES]

    def third(self, half):
        p, q, pp, qp = self.axes(half)
        landed(self.f[half])
        block = self.at(half, (p + 2) % 4, q)
        self.c[half][3] = [self.go(block, block, qp(kk)) for kk in SIDES]
        self.onward(half, (0,))

    def fourth(self, half):
        self.onward(half, (1, 2, 3))

    def onward(self, half, turns):
        p, q, pp, qp = self.axes(half)
        for j in turns:
            shift = (0, 3, 1, 2)[j]
            for i, k in enumerate(SIDES):
                landed([self.c[half][j][i]])
                piece = self.at(half, (p + shift) % 4, (q + 4 - k) % 4).at[:, self.cuts[i]]
                self.last.append(self.go(piece, piece, qp(k)))

    def finish(self):
        landed(self.last)
        self.own.wait()
        self.net.left(self.sent)
        if self.then is not None:
            self.then()


class Scatter:
    copies = 16

    def __init__(self, me, net, part, scratch, out, then=None, flip=False):
        self.me, self.net, self.part, self.out, self.then = me, net, part, out, then
        self.r1, self.r2, self.u1, self.u2 = scratch
        self.cuts = cuts(part.shape[-1], flip)
        self.sent = []

    def steps(self):
        by_half = [functools.partial(f, half) for f in (self.second, self.third, self.fourth) for half in range(2)]
        return [self.start, *by_half, self.finish]

    @staticmethod
    def shapes(columns):
        wide = columns - (columns // 256) * 128
        return ((2, 2, 4, ROWS, wide), (2, 2, 4, ROWS, columns), (2, 2, ROWS, wide), (2, 2, ROWS, columns))

    def group(self, half, q):
        return self.part.at[q, :, 0] if half == 0 else self.part.at[:, q, 1]

    def axes(self, half):
        me = self.me
        return (me.x, me.z, me.xp, me.zp) if half == 0 else (me.z, me.x, me.zp, me.xp)

    def go(self, src, dst, peer):
        copy = self.net.go(src, dst, peer)
        self.sent.append(copy)
        return copy

    def wide(self, i):
        return slice(0, self.cuts[i].stop - self.cuts[i].start)

    def start(self):
        self.one, self.two, self.three, self.four = ([[], []] for _ in range(4))
        for half in range(2):
            p, q, pp, qp = self.axes(half)
            for i, k in enumerate(SIDES):
                piece = self.group(half, (q + 2) % 4).at[:, :, self.cuts[i]]
                self.one[half].append(self.go(piece, self.r1.at[half, i, :, :, self.wide(i)], qp(k)))

    def second(self, half):
        p, q, pp, qp = self.axes(half)
        for i, k in enumerate(SIDES):
            landed([self.one[half][i]])
            mine = self.group(half, (q + k) % 4)

            def add(j, _):
                mine[j, :, self.cuts[i]] = (
                    mine[j, :, self.cuts[i]].astype(F32) + self.r1[half, i, j, :, self.wide(i)].astype(F32)
                ).astype(BF)
                return 0

            lax.fori_loop(0, 4, add, 0)
            self.two[half].append(self.go(mine, self.r2.at[half, i], qp(k)))

    def third(self, half):
        p, q, pp, qp = self.axes(half)
        landed(self.two[half])
        mine = self.group(half, q)

        def add(j, _):
            mine[j] = (
                mine[j].astype(F32) + self.r2[half, 0, j].astype(F32) + self.r2[half, 1, j].astype(F32)
            ).astype(BF)
            return 0

        lax.fori_loop(0, 4, add, 0)
        for i, k in enumerate(SIDES):
            self.three[half].append(
                self.go(mine.at[(p + 2) % 4, :, self.cuts[i]], self.u1.at[half, i, :, self.wide(i)], pp(k))
            )

    def fourth(self, half):
        p, q, pp, qp = self.axes(half)
        for i, k in enumerate(SIDES):
            landed([self.three[half][i]])
            block = self.group(half, q).at[(p + k) % 4]
            block[:, self.cuts[i]] = (
                block[:, self.cuts[i]].astype(F32) + self.u1[half, i, :, self.wide(i)].astype(F32)
            ).astype(BF)
            self.four[half].append(self.go(block, self.u2.at[half, i], pp(k)))

    def finish(self):
        for half in range(2):
            p, q, pp, qp = self.axes(half)
            landed(self.four[half])
            self.out[half] = (
                self.group(half, q)[p].astype(F32) + self.u2[half, 0].astype(F32) + self.u2[half, 1].astype(F32)
            ).astype(BF)
        self.net.left(self.sent)
        if self.then is not None:
            self.then()


class DirectScatter:
    def __init__(self, me, net, part, got, out):
        self.me, self.net, self.part, self.got, self.out = me, net, part, got, out
        self.sent = []
        for i, (dz, dx) in enumerate(OTHERS):
            src = part.at[(me.z + dz) % 4, (me.x + dx) % 4]
            self.sent.append(net.go(src, got.at[i], me.chip(dz, dx)))

    def finish(self):
        total = self.part[self.me.z, self.me.x].astype(F32)
        landed(self.sent)
        for i in range(len(OTHERS)):
            total = total + self.got[i].astype(F32)
        self.out[...] = total.astype(BF)
        self.net.left(self.sent)


class Beside:
    def __init__(self, lags, turns):
        self.lags, self.turns, self.turn, self.jobs = lags, list(turns), 0, []

    def add(self, job):
        first = self.turn
        if self.jobs:
            first = max(first, self.jobs[-1][0] + self.lags[len(self.jobs)])
        self.jobs.append((first, list(job.steps()), job))
        return job

    def step(self):
        for _ in range(self.turns.pop(0) if self.turns else 0):
            self.take()

    def take(self):
        for first, steps, _ in reversed(self.jobs):
            if self.turn >= first and steps:
                steps.pop(0)()
        self.turn += 1

    def until(self, *jobs):
        while any(steps for _, steps, job in self.jobs if job in jobs):
            self.take()

    def rest(self):
        while any(steps for _, steps, _ in self.jobs):
            self.take()


def dot(a, b, ca=1, cb=0):
    return lax.dot_general(a, b, (((ca,), (cb,)), ((), ())), preferred_element_type=F32)


def unit_rms(u):
    scale = lax.rsqrt(jnp.mean(u * u, axis=1, keepdims=True) + EPS)
    return u * scale, scale


def norm_back(u, gain, dy):
    n, scale = unit_rms(u)
    sd = dy * gain
    return scale * (sd - n * jnp.mean(sd * n, axis=1, keepdims=True)), jnp.sum(dy * n, axis=0, keepdims=True)


def turned(u, cos, sin):
    return u * cos + pltpu.roll(u, 64, 1) * sin


def turned_back(w, cos, sin):
    return w * cos - pltpu.roll(w, 64, 1) * sin


def twice(table):
    return jnp.concatenate([table, table], axis=0)


def key_places(rows):
    j = lax.broadcasted_iota(jnp.int32, (rows, 2048), 1)
    core = j // 1024
    chip = (j % 1024) // TOK
    return chip * (2 * TOK) + core * TOK + j % TOK


def masked(raw, ctx):
    rows = raw.shape[0]
    query = ctx * TOK + lax.broadcasted_iota(jnp.int32, (rows, 2048), 0) % TOK
    return jnp.where(key_places(rows) <= query, raw * (HD**-0.5), -1e30)


def columns_of(i, base=0):
    return pl.ds(pl.multiple_of(base + i * CHUNK, CHUNK), CHUNK)


def attn_forward(me, net, beside, x_ref, gain, bias, turns, wf, weights, hid, q, kv, att, part, got, mid):
    x = x_ref[...]
    normed, _ = unit_rms(x)
    hid[me.y] = (normed * gain).astype(BF)
    hid_copies = [net.go(hid.at[me.y], hid.at[me.y], me.yp(k)) for k in ORDER]
    cos, sin = twice(turns[0]), twice(turns[1])
    weights()
    beside.step()
    landed(hid_copies)
    hidden = hid[...].reshape(2 * TOK, D)
    proj = dot(hidden, whole(wf.at[0], slice(0, QKW))) + bias[:, :QKW]
    key = turned(proj[:, 384:], cos, sin).astype(BF)
    value = (dot(hidden, whole(wf.at[1], slice(384, QKW))) + bias[:, QKW:]).astype(BF)
    keyval = jnp.concatenate([key, value], axis=1)
    for m in range(2):
        kv[me.c, m, me.z, me.x] = keyval[m * TOK : (m + 1) * TOK]
    mine0, mine1 = kv.at[me.c, 0, me.z, me.x], kv.at[me.c, 1, me.z, me.x]
    first0 = [net.go(mine0, mine0, me.xp(k)) for k in ORDER]
    first1 = [net.go(mine1, mine1, me.zp(k)) for k in ORDER]
    for head in range(HEADS):
        query = turned(proj[:, head * HD : (head + 1) * HD], cos, sin).astype(BF)
        for m in range(2):
            q[m, head] = query[m * TOK : (m + 1) * TOK]
    beside.step()
    landed(first0)
    second0 = [net.go(kv.at[me.c, 0, me.z], kv.at[me.c, 0, me.z], me.zp(k)) for k in ORDER]
    landed(first1)
    second1 = [net.go(kv.at[me.c, 1, :, me.x], kv.at[me.c, 1, :, me.x], me.xp(k)) for k in ORDER]
    beside.step()
    landed(second0)
    third0 = net.go(kv.at[me.c, 0], kv.at[me.c, 0], me.cp())
    landed(second1)
    third1 = net.go(kv.at[me.c, 1], kv.at[me.c, 1], me.cp())
    for m, third in ((0, third0), (1, third1)):
        beside.step()
        landed([third])
        queries = q[m].reshape(HEADS * TOK, HD)
        keys = kv[:, m, :, :, :, :HD].reshape(2048, HD)
        values = kv[:, m, :, :, :, HD:].reshape(2048, HD)
        scores = masked(dot(queries, keys, 1, 1), me.ctx)
        weight = jnp.exp(scores - jnp.max(scores, axis=1, keepdims=True))
        total = jnp.sum(weight, axis=1, keepdims=True)
        out = (dot(weight.astype(BF), values) / total).astype(BF)
        for head in range(HEADS):
            att[m * TOK : (m + 1) * TOK, head * HD : (head + 1) * HD] = out[head * TOK : (head + 1) * TOK]
    beside.step()
    part[...] = dot(att[...], whole(wf.at[1], slice(0, 384)), 1, 1).astype(BF).reshape(4, OWN, D)
    back = [net.go(part.at[(me.y + k) % 4], got.at[k - 1], me.yp(k)) for k in ORDER]
    beside.step()
    total = x + part[me.y].astype(F32)
    landed(back)
    for k in range(3):
        total = total + got[k].astype(F32)
    mid[...] = total
    net.left(hid_copies + first0 + first1 + second0 + second1 + [third0, third1] + back)


def gather_yc(me, net, buf):
    own = buf.at[me.c, me.y]
    sent = [net.go(own, own, me.yp(k)) for k in ORDER]
    crossed = [net.go(own, own, me.cp())]

    def rest():
        for k, copy in zip(ORDER, sent):
            landed([copy])
            block = buf.at[me.c, (me.y + 4 - k) % 4]
            crossed.append(net.go(block, block, me.cp()))
        landed(crossed)
        return sent + crossed

    return rest


class ScatterYC:
    def __init__(self, me, net, part, mate, got):
        self.me, self.net, self.part, self.mate, self.got = me, net, part, mate, got
        self.swap = net.go(part.at[1 - me.c], mate, me.cp())

    def middle(self):
        me, mate = self.me, self.mate
        landed([self.swap])
        mate[...] = (self.part[me.c].astype(F32) + mate[...].astype(F32)).astype(BF)
        self.back = [self.net.go(mate.at[(me.y + k) % 4], self.got.at[k - 1], me.yp(k)) for k in ORDER]

    def end(self):
        total = self.mate[self.me.y].astype(F32)
        landed(self.back)
        for k in range(3):
            total = total + self.got[k].astype(F32)
        self.net.left([self.swap] + self.back)
        return total


def whole(ref, columns):
    return ref[:, :, :, :, columns].reshape(D, -1)


def mlp_product(me, net, beside, mid, gain, wm, weights, hid, gate, up, prod):
    normed, _ = unit_rms(mid[...])
    hid[me.c, me.y] = (normed * gain).astype(BF)
    rest = gather_yc(me, net, hid)
    beside.step()
    copies = rest()
    beside.step()
    weights(GATE, UP)

    def first(i, _):
        cols = columns_of(i)
        gate_part = dot(hid[...].reshape(256, D), whole(wm, cols))
        up_part = dot(hid[...].reshape(256, D), whole(wm, columns_of(i, UNITS)))
        gate[:, cols] = gate_part
        up[:, cols] = up_part
        prod[:, cols] = (gate_part * jax.nn.sigmoid(gate_part) * up_part).astype(BF)
        return 0

    lax.fori_loop(0, UNITS // CHUNK, first, 0)
    net.left(copies)


def mlp_down(me, net, wm, prod, part, mate, got):
    part[...] = dot(prod[...], whole(wm, DOWN), 1, 1).astype(BF).reshape(2, 4, OWN, D)
    return ScatterYC(me, net, part, mate, got)


def call(kernel, name, collective_id, ins, outs, scratch):
    names = list(ins) + list(outs) + list(scratch)

    def body(*refs):
        kernel(types.SimpleNamespace(**dict(zip(names, refs))))

    def spec(here):
        return pl.BlockSpec(memory_space=pltpu.VMEM if here else pl.ANY)

    results = pl.pallas_call(
        body,
        out_shape=tuple(jax.ShapeDtypeStruct(shape, dtype) for shape, dtype, _ in outs.values()),
        in_specs=[spec(here) for _, here in ins.values()],
        out_specs=tuple(spec(here) for _, _, here in outs.values()),
        scratch_shapes=list(scratch.values()),
        compiler_params=pltpu.CompilerParams(
            collective_id=collective_id, has_side_effects=True, vmem_limit_bytes=255 << 18
        ),
        name=name,
    )(*[array for array, _ in ins.values()])
    return dict(zip(outs, results))


def sems(local, send, recv):
    return dict(
        lsem=pltpu.SemaphoreType.DMA((local,)),
        send=pltpu.SemaphoreType.DMA((send,)),
        recv=pltpu.SemaphoreType.DMA((recv,)),
    )


KEPT = dict(
    hid=((4, OWN, D), BF),
    q=((2, HEADS, TOK, HD), BF),
    kv=((2, 2, 4, 4, TOK, 2 * HD), BF),
    att=((2 * TOK, HEADS * HD), BF),
    wf=((2, 4, 4, 2, ROWS, QKW), BF),
    x=((OWN, D), F32),
    mid=((OWN, D), F32),
    hid2=((2, 4, OWN, D), BF),
    gate=((256, UNITS), F32),
    up=((256, UNITS), F32),
    prod=((256, UNITS), BF),
    wm=((4, 4, 2, ROWS, 3 * UNITS), BF),
)
GATE, UP, DOWN = (slice(part * UNITS, (part + 1) * UNITS) for part in range(3))
FORWARD_LAGS = (5, 5, 7, 1, 3, 3, 5, 3)
FORWARD_TURNS = (4, 6, 3, 1, 1, 1, 0, 1, 1, 2, 0, 2, 1, 2, 0, 1, 1, 1, 0, 1, 0, 2, 2, 1, 8)
BACKWARD_LAGS = (5, 0, 3, 3, 1, 0, 3, 3)
BACKWARD_TURNS = (1, 0, 2, 0, 1, 0, 0, 0, 1, 2, 0, 1, 2, 1, 0, 0, 0, 1, 0, 1, 0, 1, 2, 0, 2, 2)


def vmem(shape_dtype):
    return pltpu.VMEM(*shape_dtype)


def forward_kernel(r):
    me = Place()
    me.greet()
    net, local = Links(r.send, r.recv), Local(r.lsem)
    peers = me.quad()
    early, late, arrivals = [], [], []
    everyone = me.quad() + ((me.c, me.s, None),)

    def hand_out(copies, src, dst):
        waits = []
        for core, section, peer in everyone:
            if peer is None:
                waits.append(local.go(src(core, section), dst).wait)
            else:
                copies.append(net.go(src(core, section), dst, peer))
                waits.append(functools.partial(landed, copies[-1:]))
        return waits

    def columns_for(width, core_and_section, base=0):
        return pl.ds(pl.multiple_of(core_and_section * width + base, 128), width)

    attn_dst = r.attn_rows.at[me.s, me.c]
    waits = hand_out(early, lambda c, s: r.attn_flat.at[c, :, columns_for(384, s)], attn_dst.at[:, :384])
    waits += hand_out(early, lambda c, s: r.attn_flat.at[c, :, 768:], attn_dst.at[:, 384:])
    r.padded[...] = jnp.zeros((16, D), F32)
    r.padded[:2, :48] = r.gains_here[...].astype(F32)
    eye = lax.broadcasted_iota(jnp.int32, (6, 6), 0) == lax.broadcasted_iota(jnp.int32, (6, 6), 1)
    for lane in range(4):
        row = r.bias_q_here[lane : lane + 1].astype(F32)
        r.padded[8:14, lane : lane + 1] = jnp.sum(jnp.where(eye, row, 0.0), axis=1, keepdims=True)
    r.padded[14:, :4] = r.bias_kv_here[...].astype(F32)
    spots = pltpu.roll(r.padded[:8], me.ctx * 48, 1)
    for which in range(2):
        for i in range(12):
            r.tiny_f32[12 * which + i : 12 * which + i + 1] = spots[which : which + 1, i * 128 : (i + 1) * 128]
    r.tiny_f32[24:] = pltpu.roll(r.padded[8:, :128], me.ctx * 4, 1)
    r.tiny[...] = r.tiny_f32[...].astype(BF)
    waits += hand_out(early, lambda c, s: r.tiny, r.tiny_quad.at[me.s, me.c])
    away = pl.ds(pl.multiple_of((1 - me.s) * OWN, OWN), OWN)
    home = pl.ds(pl.multiple_of(me.s * OWN, OWN), OWN)
    tokens_over = net.go(r.ends.at[me.h, away], r.tokens.at[me.s], dict(section=1 - me.s))
    tokens_here = local.go(r.ends.at[me.h, home], r.tokens.at[me.s])
    here = r.mlp_rows.at[me.s, me.c]
    for part, columns in enumerate((GATE, UP)):
        src = r.gate_up_flat.at[part]
        arrivals.append(hand_out(late, lambda c, s: src.at[:, columns_for(UNITS, 2 * s + c)], here.at[:, columns]))
    body, rest = slice(DOWN.start, DOWN.stop - 128), slice(DOWN.stop - 128, DOWN.stop)

    def rest_for(index):
        return pl.ds(pl.multiple_of(index * UNITS + 1024 - 128 * (index // 3), 128), 128)

    def body_for(index):
        return pl.ds(pl.multiple_of(index * UNITS, 128), 1024)

    waits_down = hand_out(late, lambda c, s: r.down.at[:, body_for(2 * s + c)], here.at[:, body])
    waits_down += hand_out(late, lambda c, s: r.down.at[:, rest_for(2 * s + c)], here.at[:, rest])
    arrivals.append(waits_down)

    beside = Beside(FORWARD_LAGS, FORWARD_TURNS)
    saved, done, swaps = [], [], [None, None]
    attn_jobs, mlp_jobs = [None, None], [[], []]

    def save(l, *names):
        for name in names:
            saved.append(local.go(getattr(r, name + str(l)), getattr(r, "out_" + name + str(l))))

    def add_attn(l):
        own = getattr(r, f"wf{l}").at[me.c]

        def swap():
            swaps[l] = net.go(own, own, me.cp())

        attn_jobs[l] = beside.add(Gather(me, net, local, r.attn_rows.at[l], own, (), swap))

    def add_mlp(l, columns):
        buf, out = (getattr(r, f"{name}{l}").at[:, :, :, :, columns] for name in ("wm", "out_wm"))
        ready = arrivals[columns.start // UNITS] if l == 0 else ()
        job = Gather(
            me, net, local, r.mlp_rows.at[l, :, :, columns], buf, ready, lambda: saved.append(local.go(buf, out)),
            (l + columns.start // UNITS) % 2 == 1,
        )
        mlp_jobs[l].append((columns, beside.add(job)))

    for wait in waits:
        wait()
    r.tiny_mine[...] = (r.tiny_quad[:, 0].astype(F32) + r.tiny_quad[:, 1].astype(F32)).astype(BF)
    one = [net.go(r.tiny_mine, r.tiny_x.at[k - 1], me.xp(k)) for k in ORDER]
    for l in range(2):
        add_attn(l)
        for columns in (GATE, UP, DOWN):
            add_mlp(l, columns)
    beside.step()
    landed(one)
    r.tiny_row[...] = (
        r.tiny_mine[...].astype(F32) + r.tiny_x[0].astype(F32) + r.tiny_x[1].astype(F32) + r.tiny_x[2].astype(F32)
    ).astype(BF)
    two = [net.go(r.tiny_row, r.tiny_z.at[k - 1], me.zp(k)) for k in ORDER]
    beside.step()
    landed(two)
    r.small[...] = (
        r.tiny_row[...].astype(F32) + r.tiny_z[0].astype(F32) + r.tiny_z[1].astype(F32) + r.tiny_z[2].astype(F32)
    )

    def gain(l, which):
        return jnp.concatenate([r.small[l, 12 * which + i : 12 * which + i + 1, :] for i in range(12)], axis=1)

    def bias(l):
        rows = [r.small[l, pl.ds(24 + HEADS * me.s + i, 1), :] for i in range(HEADS)]
        rows += [r.small[l, 30 + i : 31 + i, :] for i in range(2)]
        return jnp.concatenate(rows, axis=1)

    for l in range(2):
        for which in range(2):
            r.gains[l, which] = gain(l, which)
    tokens_here.wait()
    landed([tokens_over])
    r.low[me.c, me.y] = r.tokens[1].astype(BF)
    low_rest = []

    for l in range(2):
        kept = types.SimpleNamespace(**{name: getattr(r, name + str(l)) for name in KEPT})
        if l == 0:
            kept.x[...] = r.tokens[0]

        def attn_weights():
            if l == 0:
                low_rest.append(gather_yc(me, net, r.low))
            else:
                beside.step()
            beside.until(attn_jobs[l])
            landed([swaps[l]])
            done.append(swaps[l])

        attn_forward(
            me, net, beside, kept.x, r.gains[l, 0], bias(l), r.turns, kept.wf, attn_weights,
            kept.hid, kept.q, kept.kv, kept.att, getattr(r, f"part{l}"), getattr(r, f"got{l}"), kept.mid,
        )
        if l == 0:
            done += low_rest[0]()
        save(l, "hid", "q", "kv", "att", "wf", "x", "mid")
        weights = lambda *wanted: beside.until(*[job for columns, job in mlp_jobs[l] if columns in wanted])
        mlp_product(
            me, net, beside, kept.mid, r.gains[l, 1], kept.wm, weights, kept.hid2, kept.gate, kept.up, kept.prod
        )
        save(l, "hid2", "gate", "up", "prod")
        beside.step()
        if l == 0:
            weights(DOWN)
            scatter = mlp_down(me, net, kept.wm, kept.prod, r.wide0, r.mate0, r.got20)
            beside.step()
            scatter.middle()
            beside.step()
            r.x1[...] = (kept.mid[...] + scatter.end()).astype(BF).astype(F32)
    beside.rest()
    for copy in saved:
        copy.wait()
    net.left(early + late + [tokens_over] + one + two + done)


def forward(attn_flat, gate_up_flat, down, gains_here, bias_q_here, bias_kv_here, ends, turns):
    ins = dict(
        attn_flat=(attn_flat, False), gate_up_flat=(gate_up_flat, False), down=(down, False),
        gains_here=(gains_here, True), bias_q_here=(bias_q_here, True), bias_kv_here=(bias_kv_here, True),
        ends=(ends, False), turns=(turns, True),
    )
    outs = {f"out_{name}{l}": (*KEPT[name], False) for l in range(2) for name in KEPT}
    outs["gains"] = ((2, 2, 1, D), F32, True)
    outs["low"] = ((2, 4, OWN, D), BF, True)
    outs["tokens"] = ((2, OWN, D), F32, True)
    scratch = {f"{name}{l}": vmem(KEPT[name]) for l in range(2) for name in KEPT}
    scratch |= dict(
        attn_rows=pltpu.VMEM((2, 2, ROWS, QKW), BF),
        mlp_rows=pltpu.VMEM((2, 2, ROWS, 3 * UNITS), BF),
        padded=pltpu.VMEM((16, D), F32),
        tiny_f32=pltpu.VMEM((32, 128), F32),
        tiny=pltpu.VMEM((32, 128), BF),
        tiny_quad=pltpu.VMEM((2, 2, 32, 128), BF),
        tiny_mine=pltpu.VMEM((2, 32, 128), BF),
        tiny_x=pltpu.VMEM((3, 2, 32, 128), BF),
        tiny_row=pltpu.VMEM((2, 32, 128), BF),
        tiny_z=pltpu.VMEM((3, 2, 32, 128), BF),
        small=pltpu.VMEM((2, 32, 128), F32),
    )
    for l in range(2):
        scratch["part" + str(l)] = pltpu.VMEM((4, OWN, D), BF)
        scratch["got" + str(l)] = pltpu.VMEM((3, OWN, D), BF)
    scratch |= dict(
        wide0=pltpu.VMEM((2, 4, OWN, D), BF), mate0=pltpu.VMEM((4, OWN, D), BF), got20=pltpu.VMEM((3, OWN, D), BF)
    )
    return call(forward_kernel, "forward", 0, ins, outs, scratch | sems(44, 152, 415))


def attn_backward(me, net, beside, r, layer, gm, load_weights, asides, early_done):
    da, dakv, got, kpair_got = r.da.at[layer], r.dakv.at[layer], r.got.at[layer], r.kpair_got.at[layer]
    kz, kx, k3 = r.kz.at[layer], r.kx.at[layer], r.k3.at[layer]
    wf, dws = r.wm.at[:, :, :, :, : 2 * QKW], r.wm.at[:, :, :, :, UNITS : UNITS + 2 * QKW]
    r.low2[me.y] = gm.astype(BF)
    own = r.low2.at[me.y]
    gathered = [net.go(own, own, me.yp(k)) for k in ORDER]
    beside.step()
    cos, sin = twice(r.turns[0]), twice(r.turns[1])
    load_weights()
    landed(gathered)
    grad_mid = r.low2[...].reshape(2 * TOK, D)
    grad_att = dot(grad_mid, whole(wf, slice(512, 896))).astype(BF)
    for m in range(2):
        rows = slice(m * TOK, (m + 1) * TOK)
        queries = r.q[m].reshape(HEADS * TOK, HD)
        keys = r.kv[:, m, :, :, :, :HD].reshape(2048, HD)
        values = r.kv[:, m, :, :, :, HD:].reshape(2048, HD)
        grad_out = jnp.concatenate([grad_att[rows, h * HD : (h + 1) * HD] for h in range(HEADS)], axis=0)
        scores = masked(dot(queries, keys, 1, 1), me.ctx)
        weight = jnp.exp(scores - jnp.max(scores, axis=1, keepdims=True))
        soft = weight / jnp.sum(weight, axis=1, keepdims=True)
        grad_soft = dot(grad_out, values, 1, 1)
        delta = jnp.sum(soft * grad_soft, axis=1, keepdims=True)
        grad_scores = (soft * (grad_soft - delta)).astype(BF)
        grad_values = dot(soft.astype(BF), grad_out, 0, 0)
        grad_keys = dot(grad_scores, queries, 0, 0) * (HD**-0.5)
        r.dkv[:, m] = jnp.concatenate([grad_keys, grad_values], axis=1).astype(BF).reshape(2, 4, 4, TOK, 2 * HD)
        dq = dot(grad_scores, keys) * (HD**-0.5)
        for h in range(HEADS):
            r.dqs[rows, h * HD : (h + 1) * HD] = dq[h * TOK : (h + 1) * TOK]
        beside.step()
    swap = net.go(r.dkv.at[1 - me.c], r.kmate, me.cp())
    dq_low = jnp.concatenate(
        [turned_back(r.dqs[:, h * HD : (h + 1) * HD], cos, sin).astype(BF) for h in range(HEADS)], axis=1
    )
    hidden = r.hid[...].reshape(2 * TOK, D)
    beside.step()
    landed([swap])
    kmate, k2 = r.kmate, r.k2
    kmate[...] = (kmate[...].astype(F32) + r.dkv[me.c].astype(F32)).astype(BF)
    first0 = [net.go(kmate.at[0, (me.z + k) % 4], kz.at[k - 1], me.zp(k)) for k in ORDER]
    first1 = [net.go(kmate.at[1, :, (me.x + k) % 4], kx.at[k - 1], me.xp(k)) for k in ORDER]

    def blocks(value):
        return value.astype(BF).reshape(4, 4, 2, ROWS, -1)

    dws[:, :, :, :, :384] = blocks(dot(hidden, dq_low, 0, 0))
    dws[:, :, :, :, 512:896] = blocks(dot(grad_mid, r.att[...], 0, 0))
    dws[:, :, :, :, 896:1024] = jnp.zeros((4, 4, 2, ROWS, HD), BF)

    def half(core, base=0, width=384):
        return pl.ds(pl.multiple_of(core * QKW + base, 128), width)

    early_swap = net.go(dws.at[:, :, :, :, half(1 - me.c)], da, me.cp())
    asides[0]()
    beside.step()
    landed(first0)
    total0 = kmate[0, me.z].astype(F32)
    for k in range(3):
        total0 = total0 + kz[k].astype(F32)
    k2[0] = total0.astype(BF)
    second0 = [net.go(k2.at[0, (me.x + k) % 4], k3.at[0, k - 1], me.xp(k)) for k in ORDER]
    landed(first1)
    total1 = kmate[1, :, me.x].astype(F32)
    for k in range(3):
        total1 = total1 + kx[k].astype(F32)
    k2[1] = total1.astype(BF)
    second1 = [net.go(k2.at[1, (me.z + k) % 4], k3.at[1, k - 1], me.zp(k)) for k in ORDER]
    landed([early_swap])

    def add_early(j, _):
        da[j] = (dws[j, :, :, :, half(me.c)].astype(F32) + da[j].astype(F32)).astype(BF)
        return 0

    lax.fori_loop(0, 4, add_early, 0)
    early_done()
    asides[1]()
    beside.step()
    landed(second0 + second1)
    for m, place in ((0, me.x), (1, me.z)):
        total = k2[m, place].astype(F32)
        for k in range(3):
            total = total + k3[m, k].astype(F32)
        r.kpair[0, m * TOK : (m + 1) * TOK] = total[:, :HD].astype(BF)
        r.kpair[1, m * TOK : (m + 1) * TOK] = total[:, HD:].astype(BF)
    pair = net.go(r.kpair.at[1 - me.s], kpair_got, dict(section=1 - me.s))
    beside.step()
    landed([pair])
    total = r.kpair[me.s].astype(F32) + kpair_got[...].astype(F32)
    dk_low = jnp.where(me.s == 0, turned_back(total, cos, sin), total).astype(BF)
    w_own = jnp.where(me.s == 0, whole(wf, slice(384, 512)), whole(wf, slice(896, 1024)))
    r.part[...] = (
        (dot(dq_low, whole(wf, slice(0, 384)), 1, 1) + dot(dk_low, w_own, 1, 1)).astype(BF).reshape(4, OWN, D)
    )
    back = [net.go(r.part.at[(me.y + k) % 4], got.at[k - 1], me.yp(k)) for k in ORDER]
    dws[:, :, :, :, 384:512] = blocks(dot(hidden, dk_low, 0, 0))

    late_swap = net.go(dws.at[:, :, :, :, half(1 - me.c, 384, HD)], dakv, me.cp())
    asides[2]()
    beside.step()
    gbias = jnp.concatenate(
        [jnp.sum(dq_low.astype(F32), axis=0, keepdims=True), jnp.sum(dk_low.astype(F32), axis=0, keepdims=True)], axis=1
    )
    dy = r.part[me.y].astype(F32)
    landed(back)
    for k in range(3):
        dy = dy + got[k].astype(F32)
    dx, ggain = norm_back(r.x[...], r.gains[layer, 0], dy)
    gin = gm + dx
    landed([late_swap])
    dakv[...] = (dws[:, :, :, :, half(me.c, 384, HD)].astype(F32) + dakv[...].astype(F32)).astype(BF)
    net.left(gathered + [swap] + first0 + first1 + second0 + second1 + [pair] + back + [early_swap, late_swap])
    return gin, ggain, gbias


def mlp_backward(me, net, beside, r, layer, g, loaded, scatter, free):
    mate, got2 = r.mate.at[layer], r.got2.at[layer]
    loaded("prod")

    def weight_grad(base, left_ref, right_ref):
        def step(i, _):
            r.dm[:, :, :, :, columns_of(i, base)] = (
                dot(left_ref[...].reshape(256, D), right_ref[:, columns_of(i)], 0, 0)
                .astype(BF)
                .reshape(4, 4, 2, ROWS, CHUNK)
            )
            return 0

        lax.fori_loop(0, UNITS // CHUNK, step, 0)

    free(DOWN)
    weight_grad(2 * UNITS, r.low, r.prod)
    scatter(DOWN)
    beside.step()
    loaded("gate", "up", "wm", "hid2")

    def step(i, _):
        cols = columns_of(i)
        dprod = dot(r.low[...].reshape(256, D), whole(r.wm, columns_of(i, 2 * UNITS)))
        gate, up = r.gate[:, cols], r.up[:, cols]
        sigma = jax.nn.sigmoid(gate)
        dg = (dprod * up * sigma * (1.0 + gate * (1.0 - sigma))).astype(BF)
        du = (dprod * gate * sigma).astype(BF)
        r.dgate[:, cols] = dg
        r.dup[:, cols] = du
        return 0

    lax.fori_loop(0, UNITS // CHUNK, step, 0)

    def back(i, _):
        w_gate, w_up = (r.wm[i, :, :, :, part].reshape(D // 4, UNITS) for part in (GATE, UP))
        sums = dot(r.dgate[...], w_gate, 1, 1) + dot(r.dup[...], w_up, 1, 1)
        r.wide[:, :, :, columns_of(i)] = sums.astype(BF).reshape(2, 4, OWN, D // 4)
        return 0

    lax.fori_loop(0, 4, back, 0)
    sums = ScatterYC(me, net, r.wide, mate, got2)
    beside.step()
    free(GATE)
    weight_grad(0, r.hid2, r.dgate)
    sums.middle()
    scatter(GATE)
    beside.step()
    free(UP)
    weight_grad(UNITS, r.hid2, r.dup)
    scatter(UP)
    beside.step()
    dy = sums.end()
    du, ggain = norm_back(r.mid[...], r.gains[layer, 1], dy)
    return g + du, ggain


def put_small(r, base, y, ggain0, ggain1, gbias):
    r.sums[0, base + 24 : base + 40] = jnp.zeros((16, 128), F32)
    for which, ggain in enumerate((ggain0, ggain1)):
        for i in range(12):
            r.sums[0, base + 12 * which + i : base + 12 * which + i + 1] = ggain[:, i * 128 : (i + 1) * 128]
    for i in range(4):
        r.sums[0, pl.ds(base + 24 + 4 * y + i, 1)] = gbias[:, i * 128 : (i + 1) * 128]


def backward_kernel(r):
    me = Place()
    local = Local(r.lsem)
    pending = {}

    def load(layer, *names):
        for name in names:
            pending[name] = local.go(getattr(r, "in" + str(layer) + "_" + name), getattr(r, name))

    def loaded(*wanted):
        for name in wanted:
            pending.pop(name).wait()

    attention = ("hid", "q", "kv", "att", "x")
    low_here = local.go(r.in_low, r.low)
    load(1, "prod", "gate", "up", "wm", "hid2", "mid", *attention)
    me.greet(True)
    net = Links(r.send, r.recv)
    beside = Beside(BACKWARD_LAGS, BACKWARD_TURNS)
    crossed, extra = [], []
    jobs = {}

    def go_home(src, dst):
        for core, section, peer in me.quad():
            crossed.append(net.go(src.at[section, core], dst, peer))
        extra.append(local.go(src.at[me.s, me.c], dst))

    def place_of(width, index):
        return pl.ds(pl.multiple_of(index * width, 128), width)

    def attn_home():
        go_home(r.res_a.at[:, :, :, :384], r.attn_home.at[me.c, :, place_of(384, me.s)])
        go_home(r.res_a.at[:, :, :, 384:], r.kv_home.at[me.c, :, place_of(HD, me.s)])

    def scatter(layer, columns):
        dst = r.down_home if columns == DOWN else r.gate_up_home.at[columns.start // UNITS]
        dst = dst.at[:, place_of(UNITS, 2 * me.s + me.c)]
        then = functools.partial(go_home, r.res_m.at[:, :, :, columns], dst) if layer == 0 else None
        refs = tuple(getattr(r, "m" + str(columns.start) + name) for name in ("_r1", "_r2", "_u1", "_u2"))
        flip = (layer + columns.start // UNITS) % 2 == 1
        part = r.dm.at[:, :, :, :, columns]
        jobs[columns.start] = beside.add(Scatter(me, net, part, refs, r.res_m.at[layer, :, :, columns], then, flip))

    def free(columns):
        if columns.start in jobs:
            beside.until(jobs[columns.start])

    def attn_job(layer):
        refs = (r.a_r1.at[layer], r.a_r2.at[layer], r.a_u1.at[layer], r.a_u2.at[layer])
        beside.add(Scatter(me, net, r.da.at[layer], refs, r.res_a.at[layer, :, :, :384], None, layer == 1))

    def attn_weights(layer):
        refs = r.in1_wf if layer else r.in0_wf
        copies = [local.go(refs.at[i], r.wm.at[:, :, :, :, i * QKW : (i + 1) * QKW]) for i in range(2)]

        def wait():
            for copy in copies:
                copy.wait()
            loaded(*attention)

        return wait

    def kv_scatter(layer):
        return DirectScatter(me, net, r.dakv.at[layer], r.kv_got.at[layer], r.res_a.at[layer, :, :, 384:])

    nothing = lambda: None
    low_here.wait()
    loaded("mid")
    gm, ggain11 = mlp_backward(
        me, net, beside, r, 1, r.tokens[1], loaded, functools.partial(scatter, 1), lambda columns: None
    )
    load(0, "gate", "up", "hid2")
    down = []

    def start_down():
        down.append(mlp_down(me, net, r.wm, r.prod, r.wide, r.mate2, r.got3))
        load(0, "prod")

    asides = (start_down, lambda: down[0].middle(), lambda: down.append(down[0].end()))
    gin, ggain10, gbias1 = attn_backward(
        me, net, beside, r, 1, gm, attn_weights(1), asides, functools.partial(attn_job, 1)
    )
    kv_scatter1 = kv_scatter(1)
    r.out1[...] = r.mid[...] + down[1]
    load(0, "wm", "mid", *attention)
    put_small(r, 40, me.y, ggain10, ggain11, gbias1)
    g = gin.astype(BF).astype(F32)
    r.low[me.c, me.y] = g.astype(BF)
    rest = gather_yc(me, net, r.low)
    beside.step()
    low_copies = rest()
    kv_scatter1.finish()
    loaded("mid")
    gm, ggain01 = mlp_backward(me, net, beside, r, 0, g, loaded, functools.partial(scatter, 0), free)
    gin, ggain00, gbias0 = attn_backward(
        me, net, beside, r, 0, gm, attn_weights(0), (nothing,) * 3, functools.partial(attn_job, 0)
    )
    r.gin[...] = gin
    last_scatter = kv_scatter(0)
    beside.step()
    put_small(r, 0, me.y, ggain00, ggain01, gbias0)
    rounds = ((me.yp, ORDER, 0), (lambda k: me.cp(), (1,), 3), (me.xp, ORDER, 4), (me.zp, ORDER, 7))
    small = []
    for turn, (peer, ks, slot) in enumerate(rounds):
        sent = [net.go(r.sums.at[turn], r.sums_got.at[slot + k - 1], peer(k)) for k in ks]
        if turn == 0:
            r.ends2[0] = r.gin[...].astype(BF)
            r.ends2[1] = r.out1[...].astype(BF)
            edges = [net.go(r.ends2.at[((me.y + k) % 4) % 2], r.ends_got.at[k - 1], me.yp(k)) for k in ORDER]
        if turn == 2:
            last_scatter.finish()
            beside.rest()
            attn_home()
        landed(sent)
        total = r.sums[turn]
        for k in ks:
            total = total + r.sums_got[slot + k - 1]
        r.sums[turn + 1] = total
        small.extend(sent)
    total = r.sums.at[4]
    spots = [r.sums[4, pl.ds(40 * me.s + i, 1)] for i in range(24)]
    spots = jnp.concatenate(
        [jnp.concatenate(spots[12 * which : 12 * which + 12], axis=1) for which in range(2)]
        + [jnp.zeros((6, D), F32)],
        axis=0,
    )
    r.gain_home[...] = pltpu.roll(spots, ((32 - me.ctx) % 32) * 48, 1)[:2, :48]
    rows = [total[pl.ds(40 * me.s + 24 + 8 * me.h + i, 1)] for i in (0, 1, 2, 4, 5, 6, 3, 7)]
    spots = pltpu.roll(jnp.concatenate(rows, axis=0), ((32 - me.ctx) % 32) * 4, 1)
    eye = lax.broadcasted_iota(jnp.int32, (6, 6), 0) == lax.broadcasted_iota(jnp.int32, (6, 6), 1)
    for lane in range(4):
        column = jnp.where(eye, spots[:6, lane : lane + 1], 0.0)
        r.bias_q_home[lane : lane + 1] = jnp.sum(column, axis=0, keepdims=True)
    r.bias_kv_home[...] = spots[6:, :4]
    r.boundary[me.y] = jnp.where(me.s == 0, r.gin[...], r.out1[...])
    landed(edges)
    for k in ORDER:
        r.boundary[(me.y + 4 - k) % 4] = r.ends_got[k - 1].astype(F32)
    beside.rest()
    landed(crossed)
    for copy in extra:
        copy.wait()
    net.left(low_copies + crossed + edges + small)


def backward(kept, gains, turns, low, tokens):
    ins = {"in" + str(l) + "_" + name: (kept[l][name], False) for l in range(2) for name in KEPT}
    ins |= dict(gains=(gains, True), turns=(turns, True), in_low=(low, False), tokens=(tokens, True))
    outs = dict(
        gate_up_home=((2, ROWS, 4 * UNITS), BF, False),
        down_home=((ROWS, 4 * UNITS), BF, False),
        attn_home=((2, ROWS, 768), BF, False),
        kv_home=((2, ROWS, 2 * HD), BF, False),
        boundary=((4, OWN, D), F32, True),
        gain_home=((2, 48), F32, True),
        bias_q_home=((4, 2 * HEADS), F32, True),
        bias_kv_home=((2, 4), F32, True),
    )
    scratch = {name: vmem(KEPT[name]) for name in KEPT if name != "wf"}
    scratch |= dict(
        low=pltpu.VMEM((2, 4, OWN, D), BF),
        dgate=pltpu.VMEM((256, UNITS), BF),
        dup=pltpu.VMEM((256, UNITS), BF),
        wide=pltpu.VMEM((2, 4, OWN, D), BF),
        mate=pltpu.VMEM((2, 4, OWN, D), BF),
        got2=pltpu.VMEM((2, 3, OWN, D), BF),
        dm=pltpu.VMEM((4, 4, 2, ROWS, 3 * UNITS), BF),
        low2=pltpu.VMEM((4, OWN, D), BF),
        dkv=pltpu.VMEM((2, 2, 4, 4, TOK, 2 * HD), BF),
        kmate=pltpu.VMEM((2, 4, 4, TOK, 2 * HD), BF),
        kz=pltpu.VMEM((2, 3, 4, TOK, 2 * HD), BF),
        kx=pltpu.VMEM((2, 3, 4, TOK, 2 * HD), BF),
        k2=pltpu.VMEM((2, 4, TOK, 2 * HD), BF),
        k3=pltpu.VMEM((2, 2, 3, TOK, 2 * HD), BF),
        kpair=pltpu.VMEM((2, 2 * TOK, HD), BF),
        kpair_got=pltpu.VMEM((2, 2 * TOK, HD), BF),
        dqs=pltpu.VMEM((2 * TOK, HEADS * HD), F32),
        da=pltpu.VMEM((2, 4, 4, 2, ROWS, 384), BF),
        dakv=pltpu.VMEM((2, 4, 4, 2, ROWS, HD), BF),
        part=pltpu.VMEM((4, OWN, D), BF),
        got=pltpu.VMEM((2, 3, OWN, D), BF),
        sums=pltpu.VMEM((5, 80, 128), F32),
        sums_got=pltpu.VMEM((10, 80, 128), F32),
        gin=pltpu.VMEM((OWN, D), F32),
        out1=pltpu.VMEM((OWN, D), F32),
        res_m=pltpu.VMEM((2, 2, ROWS, 3 * UNITS), BF),
        res_a=pltpu.VMEM((2, 2, ROWS, QKW), BF),
        kv_got=pltpu.VMEM((2, 15, 2, ROWS, HD), BF),
        ends2=pltpu.VMEM((2, OWN, D), BF),
        ends_got=pltpu.VMEM((3, OWN, D), BF),
        mate2=pltpu.VMEM((4, OWN, D), BF),
        got3=pltpu.VMEM((3, OWN, D), BF),
    )
    for columns in (GATE, UP, DOWN):
        for name, shape in zip(("_r1", "_r2", "_u1", "_u2"), Scatter.shapes(UNITS)):
            scratch["m" + str(columns.start) + name] = pltpu.VMEM(shape, BF)
    for name, shape in zip(("a_r1", "a_r2", "a_u1", "a_u2"), Scatter.shapes(384)):
        scratch[name] = pltpu.VMEM((2,) + shape, BF)
    return call(backward_kernel, "backward", 1, ins, outs, scratch | sems(32, 75, 249))


def body(ends, w_query, w_kv, w_out, w_gate_up, w_down, gains, bias_query, bias_kv):
    me = Place()
    kv = w_kv[0].transpose(1, 0, 2)
    attn_flat = jnp.concatenate([jnp.stack([w_query[0], w_out[0]]), kv], axis=2)
    missing = 4 * UNITS - w_down.shape[2]
    gate_up_flat = jnp.pad(w_gate_up[0].transpose(1, 0, 2), ((0, 0), (0, 0), (0, missing)))
    lane = jnp.arange(HD, dtype=jnp.int32)
    inverse = 1.0 / THETA ** ((lane % 64).astype(F32) * (2.0 / HD))
    positions = (me.ctx * TOK + jnp.arange(TOK, dtype=jnp.int32)).astype(F32)
    angles = positions[:, None] * inverse[None, :]
    turns = jnp.stack([jnp.cos(angles), jnp.where(lane < 64, -1.0, 1.0) * jnp.sin(angles)])

    ahead = forward(attn_flat, gate_up_flat, w_down[0], gains[0], bias_query[0].T, bias_kv[0, :, 0], ends[0], turns)
    kept = [{name: ahead[f"out_{name}{l}"] for name in KEPT} for l in range(2)]
    done = backward(kept, ahead["gains"], turns, ahead["low"], ahead["tokens"])

    units = w_down.shape[2]
    return (
        done["boundary"].reshape(1, 2, TOK, D),
        done["attn_home"][0].astype(F32)[None],
        done["kv_home"][0].astype(F32).reshape(1, ROWS, 2, HD),
        done["attn_home"][1].astype(F32)[None],
        done["gate_up_home"][:, :, :units].astype(F32).transpose(1, 0, 2)[None],
        done["down_home"][:, :units].astype(F32)[None],
        done["gain_home"][None],
        done["bias_q_home"].T[None],
        done["bias_kv_home"].reshape(1, 2, 1, 4),
    )


def solution(mesh):
    placed = (
        P("section", None, "ctx", None),
        P("section", "ctx", "shard"),
        P("section", "ctx", None, "shard"),
        P("section", "ctx", "shard"),
        P("section", "ctx", None, "shard"),
        P("section", "ctx", "shard"),
        P("section", None, "ctx"),
        P("section", "shard", "ctx"),
        P("section", None, "shard", "ctx"),
    )
    return jax.shard_map(
        body,
        mesh=mesh,
        in_specs=placed,
        out_specs=(
            P("section", None, "ctx", None),
            P("section", "ctx", "shard"),
            P("section", "ctx", None, "shard"),
            P("section", "ctx", "shard"),
            P("section", "ctx", None, "shard"),
            P("section", "ctx", "shard"),
            P("section", None, "ctx"),
            P("section", "shard", "ctx"),
            P("section", None, "shard", "ctx"),
        ),
        check_vma=False,
    )
```

```python
import functools
import types

import jax
import jax.numpy as jnp
from jax import lax
from jax.experimental import pallas as pl
from jax.experimental.pallas import tpu as pltpu
from jax.sharding import PartitionSpec as P

MESH = pl.DeviceIdType.MESH
BF = jnp.bfloat16
F32 = jnp.float32
EPS = 1e-06
THETA = 1000000.0
D = 1536
HD = 128
HEADS = 3
UNITS = 1152
CHUNK = 384
TOK = 64
OWN = 32
ROWS = 48
QKW = 512
ORDER = (1, 3, 2)
SIDES = (1, 3)
OTHERS = tuple((dz, dx) for dz in range(4) for dx in range(4) if (dz, dx) != (0, 0))


class Place:
    def __init__(self):
        self.ctx = lax.axis_index("ctx")
        self.s = lax.axis_index("section")
        self.h = lax.axis_index("shard")
        self.z = self.ctx // 8
        self.x = (self.ctx // 2) % 4
        self.c = self.ctx % 2
        self.y = self.h * 2 + self.s

    def yp(self, k):
        other = (self.y + k) % 4
        return dict(section=other % 2, shard=other // 2)

    def xp(self, k):
        return dict(ctx=self.z * 8 + ((self.x + k) % 4) * 2 + self.c)

    def zp(self, k):
        return dict(ctx=(self.ctx + 8 * k) % 32)

    def cp(self):
        return dict(ctx=self.ctx + 1 - 2 * self.c)

    def quad(self):
        return (
            (self.c, 1 - self.s, dict(section=1 - self.s)),
            (1 - self.c, self.s, self.cp()),
            (1 - self.c, 1 - self.s, dict(section=1 - self.s, ctx=self.ctx + 1 - 2 * self.c)),
        )

    def chip(self, dz, dx):
        return dict(ctx=((self.z + dz) % 4) * 8 + ((self.x + dx) % 4) * 2 + self.c)

    def greet(self, far=False):
        peers = [self.yp(k) for k in ORDER] + [self.cp(), self.quad()[2][2]]
        peers += [self.xp(k) for k in ORDER] + [self.zp(k) for k in ORDER]
        if far:
            peers += [self.chip(dz, dx) for dz, dx in OTHERS if dz and dx]
        barrier = pltpu.get_barrier_semaphore()
        for peer in peers:
            pl.semaphore_signal(barrier, 1, device_id=peer, device_id_type=MESH)
        pl.semaphore_wait(barrier, len(peers))


class Links:
    def __init__(self, send, recv):
        self.send, self.recv, self.count = send, recv, 0
        self.free = list(range(send.shape[0]))

    def go(self, src, dst, peer):
        index = self.count
        self.count += 1
        slot = self.free.pop(0)
        copy = pltpu.make_async_remote_copy(
            src, dst, self.send.at[slot], self.recv.at[index], device_id=peer, device_id_type=MESH
        )
        copy.start()
        return copy, slot

    def left(self, copies):
        for copy, slot in copies:
            copy.wait_send()
            self.free.append(slot)


def landed(copies):
    for copy, _ in copies:
        copy.wait_recv()


class Local:
    def __init__(self, sems):
        self.sems, self.count = sems, 0

    def go(self, src, dst):
        copy = pltpu.make_async_copy(src, dst, self.sems.at[self.count])
        self.count += 1
        copy.start()
        return copy


def cuts(columns, flip):
    cut = (columns // 256) * 128
    both = (slice(0, cut), slice(cut, columns))
    return both[::-1] if flip else both


class Gather:
    copies = 40

    def __init__(self, me, net, local, src, buf, ready=(), then=None, flip=False):
        self.me, self.net, self.local, self.src, self.buf, self.ready = me, net, local, src, buf, ready
        self.then = then
        self.cuts = cuts(src.shape[-1], flip)
        self.sent = []

    def steps(self):
        by_half = [functools.partial(f, half) for f in (self.second, self.third, self.fourth) for half in range(2)]
        return [self.start, *by_half, self.finish]

    def at(self, half, p, q):
        return self.buf.at[q, p, 0] if half == 0 else self.buf.at[p, q, 1]

    def axes(self, half):
        me = self.me
        return (me.x, me.z, me.xp, me.zp) if half == 0 else (me.z, me.x, me.zp, me.xp)

    def go(self, src, dst, peer):
        copy = self.net.go(src, dst, peer)
        self.sent.append(copy)
        return copy

    def start(self):
        me = self.me
        for wait in self.ready:
            wait()
        self.own = self.local.go(self.src, self.buf.at[me.z, me.x])
        self.a, self.c = [None, None], [[None] * 4, [None] * 4]
        self.f, self.last = [[], []], []
        for half in range(2):
            p, q, pp, qp = self.axes(half)
            self.a[half] = [self.go(self.src.at[half], self.at(half, p, q), pp(k)) for k in SIDES]
        for half in range(2):
            p, q, pp, qp = self.axes(half)
            self.c[half][0] = [self.go(self.src.at[half], self.at(half, p, q), qp(k)) for k in SIDES]

    def second(self, half):
        p, q, pp, qp = self.axes(half)
        for i, k in enumerate(SIDES):
            landed([self.a[half][i]])
            piece = self.at(half, (p + 4 - k) % 4, q).at[:, self.cuts[i]]
            self.f[half].append(self.go(piece, piece, pp(k)))
        for i, k in enumerate(SIDES):
            block = self.at(half, (p + 4 - k) % 4, q)
            self.c[half][i + 1] = [self.go(block, block, qp(kk)) for kk in SIDES]

    def third(self, half):
        p, q, pp, qp = self.axes(half)
        landed(self.f[half])
        block = self.at(half, (p + 2) % 4, q)
        self.c[half][3] = [self.go(block, block, qp(kk)) for kk in SIDES]
        self.onward(half, (0,))

    def fourth(self, half):
        self.onward(half, (1, 2, 3))

    def onward(self, half, turns):
        p, q, pp, qp = self.axes(half)
        for j in turns:
            shift = (0, 3, 1, 2)[j]
            for i, k in enumerate(SIDES):
                landed([self.c[half][j][i]])
                piece = self.at(half, (p + shift) % 4, (q + 4 - k) % 4).at[:, self.cuts[i]]
                self.last.append(self.go(piece, piece, qp(k)))

    def finish(self):
        landed(self.last)
        self.own.wait()
        self.net.left(self.sent)
        if self.then is not None:
            self.then()


class Scatter:
    copies = 16

    def __init__(self, me, net, part, scratch, out, then=None, flip=False):
        self.me, self.net, self.part, self.out, self.then = me, net, part, out, then
        self.r1, self.r2, self.u1, self.u2 = scratch
        self.cuts = cuts(part.shape[-1], flip)
        self.sent = []

    def steps(self):
        by_half = [functools.partial(f, half) for f in (self.second, self.third, self.fourth) for half in range(2)]
        return [self.start, *by_half, self.finish]

    @staticmethod
    def shapes(columns):
        wide = columns - (columns // 256) * 128
        return ((2, 2, 4, ROWS, wide), (2, 2, 4, ROWS, columns), (2, 2, ROWS, wide), (2, 2, ROWS, columns))

    def group(self, half, q):
        return self.part.at[q, :, 0] if half == 0 else self.part.at[:, q, 1]

    def axes(self, half):
        me = self.me
        return (me.x, me.z, me.xp, me.zp) if half == 0 else (me.z, me.x, me.zp, me.xp)

    def go(self, src, dst, peer):
        copy = self.net.go(src, dst, peer)
        self.sent.append(copy)
        return copy

    def wide(self, i):
        return slice(0, self.cuts[i].stop - self.cuts[i].start)

    def start(self):
        self.one, self.two, self.three, self.four = ([[], []] for _ in range(4))
        for half in range(2):
            p, q, pp, qp = self.axes(half)
            for i, k in enumerate(SIDES):
                piece = self.group(half, (q + 2) % 4).at[:, :, self.cuts[i]]
                self.one[half].append(self.go(piece, self.r1.at[half, i, :, :, self.wide(i)], qp(k)))

    def second(self, half):
        p, q, pp, qp = self.axes(half)
        for i, k in enumerate(SIDES):
            landed([self.one[half][i]])
            mine = self.group(half, (q + k) % 4)

            def add(j, _):
                mine[j, :, self.cuts[i]] = (
                    mine[j, :, self.cuts[i]].astype(F32) + self.r1[half, i, j, :, self.wide(i)].astype(F32)
                ).astype(BF)
                return 0

            lax.fori_loop(0, 4, add, 0)
            self.two[half].append(self.go(mine, self.r2.at[half, i], qp(k)))

    def third(self, half):
        p, q, pp, qp = self.axes(half)
        landed(self.two[half])
        mine = self.group(half, q)

        def add(j, _):
            mine[j] = (
                mine[j].astype(F32) + self.r2[half, 0, j].astype(F32) + self.r2[half, 1, j].astype(F32)
            ).astype(BF)
            return 0

        lax.fori_loop(0, 4, add, 0)
        for i, k in enumerate(SIDES):
            self.three[half].append(
                self.go(mine.at[(p + 2) % 4, :, self.cuts[i]], self.u1.at[half, i, :, self.wide(i)], pp(k))
            )

    def fourth(self, half):
        p, q, pp, qp = self.axes(half)
        for i, k in enumerate(SIDES):
            landed([self.three[half][i]])
            block = self.group(half, q).at[(p + k) % 4]
            block[:, self.cuts[i]] = (
                block[:, self.cuts[i]].astype(F32) + self.u1[half, i, :, self.wide(i)].astype(F32)
            ).astype(BF)
            self.four[half].append(self.go(block, self.u2.at[half, i], pp(k)))

    def finish(self):
        for half in range(2):
            p, q, pp, qp = self.axes(half)
            landed(self.four[half])
            self.out[half] = (
                self.group(half, q)[p].astype(F32) + self.u2[half, 0].astype(F32) + self.u2[half, 1].astype(F32)
            ).astype(BF)
        self.net.left(self.sent)
        if self.then is not None:
            self.then()


class DirectScatter:
    def __init__(self, me, net, part, got, out):
        self.me, self.net, self.part, self.got, self.out = me, net, part, got, out
        self.sent = []
        for i, (dz, dx) in enumerate(OTHERS):
            src = part.at[(me.z + dz) % 4, (me.x + dx) % 4]
            self.sent.append(net.go(src, got.at[i], me.chip(dz, dx)))

    def finish(self):
        total = self.part[self.me.z, self.me.x].astype(F32)
        landed(self.sent)
        for i in range(len(OTHERS)):
            total = total + self.got[i].astype(F32)
        self.out[...] = total.astype(BF)
        self.net.left(self.sent)


class Beside:
    def __init__(self, lags, turns):
        self.lags, self.turns, self.turn, self.jobs = lags, list(turns), 0, []

    def add(self, job):
        first = self.turn
        if self.jobs:
            first = max(first, self.jobs[-1][0] + self.lags[len(self.jobs)])
        self.jobs.append((first, list(job.steps()), job))
        return job

    def step(self):
        for _ in range(self.turns.pop(0) if self.turns else 0):
            self.take()

    def take(self):
        for first, steps, _ in reversed(self.jobs):
            if self.turn >= first and steps:
                steps.pop(0)()
        self.turn += 1

    def until(self, *jobs):
        while any(steps for _, steps, job in self.jobs if job in jobs):
            self.take()

    def rest(self):
        while any(steps for _, steps, _ in self.jobs):
            self.take()


def dot(a, b, ca=1, cb=0):
    return lax.dot_general(a, b, (((ca,), (cb,)), ((), ())), preferred_element_type=F32)


def unit_rms(u):
    scale = lax.rsqrt(jnp.mean(u * u, axis=1, keepdims=True) + EPS)
    return u * scale, scale


def norm_back(u, gain, dy):
    n, scale = unit_rms(u)
    sd = dy * gain
    return scale * (sd - n * jnp.mean(sd * n, axis=1, keepdims=True)), jnp.sum(dy * n, axis=0, keepdims=True)


def turned(u, cos, sin):
    return u * cos + pltpu.roll(u, 64, 1) * sin


def turned_back(w, cos, sin):
    return w * cos - pltpu.roll(w, 64, 1) * sin


def twice(table):
    return jnp.concatenate([table, table], axis=0)


def key_places(rows):
    j = lax.broadcasted_iota(jnp.int32, (rows, 2048), 1)
    core = j // 1024
    chip = (j % 1024) // TOK
    return chip * (2 * TOK) + core * TOK + j % TOK


def masked(raw, ctx):
    rows = raw.shape[0]
    query = ctx * TOK + lax.broadcasted_iota(jnp.int32, (rows, 2048), 0) % TOK
    return jnp.where(key_places(rows) <= query, raw * (HD**-0.5), -1e30)


def columns_of(i, base=0):
    return pl.ds(pl.multiple_of(base + i * CHUNK, CHUNK), CHUNK)


def attn_forward(me, net, beside, x_ref, gain, bias, turns, wf, weights, hid, q, kv, att, part, got, mid):
    x = x_ref[...]
    normed, _ = unit_rms(x)
    hid[me.y] = (normed * gain).astype(BF)
    hid_copies = [net.go(hid.at[me.y], hid.at[me.y], me.yp(k)) for k in ORDER]
    cos, sin = twice(turns[0]), twice(turns[1])
    weights()
    beside.step()
    landed(hid_copies)
    hidden = hid[...].reshape(2 * TOK, D)
    proj = dot(hidden, whole(wf.at[0], slice(0, QKW))) + bias[:, :QKW]
    key = turned(proj[:, 384:], cos, sin).astype(BF)
    value = (dot(hidden, whole(wf.at[1], slice(384, QKW))) + bias[:, QKW:]).astype(BF)
    keyval = jnp.concatenate([key, value], axis=1)
    for m in range(2):
        kv[me.c, m, me.z, me.x] = keyval[m * TOK : (m + 1) * TOK]
    mine0, mine1 = kv.at[me.c, 0, me.z, me.x], kv.at[me.c, 1, me.z, me.x]
    first0 = [net.go(mine0, mine0, me.xp(k)) for k in ORDER]
    first1 = [net.go(mine1, mine1, me.zp(k)) for k in ORDER]
    for head in range(HEADS):
        query = turned(proj[:, head * HD : (head + 1) * HD], cos, sin).astype(BF)
        for m in range(2):
            q[m, head] = query[m * TOK : (m + 1) * TOK]
    beside.step()
    landed(first0)
    second0 = [net.go(kv.at[me.c, 0, me.z], kv.at[me.c, 0, me.z], me.zp(k)) for k in ORDER]
    landed(first1)
    second1 = [net.go(kv.at[me.c, 1, :, me.x], kv.at[me.c, 1, :, me.x], me.xp(k)) for k in ORDER]
    beside.step()
    landed(second0)
    third0 = net.go(kv.at[me.c, 0], kv.at[me.c, 0], me.cp())
    landed(second1)
    third1 = net.go(kv.at[me.c, 1], kv.at[me.c, 1], me.cp())
    for m, third in ((0, third0), (1, third1)):
        beside.step()
        landed([third])
        queries = q[m].reshape(HEADS * TOK, HD)
        keys = kv[:, m, :, :, :, :HD].reshape(2048, HD)
        values = kv[:, m, :, :, :, HD:].reshape(2048, HD)
        scores = masked(dot(queries, keys, 1, 1), me.ctx)
        weight = jnp.exp(scores - jnp.max(scores, axis=1, keepdims=True))
        total = jnp.sum(weight, axis=1, keepdims=True)
        out = (dot(weight.astype(BF), values) / total).astype(BF)
        for head in range(HEADS):
            att[m * TOK : (m + 1) * TOK, head * HD : (head + 1) * HD] = out[head * TOK : (head + 1) * TOK]
    beside.step()
    part[...] = dot(att[...], whole(wf.at[1], slice(0, 384)), 1, 1).astype(BF).reshape(4, OWN, D)
    back = [net.go(part.at[(me.y + k) % 4], got.at[k - 1], me.yp(k)) for k in ORDER]
    beside.step()
    total = x + part[me.y].astype(F32)
    landed(back)
    for k in range(3):
        total = total + got[k].astype(F32)
    mid[...] = total
    net.left(hid_copies + first0 + first1 + second0 + second1 + [third0, third1] + back)


def gather_yc(me, net, buf):
    own = buf.at[me.c, me.y]
    sent = [net.go(own, own, me.yp(k)) for k in ORDER]
    crossed = [net.go(own, own, me.cp())]

    def rest():
        for k, copy in zip(ORDER, sent):
            landed([copy])
            block = buf.at[me.c, (me.y + 4 - k) % 4]
            crossed.append(net.go(block, block, me.cp()))
        landed(crossed)
        return sent + crossed

    return rest


class ScatterYC:
    def __init__(self, me, net, part, mate, got):
        self.me, self.net, self.part, self.mate, self.got = me, net, part, mate, got
        self.swap = net.go(part.at[1 - me.c], mate, me.cp())

    def middle(self):
        me, mate = self.me, self.mate
        landed([self.swap])
        mate[...] = (self.part[me.c].astype(F32) + mate[...].astype(F32)).astype(BF)
        self.back = [self.net.go(mate.at[(me.y + k) % 4], self.got.at[k - 1], me.yp(k)) for k in ORDER]

    def end(self):
        total = self.mate[self.me.y].astype(F32)
        landed(self.back)
        for k in range(3):
            total = total + self.got[k].astype(F32)
        self.net.left([self.swap] + self.back)
        return total


def whole(ref, columns):
    return ref[:, :, :, :, columns].reshape(D, -1)


def mlp_product(me, net, beside, mid, gain, wm, weights, hid, gate, up, prod):
    normed, _ = unit_rms(mid[...])
    hid[me.c, me.y] = (normed * gain).astype(BF)
    rest = gather_yc(me, net, hid)
    beside.step()
    copies = rest()
    beside.step()
    weights(GATE, UP)

    def first(i, _):
        cols = columns_of(i)
        gate_part = dot(hid[...].reshape(256, D), whole(wm, cols))
        up_part = dot(hid[...].reshape(256, D), whole(wm, columns_of(i, UNITS)))
        gate[:, cols] = gate_part
        up[:, cols] = up_part
        prod[:, cols] = (gate_part * jax.nn.sigmoid(gate_part) * up_part).astype(BF)
        return 0

    lax.fori_loop(0, UNITS // CHUNK, first, 0)
    net.left(copies)


def mlp_down(me, net, wm, prod, part, mate, got):
    part[...] = dot(prod[...], whole(wm, DOWN), 1, 1).astype(BF).reshape(2, 4, OWN, D)
    return ScatterYC(me, net, part, mate, got)


def call(kernel, name, collective_id, ins, outs, scratch):
    names = list(ins) + list(outs) + list(scratch)

    def body(*refs):
        kernel(types.SimpleNamespace(**dict(zip(names, refs))))

    def spec(here):
        return pl.BlockSpec(memory_space=pltpu.VMEM if here else pl.ANY)

    results = pl.pallas_call(
        body,
        out_shape=tuple(jax.ShapeDtypeStruct(shape, dtype) for shape, dtype, _ in outs.values()),
        in_specs=[spec(here) for _, here in ins.values()],
        out_specs=tuple(spec(here) for _, _, here in outs.values()),
        scratch_shapes=list(scratch.values()),
        compiler_params=pltpu.CompilerParams(
            collective_id=collective_id, has_side_effects=True, vmem_limit_bytes=255 << 18
        ),
        name=name,
    )(*[array for array, _ in ins.values()])
    return dict(zip(outs, results))


def sems(local, send, recv):
    return dict(
        lsem=pltpu.SemaphoreType.DMA((local,)),
        send=pltpu.SemaphoreType.DMA((send,)),
        recv=pltpu.SemaphoreType.DMA((recv,)),
    )


KEPT = dict(
    hid=((4, OWN, D), BF),
    q=((2, HEADS, TOK, HD), BF),
    kv=((2, 2, 4, 4, TOK, 2 * HD), BF),
    att=((2 * TOK, HEADS * HD), BF),
    wf=((2, 4, 4, 2, ROWS, QKW), BF),
    x=((OWN, D), F32),
    mid=((OWN, D), F32),
    hid2=((2, 4, OWN, D), BF),
    gate=((256, UNITS), F32),
    up=((256, UNITS), F32),
    prod=((256, UNITS), BF),
    wm=((4, 4, 2, ROWS, 3 * UNITS), BF),
)
GATE, UP, DOWN = (slice(part * UNITS, (part + 1) * UNITS) for part in range(3))
FORWARD_LAGS = (5, 5, 1, 5, 5, 1, 6, 3)
FORWARD_TURNS = (3, 4, 0, 1, 2, 1, 0, 0, 1, 4, 1, 2, 0, 3, 0, 0, 2, 1, 0, 1, 1, 1, 3, 0, 9)
BACKWARD_LAGS = (5, 0, 3, 4, 2, 0, 3, 3)
BACKWARD_TURNS = (1, 0, 2, 0, 1, 0, 0, 0, 1, 2, 0, 1, 2, 1, 0, 1, 0, 1, 0, 1, 0, 1, 2, 0, 2, 2)


def vmem(shape_dtype):
    return pltpu.VMEM(*shape_dtype)


def forward_kernel(r):
    me = Place()
    me.greet()
    net, local = Links(r.send, r.recv), Local(r.lsem)
    peers = me.quad()
    early, late, arrivals = [], [], []
    everyone = me.quad() + ((me.c, me.s, None),)

    def hand_out(copies, src, dst):
        waits = []
        for core, section, peer in everyone:
            if peer is None:
                waits.append(local.go(src(core, section), dst).wait)
            else:
                copies.append(net.go(src(core, section), dst, peer))
                waits.append(functools.partial(landed, copies[-1:]))
        return waits

    def columns_for(width, core_and_section, base=0):
        return pl.ds(pl.multiple_of(core_and_section * width + base, 128), width)

    attn_dst = r.attn_rows.at[me.s, me.c]
    waits = hand_out(early, lambda c, s: r.attn_flat.at[c, :, columns_for(384, s)], attn_dst.at[:, :384])
    waits += hand_out(early, lambda c, s: r.attn_flat.at[c, :, 768:], attn_dst.at[:, 384:])
    r.padded[...] = jnp.zeros((16, D), F32)
    r.padded[:2, :48] = r.gains_here[...].astype(F32)
    eye = lax.broadcasted_iota(jnp.int32, (6, 6), 0) == lax.broadcasted_iota(jnp.int32, (6, 6), 1)
    for lane in range(4):
        row = r.bias_q_here[lane : lane + 1].astype(F32)
        r.padded[8:14, lane : lane + 1] = jnp.sum(jnp.where(eye, row, 0.0), axis=1, keepdims=True)
    r.padded[14:, :4] = r.bias_kv_here[...].astype(F32)
    spots = pltpu.roll(r.padded[:8], me.ctx * 48, 1)
    for which in range(2):
        for i in range(12):
            r.tiny_f32[12 * which + i : 12 * which + i + 1] = spots[which : which + 1, i * 128 : (i + 1) * 128]
    r.tiny_f32[24:] = pltpu.roll(r.padded[8:, :128], me.ctx * 4, 1)
    r.tiny[...] = r.tiny_f32[...].astype(BF)
    waits += hand_out(early, lambda c, s: r.tiny, r.tiny_quad.at[me.s, me.c])
    away = pl.ds(pl.multiple_of((1 - me.s) * OWN, OWN), OWN)
    home = pl.ds(pl.multiple_of(me.s * OWN, OWN), OWN)
    tokens_over = net.go(r.ends.at[me.h, away], r.tokens.at[me.s], dict(section=1 - me.s))
    tokens_here = local.go(r.ends.at[me.h, home], r.tokens.at[me.s])
    here = r.mlp_rows.at[me.s, me.c]
    for part, columns in enumerate((GATE, UP)):
        src = r.gate_up_flat.at[part]
        arrivals.append(hand_out(late, lambda c, s: src.at[:, columns_for(UNITS, 2 * s + c)], here.at[:, columns]))
    body, rest = slice(DOWN.start, DOWN.stop - 128), slice(DOWN.stop - 128, DOWN.stop)

    def rest_for(index):
        return pl.ds(pl.multiple_of(index * UNITS + 1024 - 128 * (index // 3), 128), 128)

    def body_for(index):
        return pl.ds(pl.multiple_of(index * UNITS, 128), 1024)

    waits_down = hand_out(late, lambda c, s: r.down.at[:, body_for(2 * s + c)], here.at[:, body])
    waits_down += hand_out(late, lambda c, s: r.down.at[:, rest_for(2 * s + c)], here.at[:, rest])
    arrivals.append(waits_down)

    beside = Beside(FORWARD_LAGS, FORWARD_TURNS)
    saved, done, swaps = [], [], [None, None]
    attn_jobs, mlp_jobs = [None, None], [[], []]

    def save(l, *names):
        for name in names:
            saved.append(local.go(getattr(r, name + str(l)), getattr(r, "out_" + name + str(l))))

    def add_attn(l):
        own = getattr(r, f"wf{l}").at[me.c]

        def swap():
            swaps[l] = net.go(own, own, me.cp())

        attn_jobs[l] = beside.add(Gather(me, net, local, r.attn_rows.at[l], own, (), swap))

    def add_mlp(l, columns):
        buf, out = (getattr(r, f"{name}{l}").at[:, :, :, :, columns] for name in ("wm", "out_wm"))
        ready = arrivals[columns.start // UNITS] if l == 0 else ()
        job = Gather(
            me, net, local, r.mlp_rows.at[l, :, :, columns], buf, ready, lambda: saved.append(local.go(buf, out)),
            (l + columns.start // UNITS) % 2 == 1,
        )
        mlp_jobs[l].append((columns, beside.add(job)))

    for wait in waits:
        wait()
    r.tiny_mine[...] = (r.tiny_quad[:, 0].astype(F32) + r.tiny_quad[:, 1].astype(F32)).astype(BF)
    one = [net.go(r.tiny_mine, r.tiny_x.at[k - 1], me.xp(k)) for k in ORDER]
    for l in range(2):
        add_attn(l)
        for columns in (GATE, UP, DOWN):
            add_mlp(l, columns)
    beside.step()
    landed(one)
    r.tiny_row[...] = (
        r.tiny_mine[...].astype(F32) + r.tiny_x[0].astype(F32) + r.tiny_x[1].astype(F32) + r.tiny_x[2].astype(F32)
    ).astype(BF)
    two = [net.go(r.tiny_row, r.tiny_z.at[k - 1], me.zp(k)) for k in ORDER]
    beside.step()
    landed(two)
    r.small[...] = (
        r.tiny_row[...].astype(F32) + r.tiny_z[0].astype(F32) + r.tiny_z[1].astype(F32) + r.tiny_z[2].astype(F32)
    )

    def gain(l, which):
        return jnp.concatenate([r.small[l, 12 * which + i : 12 * which + i + 1, :] for i in range(12)], axis=1)

    def bias(l):
        rows = [r.small[l, pl.ds(24 + HEADS * me.s + i, 1), :] for i in range(HEADS)]
        rows += [r.small[l, 30 + i : 31 + i, :] for i in range(2)]
        return jnp.concatenate(rows, axis=1)

    for l in range(2):
        for which in range(2):
            r.gains[l, which] = gain(l, which)
    tokens_here.wait()
    landed([tokens_over])
    r.low[me.c, me.y] = r.tokens[1].astype(BF)
    low_rest = []

    for l in range(2):
        kept = types.SimpleNamespace(**{name: getattr(r, name + str(l)) for name in KEPT})
        if l == 0:
            kept.x[...] = r.tokens[0]

        def attn_weights():
            if l == 0:
                low_rest.append(gather_yc(me, net, r.low))
            else:
                beside.step()
            beside.until(attn_jobs[l])
            landed([swaps[l]])
            done.append(swaps[l])

        attn_forward(
            me, net, beside, kept.x, r.gains[l, 0], bias(l), r.turns, kept.wf, attn_weights,
            kept.hid, kept.q, kept.kv, kept.att, getattr(r, f"part{l}"), getattr(r, f"got{l}"), kept.mid,
        )
        if l == 0:
            done += low_rest[0]()
        save(l, "hid", "q", "kv", "att", "wf", "x", "mid")
        weights = lambda *wanted: beside.until(*[job for columns, job in mlp_jobs[l] if columns in wanted])
        mlp_product(
            me, net, beside, kept.mid, r.gains[l, 1], kept.wm, weights, kept.hid2, kept.gate, kept.up, kept.prod
        )
        save(l, "hid2", "gate", "up", "prod")
        beside.step()
        if l == 0:
            weights(DOWN)
            scatter = mlp_down(me, net, kept.wm, kept.prod, r.wide0, r.mate0, r.got20)
            beside.step()
            scatter.middle()
            beside.step()
            r.x1[...] = (kept.mid[...] + scatter.end()).astype(BF).astype(F32)
    beside.rest()
    for copy in saved:
        copy.wait()
    net.left(early + late + [tokens_over] + one + two + done)


def forward(attn_flat, gate_up_flat, down, gains_here, bias_q_here, bias_kv_here, ends, turns):
    ins = dict(
        attn_flat=(attn_flat, False), gate_up_flat=(gate_up_flat, False), down=(down, False),
        gains_here=(gains_here, True), bias_q_here=(bias_q_here, True), bias_kv_here=(bias_kv_here, True),
        ends=(ends, False), turns=(turns, True),
    )
    outs = {f"out_{name}{l}": (*KEPT[name], False) for l in range(2) for name in KEPT}
    outs["gains"] = ((2, 2, 1, D), F32, True)
    outs["low"] = ((2, 4, OWN, D), BF, True)
    outs["tokens"] = ((2, OWN, D), F32, True)
    scratch = {f"{name}{l}": vmem(KEPT[name]) for l in range(2) for name in KEPT}
    scratch |= dict(
        attn_rows=pltpu.VMEM((2, 2, ROWS, QKW), BF),
        mlp_rows=pltpu.VMEM((2, 2, ROWS, 3 * UNITS), BF),
        padded=pltpu.VMEM((16, D), F32),
        tiny_f32=pltpu.VMEM((32, 128), F32),
        tiny=pltpu.VMEM((32, 128), BF),
        tiny_quad=pltpu.VMEM((2, 2, 32, 128), BF),
        tiny_mine=pltpu.VMEM((2, 32, 128), BF),
        tiny_x=pltpu.VMEM((3, 2, 32, 128), BF),
        tiny_row=pltpu.VMEM((2, 32, 128), BF),
        tiny_z=pltpu.VMEM((3, 2, 32, 128), BF),
        small=pltpu.VMEM((2, 32, 128), F32),
    )
    for l in range(2):
        scratch["part" + str(l)] = pltpu.VMEM((4, OWN, D), BF)
        scratch["got" + str(l)] = pltpu.VMEM((3, OWN, D), BF)
    scratch |= dict(
        wide0=pltpu.VMEM((2, 4, OWN, D), BF), mate0=pltpu.VMEM((4, OWN, D), BF), got20=pltpu.VMEM((3, OWN, D), BF)
    )
    return call(forward_kernel, "forward", 0, ins, outs, scratch | sems(44, 152, 415))


def attn_backward(me, net, beside, r, layer, gm, load_weights, asides, early_done):
    da, dakv, got, kpair_got = r.da.at[layer], r.dakv.at[layer], r.got.at[layer], r.kpair_got.at[layer]
    kz, kx, k3 = r.kz.at[layer], r.kx.at[layer], r.k3.at[layer]
    wf, dws = r.wm.at[:, :, :, :, : 2 * QKW], r.wm.at[:, :, :, :, UNITS : UNITS + 2 * QKW]
    r.low2[me.y] = gm.astype(BF)
    own = r.low2.at[me.y]
    gathered = [net.go(own, own, me.yp(k)) for k in ORDER]
    beside.step()
    cos, sin = twice(r.turns[0]), twice(r.turns[1])
    load_weights()
    landed(gathered)
    grad_mid = r.low2[...].reshape(2 * TOK, D)
    grad_att = dot(grad_mid, whole(wf, slice(512, 896))).astype(BF)
    for m in range(2):
        rows = slice(m * TOK, (m + 1) * TOK)
        queries = r.q[m].reshape(HEADS * TOK, HD)
        keys = r.kv[:, m, :, :, :, :HD].reshape(2048, HD)
        values = r.kv[:, m, :, :, :, HD:].reshape(2048, HD)
        grad_out = jnp.concatenate([grad_att[rows, h * HD : (h + 1) * HD] for h in range(HEADS)], axis=0)
        scores = masked(dot(queries, keys, 1, 1), me.ctx)
        weight = jnp.exp(scores - jnp.max(scores, axis=1, keepdims=True))
        soft = weight / jnp.sum(weight, axis=1, keepdims=True)
        grad_soft = dot(grad_out, values, 1, 1)
        delta = jnp.sum(soft * grad_soft, axis=1, keepdims=True)
        grad_scores = (soft * (grad_soft - delta)).astype(BF)
        grad_values = dot(soft.astype(BF), grad_out, 0, 0)
        grad_keys = dot(grad_scores, queries, 0, 0) * (HD**-0.5)
        r.dkv[:, m] = jnp.concatenate([grad_keys, grad_values], axis=1).astype(BF).reshape(2, 4, 4, TOK, 2 * HD)
        dq = dot(grad_scores, keys) * (HD**-0.5)
        for h in range(HEADS):
            r.dqs[rows, h * HD : (h + 1) * HD] = dq[h * TOK : (h + 1) * TOK]
        beside.step()
    swap = net.go(r.dkv.at[1 - me.c], r.kmate, me.cp())
    dq_low = jnp.concatenate(
        [turned_back(r.dqs[:, h * HD : (h + 1) * HD], cos, sin).astype(BF) for h in range(HEADS)], axis=1
    )
    hidden = r.hid[...].reshape(2 * TOK, D)
    beside.step()
    landed([swap])
    kmate, k2 = r.kmate, r.k2
    kmate[...] = (kmate[...].astype(F32) + r.dkv[me.c].astype(F32)).astype(BF)
    first0 = [net.go(kmate.at[0, (me.z + k) % 4], kz.at[k - 1], me.zp(k)) for k in ORDER]
    first1 = [net.go(kmate.at[1, :, (me.x + k) % 4], kx.at[k - 1], me.xp(k)) for k in ORDER]

    def blocks(value):
        return value.astype(BF).reshape(4, 4, 2, ROWS, -1)

    dws[:, :, :, :, :384] = blocks(dot(hidden, dq_low, 0, 0))
    dws[:, :, :, :, 512:896] = blocks(dot(grad_mid, r.att[...], 0, 0))
    dws[:, :, :, :, 896:1024] = jnp.zeros((4, 4, 2, ROWS, HD), BF)

    def half(core, base=0, width=384):
        return pl.ds(pl.multiple_of(core * QKW + base, 128), width)

    early_swap = net.go(dws.at[:, :, :, :, half(1 - me.c)], da, me.cp())
    asides[0]()
    beside.step()
    landed(first0)
    total0 = kmate[0, me.z].astype(F32)
    for k in range(3):
        total0 = total0 + kz[k].astype(F32)
    k2[0] = total0.astype(BF)
    second0 = [net.go(k2.at[0, (me.x + k) % 4], k3.at[0, k - 1], me.xp(k)) for k in ORDER]
    landed(first1)
    total1 = kmate[1, :, me.x].astype(F32)
    for k in range(3):
        total1 = total1 + kx[k].astype(F32)
    k2[1] = total1.astype(BF)
    second1 = [net.go(k2.at[1, (me.z + k) % 4], k3.at[1, k - 1], me.zp(k)) for k in ORDER]
    landed([early_swap])

    def add_early(j, _):
        da[j] = (dws[j, :, :, :, half(me.c)].astype(F32) + da[j].astype(F32)).astype(BF)
        return 0

    lax.fori_loop(0, 4, add_early, 0)
    early_done()
    asides[1]()
    beside.step()
    landed(second0 + second1)
    for m, place in ((0, me.x), (1, me.z)):
        total = k2[m, place].astype(F32)
        for k in range(3):
            total = total + k3[m, k].astype(F32)
        r.kpair[0, m * TOK : (m + 1) * TOK] = total[:, :HD].astype(BF)
        r.kpair[1, m * TOK : (m + 1) * TOK] = total[:, HD:].astype(BF)
    pair = net.go(r.kpair.at[1 - me.s], kpair_got, dict(section=1 - me.s))
    beside.step()
    landed([pair])
    total = r.kpair[me.s].astype(F32) + kpair_got[...].astype(F32)
    dk_low = jnp.where(me.s == 0, turned_back(total, cos, sin), total).astype(BF)
    w_own = jnp.where(me.s == 0, whole(wf, slice(384, 512)), whole(wf, slice(896, 1024)))
    r.part[...] = (
        (dot(dq_low, whole(wf, slice(0, 384)), 1, 1) + dot(dk_low, w_own, 1, 1)).astype(BF).reshape(4, OWN, D)
    )
    back = [net.go(r.part.at[(me.y + k) % 4], got.at[k - 1], me.yp(k)) for k in ORDER]
    dws[:, :, :, :, 384:512] = blocks(dot(hidden, dk_low, 0, 0))

    late_swap = net.go(dws.at[:, :, :, :, half(1 - me.c, 384, HD)], dakv, me.cp())
    asides[2]()
    beside.step()
    gbias = jnp.concatenate(
        [jnp.sum(dq_low.astype(F32), axis=0, keepdims=True), jnp.sum(dk_low.astype(F32), axis=0, keepdims=True)], axis=1
    )
    dy = r.part[me.y].astype(F32)
    landed(back)
    for k in range(3):
        dy = dy + got[k].astype(F32)
    dx, ggain = norm_back(r.x[...], r.gains[layer, 0], dy)
    gin = gm + dx
    landed([late_swap])
    dakv[...] = (dws[:, :, :, :, half(me.c, 384, HD)].astype(F32) + dakv[...].astype(F32)).astype(BF)
    net.left(gathered + [swap] + first0 + first1 + second0 + second1 + [pair] + back + [early_swap, late_swap])
    return gin, ggain, gbias


def mlp_backward(me, net, beside, r, layer, g, loaded, scatter, free):
    mate, got2 = r.mate.at[layer], r.got2.at[layer]
    loaded("prod")

    def weight_grad(base, left_ref, right_ref):
        def step(i, _):
            r.dm[:, :, :, :, columns_of(i, base)] = (
                dot(left_ref[...].reshape(256, D), right_ref[:, columns_of(i)], 0, 0)
                .astype(BF)
                .reshape(4, 4, 2, ROWS, CHUNK)
            )
            return 0

        lax.fori_loop(0, UNITS // CHUNK, step, 0)

    free(DOWN)
    weight_grad(2 * UNITS, r.low, r.prod)
    scatter(DOWN)
    beside.step()
    loaded("gate", "up", "wm", "hid2")

    def step(i, _):
        cols = columns_of(i)
        dprod = dot(r.low[...].reshape(256, D), whole(r.wm, columns_of(i, 2 * UNITS)))
        gate, up = r.gate[:, cols], r.up[:, cols]
        sigma = jax.nn.sigmoid(gate)
        dg = (dprod * up * sigma * (1.0 + gate * (1.0 - sigma))).astype(BF)
        du = (dprod * gate * sigma).astype(BF)
        r.dgate[:, cols] = dg
        r.dup[:, cols] = du
        return 0

    lax.fori_loop(0, UNITS // CHUNK, step, 0)

    def back(i, _):
        w_gate, w_up = (r.wm[i, :, :, :, part].reshape(D // 4, UNITS) for part in (GATE, UP))
        sums = dot(r.dgate[...], w_gate, 1, 1) + dot(r.dup[...], w_up, 1, 1)
        r.wide[:, :, :, columns_of(i)] = sums.astype(BF).reshape(2, 4, OWN, D // 4)
        return 0

    lax.fori_loop(0, 4, back, 0)
    sums = ScatterYC(me, net, r.wide, mate, got2)
    beside.step()
    free(GATE)
    weight_grad(0, r.hid2, r.dgate)
    sums.middle()
    scatter(GATE)
    beside.step()
    free(UP)
    weight_grad(UNITS, r.hid2, r.dup)
    scatter(UP)
    beside.step()
    dy = sums.end()
    du, ggain = norm_back(r.mid[...], r.gains[layer, 1], dy)
    return g + du, ggain


def put_small(r, base, y, ggain0, ggain1, gbias):
    r.sums[0, base + 24 : base + 40] = jnp.zeros((16, 128), F32)
    for which, ggain in enumerate((ggain0, ggain1)):
        for i in range(12):
            r.sums[0, base + 12 * which + i : base + 12 * which + i + 1] = ggain[:, i * 128 : (i + 1) * 128]
    for i in range(4):
        r.sums[0, pl.ds(base + 24 + 4 * y + i, 1)] = gbias[:, i * 128 : (i + 1) * 128]


def backward_kernel(r):
    me = Place()
    local = Local(r.lsem)
    pending = {}

    def load(layer, *names):
        for name in names:
            pending[name] = local.go(getattr(r, "in" + str(layer) + "_" + name), getattr(r, name))

    def loaded(*wanted):
        for name in wanted:
            pending.pop(name).wait()

    attention = ("hid", "q", "kv", "att", "x")
    low_here = local.go(r.in_low, r.low)
    load(1, "prod", "gate", "up", "wm", "hid2", "mid", *attention)
    me.greet(True)
    net = Links(r.send, r.recv)
    beside = Beside(BACKWARD_LAGS, BACKWARD_TURNS)
    crossed, extra = [], []
    jobs = {}

    def go_home(src, dst):
        for core, section, peer in me.quad():
            crossed.append(net.go(src.at[section, core], dst, peer))
        extra.append(local.go(src.at[me.s, me.c], dst))

    def place_of(width, index):
        return pl.ds(pl.multiple_of(index * width, 128), width)

    def attn_home():
        go_home(r.res_a.at[:, :, :, :384], r.attn_home.at[me.c, :, place_of(384, me.s)])
        go_home(r.res_a.at[:, :, :, 384:], r.kv_home.at[me.c, :, place_of(HD, me.s)])

    def scatter(layer, columns):
        dst = r.down_home if columns == DOWN else r.gate_up_home.at[columns.start // UNITS]
        dst = dst.at[:, place_of(UNITS, 2 * me.s + me.c)]
        then = functools.partial(go_home, r.res_m.at[:, :, :, columns], dst) if layer == 0 else None
        refs = tuple(getattr(r, "m" + str(columns.start) + name) for name in ("_r1", "_r2", "_u1", "_u2"))
        flip = (layer + columns.start // UNITS) % 2 == 1
        part = r.dm.at[:, :, :, :, columns]
        jobs[columns.start] = beside.add(Scatter(me, net, part, refs, r.res_m.at[layer, :, :, columns], then, flip))

    def free(columns):
        if columns.start in jobs:
            beside.until(jobs[columns.start])

    def attn_job(layer):
        refs = (r.a_r1.at[layer], r.a_r2.at[layer], r.a_u1.at[layer], r.a_u2.at[layer])
        beside.add(Scatter(me, net, r.da.at[layer], refs, r.res_a.at[layer, :, :, :384], None, layer == 1))

    def attn_weights(layer):
        refs = r.in1_wf if layer else r.in0_wf
        copies = [local.go(refs.at[i], r.wm.at[:, :, :, :, i * QKW : (i + 1) * QKW]) for i in range(2)]

        def wait():
            for copy in copies:
                copy.wait()
            loaded(*attention)

        return wait

    def kv_scatter(layer):
        return DirectScatter(me, net, r.dakv.at[layer], r.kv_got.at[layer], r.res_a.at[layer, :, :, 384:])

    nothing = lambda: None
    low_here.wait()
    loaded("mid")
    gm, ggain11 = mlp_backward(
        me, net, beside, r, 1, r.tokens[1], loaded, functools.partial(scatter, 1), lambda columns: None
    )
    load(0, "gate", "up", "hid2")
    down = []

    def start_down():
        down.append(mlp_down(me, net, r.wm, r.prod, r.wide, r.mate2, r.got3))
        load(0, "prod")

    asides = (start_down, lambda: down[0].middle(), lambda: down.append(down[0].end()))
    gin, ggain10, gbias1 = attn_backward(
        me, net, beside, r, 1, gm, attn_weights(1), asides, functools.partial(attn_job, 1)
    )
    kv_scatter1 = kv_scatter(1)
    r.out1[...] = r.mid[...] + down[1]
    load(0, "wm", "mid", *attention)
    put_small(r, 40, me.y, ggain10, ggain11, gbias1)
    g = gin.astype(BF).astype(F32)
    r.low[me.c, me.y] = g.astype(BF)
    rest = gather_yc(me, net, r.low)
    beside.step()
    low_copies = rest()
    kv_scatter1.finish()
    loaded("mid")
    gm, ggain01 = mlp_backward(me, net, beside, r, 0, g, loaded, functools.partial(scatter, 0), free)
    gin, ggain00, gbias0 = attn_backward(
        me, net, beside, r, 0, gm, attn_weights(0), (nothing,) * 3, functools.partial(attn_job, 0)
    )
    r.gin[...] = gin
    last_scatter = kv_scatter(0)
    beside.step()
    put_small(r, 0, me.y, ggain00, ggain01, gbias0)
    rounds = ((me.yp, ORDER, 0), (lambda k: me.cp(), (1,), 3), (me.xp, ORDER, 4), (me.zp, ORDER, 7))
    small = []
    for turn, (peer, ks, slot) in enumerate(rounds):
        sent = [net.go(r.sums.at[turn], r.sums_got.at[slot + k - 1], peer(k)) for k in ks]
        if turn == 0:
            r.ends2[0] = r.gin[...].astype(BF)
            r.ends2[1] = r.out1[...].astype(BF)
            edges = [net.go(r.ends2.at[((me.y + k) % 4) % 2], r.ends_got.at[k - 1], me.yp(k)) for k in ORDER]
        if turn == 2:
            last_scatter.finish()
            beside.rest()
            attn_home()
        landed(sent)
        total = r.sums[turn]
        for k in ks:
            total = total + r.sums_got[slot + k - 1]
        r.sums[turn + 1] = total
        small.extend(sent)
    total = r.sums.at[4]
    spots = [r.sums[4, pl.ds(40 * me.s + i, 1)] for i in range(24)]
    spots = jnp.concatenate(
        [jnp.concatenate(spots[12 * which : 12 * which + 12], axis=1) for which in range(2)]
        + [jnp.zeros((6, D), F32)],
        axis=0,
    )
    r.gain_home[...] = pltpu.roll(spots, ((32 - me.ctx) % 32) * 48, 1)[:2, :48]
    rows = [total[pl.ds(40 * me.s + 24 + 8 * me.h + i, 1)] for i in (0, 1, 2, 4, 5, 6, 3, 7)]
    spots = pltpu.roll(jnp.concatenate(rows, axis=0), ((32 - me.ctx) % 32) * 4, 1)
    eye = lax.broadcasted_iota(jnp.int32, (6, 6), 0) == lax.broadcasted_iota(jnp.int32, (6, 6), 1)
    for lane in range(4):
        column = jnp.where(eye, spots[:6, lane : lane + 1], 0.0)
        r.bias_q_home[lane : lane + 1] = jnp.sum(column, axis=0, keepdims=True)
    r.bias_kv_home[...] = spots[6:, :4]
    r.boundary[me.y] = jnp.where(me.s == 0, r.gin[...], r.out1[...])
    landed(edges)
    for k in ORDER:
        r.boundary[(me.y + 4 - k) % 4] = r.ends_got[k - 1].astype(F32)
    beside.rest()
    landed(crossed)
    for copy in extra:
        copy.wait()
    net.left(low_copies + crossed + edges + small)


def backward(kept, gains, turns, low, tokens):
    ins = {"in" + str(l) + "_" + name: (kept[l][name], False) for l in range(2) for name in KEPT}
    ins |= dict(gains=(gains, True), turns=(turns, True), in_low=(low, False), tokens=(tokens, True))
    outs = dict(
        gate_up_home=((2, ROWS, 4 * UNITS), BF, False),
        down_home=((ROWS, 4 * UNITS), BF, False),
        attn_home=((2, ROWS, 768), BF, False),
        kv_home=((2, ROWS, 2 * HD), BF, False),
        boundary=((4, OWN, D), F32, True),
        gain_home=((2, 48), F32, True),
        bias_q_home=((4, 2 * HEADS), F32, True),
        bias_kv_home=((2, 4), F32, True),
    )
    scratch = {name: vmem(KEPT[name]) for name in KEPT if name != "wf"}
    scratch |= dict(
        low=pltpu.VMEM((2, 4, OWN, D), BF),
        dgate=pltpu.VMEM((256, UNITS), BF),
        dup=pltpu.VMEM((256, UNITS), BF),
        wide=pltpu.VMEM((2, 4, OWN, D), BF),
        mate=pltpu.VMEM((2, 4, OWN, D), BF),
        got2=pltpu.VMEM((2, 3, OWN, D), BF),
        dm=pltpu.VMEM((4, 4, 2, ROWS, 3 * UNITS), BF),
        low2=pltpu.VMEM((4, OWN, D), BF),
        dkv=pltpu.VMEM((2, 2, 4, 4, TOK, 2 * HD), BF),
        kmate=pltpu.VMEM((2, 4, 4, TOK, 2 * HD), BF),
        kz=pltpu.VMEM((2, 3, 4, TOK, 2 * HD), BF),
        kx=pltpu.VMEM((2, 3, 4, TOK, 2 * HD), BF),
        k2=pltpu.VMEM((2, 4, TOK, 2 * HD), BF),
        k3=pltpu.VMEM((2, 2, 3, TOK, 2 * HD), BF),
        kpair=pltpu.VMEM((2, 2 * TOK, HD), BF),
        kpair_got=pltpu.VMEM((2, 2 * TOK, HD), BF),
        dqs=pltpu.VMEM((2 * TOK, HEADS * HD), F32),
        da=pltpu.VMEM((2, 4, 4, 2, ROWS, 384), BF),
        dakv=pltpu.VMEM((2, 4, 4, 2, ROWS, HD), BF),
        part=pltpu.VMEM((4, OWN, D), BF),
        got=pltpu.VMEM((2, 3, OWN, D), BF),
        sums=pltpu.VMEM((5, 80, 128), F32),
        sums_got=pltpu.VMEM((10, 80, 128), F32),
        gin=pltpu.VMEM((OWN, D), F32),
        out1=pltpu.VMEM((OWN, D), F32),
        res_m=pltpu.VMEM((2, 2, ROWS, 3 * UNITS), BF),
        res_a=pltpu.VMEM((2, 2, ROWS, QKW), BF),
        kv_got=pltpu.VMEM((2, 15, 2, ROWS, HD), BF),
        ends2=pltpu.VMEM((2, OWN, D), BF),
        ends_got=pltpu.VMEM((3, OWN, D), BF),
        mate2=pltpu.VMEM((4, OWN, D), BF),
        got3=pltpu.VMEM((3, OWN, D), BF),
    )
    for columns in (GATE, UP, DOWN):
        for name, shape in zip(("_r1", "_r2", "_u1", "_u2"), Scatter.shapes(UNITS)):
            scratch["m" + str(columns.start) + name] = pltpu.VMEM(shape, BF)
    for name, shape in zip(("a_r1", "a_r2", "a_u1", "a_u2"), Scatter.shapes(384)):
        scratch[name] = pltpu.VMEM((2,) + shape, BF)
    return call(backward_kernel, "backward", 1, ins, outs, scratch | sems(32, 75, 249))


def body(ends, w_query, w_kv, w_out, w_gate_up, w_down, gains, bias_query, bias_kv):
    me = Place()
    kv = w_kv[0].transpose(1, 0, 2)
    attn_flat = jnp.concatenate([jnp.stack([w_query[0], w_out[0]]), kv], axis=2)
    missing = 4 * UNITS - w_down.shape[2]
    gate_up_flat = jnp.pad(w_gate_up[0].transpose(1, 0, 2), ((0, 0), (0, 0), (0, missing)))
    lane = jnp.arange(HD, dtype=jnp.int32)
    inverse = 1.0 / THETA ** ((lane % 64).astype(F32) * (2.0 / HD))
    positions = (me.ctx * TOK + jnp.arange(TOK, dtype=jnp.int32)).astype(F32)
    angles = positions[:, None] * inverse[None, :]
    turns = jnp.stack([jnp.cos(angles), jnp.where(lane < 64, -1.0, 1.0) * jnp.sin(angles)])

    ahead = forward(attn_flat, gate_up_flat, w_down[0], gains[0], bias_query[0].T, bias_kv[0, :, 0], ends[0], turns)
    kept = [{name: ahead[f"out_{name}{l}"] for name in KEPT} for l in range(2)]
    done = backward(kept, ahead["gains"], turns, ahead["low"], ahead["tokens"])

    units = w_down.shape[2]
    return (
        done["boundary"].reshape(1, 2, TOK, D),
        done["attn_home"][0].astype(F32)[None],
        done["kv_home"][0].astype(F32).reshape(1, ROWS, 2, HD),
        done["attn_home"][1].astype(F32)[None],
        done["gate_up_home"][:, :, :units].astype(F32).transpose(1, 0, 2)[None],
        done["down_home"][:, :units].astype(F32)[None],
        done["gain_home"][None],
        done["bias_q_home"].T[None],
        done["bias_kv_home"].reshape(1, 2, 1, 4),
    )


def solution(mesh):
    placed = (
        P("section", None, "ctx", None),
        P("section", "ctx", "shard"),
        P("section", "ctx", None, "shard"),
        P("section", "ctx", "shard"),
        P("section", "ctx", None, "shard"),
        P("section", "ctx", "shard"),
        P("section", None, "ctx"),
        P("section", "shard", "ctx"),
        P("section", None, "shard", "ctx"),
    )
    return jax.shard_map(
        body,
        mesh=mesh,
        in_specs=placed,
        out_specs=(
            P("section", None, "ctx", None),
            P("section", "ctx", "shard"),
            P("section", "ctx", None, "shard"),
            P("section", "ctx", "shard"),
            P("section", "ctx", None, "shard"),
            P("section", "ctx", "shard"),
            P("section", None, "ctx"),
            P("section", "shard", "ctx"),
            P("section", None, "shard", "ctx"),
        ),
        check_vma=False,
    )
```
